32 devices in a mesh: seq: 4 (over x, core), fsdp: 8 (over z, y).
Axes of the slice: x: 2, y: 2, z: 4, core: 2. Of those that a mesh axis runs over, the one named last changes fastest.
Arguments:
- tokens: bfloat16 [8, 2560, 1280], P('fsdp', 'seq'), may hold values from -6 to 6
- cont_lengths: int32 [8, 2], P('fsdp'), may hold values from 128 to 384, as said below
- adapter_ids: int32 [8, 3], P('fsdp'), may hold values from 0 to 7
- attn_gain: float32 [2, 1280], replicated, may hold values from 0.25 to 1.75
- mlp_gain: float32 [2, 1280], replicated, may hold values from 0.25 to 1.75
- query_scale: float32 [2, 80], replicated, may hold values from -1 to 1
- w_qkv: bfloat16 [2, 1280, 3840], P(None, 'fsdp'), may hold values from -0.15625 to 0.15625
- output_weight: bfloat16 [2, 1280, 1280], P(None, 'fsdp'), may hold values from -1.25 to 1.25
- inward_weight: bfloat16 [2, 1280, 1280], P(None, 'fsdp'), may hold values from -0.15625 to 0.15625
- down_weight: bfloat16 [2, 1280, 1280], P(None, 'fsdp'), may hold values from -0.15625 to 0.15625
- projection_first_factor: bfloat16 [2, 1280, 384], P(None, 'fsdp'), may hold values from -0.15625 to 0.15625
- b_qkv: bfloat16 [2, 3, 128, 1280], P(None, None, None, 'fsdp'), may hold values from -0.75 to 0.75
- output_first_factor: bfloat16 [2, 1280, 128], P(None, 'fsdp'), may hold values from -0.15625 to 0.15625
- output_second_factor: bfloat16 [2, 128, 1280], P(None, None, 'fsdp'), may hold values from -2 to 2
- inward_first_factor: bfloat16 [2, 1280, 128], P(None, 'fsdp'), may hold values from -0.15625 to 0.15625
- inward_second_factor: bfloat16 [2, 128, 1280], P(None, None, 'fsdp'), may hold values from -0.75 to 0.75
- down_first_factor: bfloat16 [2, 1280, 128], P(None, 'fsdp'), may hold values from -0.15625 to 0.15625
- down_second_factor: bfloat16 [2, 128, 1280], P(None, None, 'fsdp'), may hold values from -0.75 to 0.75
- cotangent: bfloat16 [8, 2560, 1280], P('fsdp', 'seq'), may hold values from -6 to 6
Outputs:
- layer_output: bfloat16 [8, 2560, 1280], P('fsdp', 'seq')
- input_grad: float32 [8, 2560, 1280], P('fsdp', 'seq')
- projection_first_gradient: float32 [2, 1280, 384], P(None, 'fsdp')
- grad_b_qkv: float32 [2, 3, 128, 1280], P(None, None, None, 'fsdp')
- output_first_gradient: float32 [2, 1280, 128], P(None, 'fsdp')
- grad_b_out: float32 [2, 128, 1280], P(None, None, 'fsdp')
- inward_first_gradient: float32 [2, 1280, 128], P(None, 'fsdp')
- grad_b_in: float32 [2, 128, 1280], P(None, None, 'fsdp')
- down_first_gradient: float32 [2, 1280, 128], P(None, 'fsdp')
- grad_b_down: float32 [2, 128, 1280], P(None, None, 'fsdp')
The draws below stay inside these ranges and needn't reach their ends.
Inputs may be any that keep to these rules, and one draw needn't show every extreme that they name: `cont_lengths`: each group's 2 continuation lengths add up to 512; in every group one continuation has exactly 384 tokens and one exactly 128.
All inputs are finite; a program needn't handle non-finite values.
Results may differ from the reference program's by a relative error of at most 0.023.
Values may be sent and summed in bfloat16 or wider, within the bound.
No kernel may reach another device: no remote copies, remote signals or barrier semaphores. Data moves between devices by JAX's collectives and lax.ppermute only.
A program may use at most 320 MiB of HBM per device.

```python
import math
import jax
import jax.numpy as jnp
from jax import lax

D = 1280
HEADS = 16
HD = 80
FF = 1280
R = 16
ADAPTERS = 8
LAYERS = 2
PROMPT = 2048
CONT_LEN = 256
CONTS = 2
AR = 128
GLEN = 2560
GROUPS = 8


def draw_cont_lengths(key, part):
    key = jax.random.fold_in(key, 5)
    spread_key, order_key = jax.random.split(key)
    offsets = jax.random.randint(spread_key, (GROUPS, CONTS // 2), 0, CONT_LEN // 2 + 1)
    offsets = offsets.at[:, 0].set(CONT_LEN // 2)
    paired = jnp.concatenate([CONT_LEN - offsets, CONT_LEN + offsets], axis=1)
    group_keys = jax.random.split(order_key, GROUPS)
    orders = jax.vmap(lambda single: jax.random.permutation(single, CONTS))(group_keys)
    return jnp.take_along_axis(paired, orders, axis=1).astype(jnp.int32)


def place_ends(values, stream_key, smallest, top_value):
    dims = values.shape
    index_at = [jax.random.randint(jax.random.fold_in(stream_key, axis), (), 0, dims[axis]) for axis in range(len(dims))]
    values = values.at[tuple(index_at)].set(smallest)
    longest = dims.index(max(dims))
    index_at[longest] = (index_at[longest] + 1) % dims[longest]
    return values.at[tuple(index_at)].set(top_value)


def strengthened(drawn, rng, source, target, parts, factor):
    owner, partner = [(jnp.arange(drawn.shape[axis_at]) // (drawn.shape[axis_at] // parts)).reshape([-1 if axis == axis_at else 1 for axis in range(drawn.ndim)]) for axis_at in (source, target)]
    chosen = jax.random.permutation(rng, parts)[partner]
    strong = (owner == chosen) | (owner == (partner + parts // 2) % parts)
    return jnp.where(strong, factor * drawn, drawn)


def block_levels(key, dims, pieces, smallest, top_value):
    level = 1.0
    for dim, blocks in pieces:
        heights = jax.random.uniform(jax.random.fold_in(jax.random.fold_in(key, 6), dim), (blocks,), jnp.float32, smallest / len(pieces), top_value / len(pieces))
        level = level * jnp.repeat(jnp.exp(heights), dims[dim] // blocks).reshape((-1,) + (1,) * (len(dims) - 1 - dim))
    return level


def noise(stream_key, dims, scale, bound, shards=(), kind=jnp.bfloat16):
    loudness = block_levels(stream_key, dims, shards, -0.22, 0.18) if shards else 1.0
    entries = jax.random.normal(stream_key, dims, jnp.float32) * scale * loudness
    return jnp.minimum(jnp.maximum(entries, -bound), bound).astype(kind)


def bell_draw_with(rng, shape, spread, limit, shards, heavy, kind=jnp.bfloat16):
    entries = spread * jax.random.normal(rng, shape, jnp.float32)
    if shards:
        entries = entries * block_levels(rng, shape, shards, -0.22, 0.18)
    return jnp.clip(strengthened(entries, jax.random.fold_in(rng, 3), *heavy), -limit, limit).astype(kind)


def setup_inputs(seed: int = 0) -> dict:
    streams_of = jax.random.split(jax.random.key(seed), 20)
    return {
        "tokens": noise(streams_of[0], (GROUPS, GLEN, D), 1.0, 6.0, ((0, 8), (1, 4))),
        "cont_lengths": draw_cont_lengths(jax.random.fold_in(streams_of[19], 71), 0),
        "adapter_ids": place_ends(jax.random.randint(streams_of[2], (GROUPS, CONTS + 1), 0, ADAPTERS), jax.random.fold_in(streams_of[2], 1), 0, ADAPTERS - 1).astype(jnp.int32),
        "attn_gain": jnp.clip(1.0 + 0.15 * jax.random.normal(streams_of[3], (LAYERS, D), jnp.float32), 0.25, 1.75),
        "mlp_gain": jnp.clip(1.0 + 0.15 * jax.random.normal(streams_of[4], (LAYERS, D), jnp.float32), 0.25, 1.75),
        "query_scale": jnp.clip(jax.random.uniform(streams_of[5], (LAYERS, HD), jnp.float32, -1.0, 1.0), -1.0, 1.0),
        "w_qkv": noise(streams_of[6], (LAYERS, D, 3 * D), D ** -0.5, 0.15625, ((1, 8),)),
        "output_weight": noise(streams_of[7], (LAYERS, D, D), (D // 64) ** -0.5, 1.25, ((1, 8),)),
        "inward_weight": noise(streams_of[8], (LAYERS, D, FF), D ** -0.5, 0.15625, ((1, 8),)),
        "down_weight": noise(streams_of[9], (LAYERS, FF, D), FF ** -0.5, 0.15625, ((1, 8),)),
        "projection_first_factor": noise(streams_of[10], (LAYERS, D, 3 * AR), D ** -0.5, 0.15625, ((1, 8),)),
        "b_qkv": noise(streams_of[11], (LAYERS, 3, AR, D), (4 * R) ** -0.5, 0.75, ((3, 8),)),
        "output_first_factor": noise(streams_of[12], (LAYERS, D, AR), D ** -0.5, 0.15625, ((1, 8),)),
        "output_second_factor": noise(streams_of[13], (LAYERS, AR, D), (R // 2) ** -0.5, 2.0, ((2, 8),)),
        "inward_first_factor": noise(streams_of[14], (LAYERS, D, AR), D ** -0.5, 0.15625, ((1, 8),)),
        "inward_second_factor": noise(streams_of[15], (LAYERS, AR, FF), (4 * R) ** -0.5, 0.75, ((2, 8),)),
        "down_first_factor": noise(streams_of[16], (LAYERS, FF, AR), FF ** -0.5, 0.15625, ((1, 8),)),
        "down_second_factor": noise(streams_of[17], (LAYERS, AR, D), (4 * R) ** -0.5, 0.75, ((2, 8),)),
        "cotangent": bell_draw_with(streams_of[18], (GROUPS, GLEN, D), 1.0, 6.0, ((0, 8), (1, 4)), (0, 2, 8, 2.0)),
    }


@jax.custom_vjp
def low(v):
    return lax.optimization_barrier(v.astype(jnp.bfloat16)).astype(jnp.float32)

@jax.custom_vjp
def low_back(v):
    return v

def low_keep(v):
    return (low(v), None)

def low_pass(kept, grad):
    return (grad,)

def back_keep(v):
    return (v, None)

def back_low(kept, grad):
    return (low(grad),)
low.defvjp(low_keep, low_pass)
low_back.defvjp(back_keep, back_low)

def matmul(left, right):
    return jnp.dot(left, right, precision=lax.Precision.HIGHEST, preferred_element_type=jnp.float32)

def einsum_high(pattern, left, right):
    return jnp.einsum(pattern, left, right, precision=lax.Precision.HIGHEST, preferred_element_type=jnp.float32)

def rms_scale(hidden, gain):
    return hidden * lax.rsqrt(lax.optimization_barrier(jnp.mean(hidden * hidden, axis=-1, keepdims=True)) + 1e-06) * gain

def segment_ids(lengths):
    seg_ends = PROMPT + jnp.cumsum(lengths).astype(jnp.int32)
    places = jnp.arange(GLEN, dtype=jnp.int32)
    later = lax.optimization_barrier(jnp.sum((places[:, None] >= seg_ends[None, :-1]).astype(jnp.int32), axis=1)).astype(jnp.int32)
    return (places >= PROMPT).astype(jnp.int32) + later

def attention(queries, key_heads, value_heads, segments):
    block_rows = math.gcd(GLEN, 512)
    block_count = GLEN // block_rows
    col_index = jnp.arange(GLEN, dtype=jnp.int32)

    def one_block(inputs):
        query_block, row_start = inputs
        row_index = row_start + jnp.arange(block_rows, dtype=jnp.int32)
        row_segments = lax.dynamic_slice_in_dim(segments, row_start, block_rows)
        same_seq = segments[None, :] == row_segments[:, None]
        allowed = (col_index[None, :] <= row_index[:, None]) & (same_seq | (segments[None, :] == 0))
        scores = einsum_high('qhd,khd->hqk', query_block, key_heads)
        scores = low_back(jnp.where(allowed[None], scores, -1e+30))
        row_peak = lax.optimization_barrier(jnp.max(scores, axis=-1, keepdims=True))
        row_exp = jnp.exp(scores - row_peak)
        attn_probs = low(row_exp / lax.optimization_barrier(jnp.sum(row_exp, axis=-1, keepdims=True)))
        return einsum_high('hqk,khd->qhd', attn_probs, value_heads)
    starts = jnp.arange(block_count, dtype=jnp.int32) * block_rows
    outputs = lax.map(jax.checkpoint(one_block), (queries.reshape(block_count, block_rows, HEADS, HD), starts))
    return outputs.reshape(GLEN, HEADS * HD)

def apply_layer(hidden, frozen, adapters, gain_pair, factor, segments, adapter_select_mask):
    w_qkv, output_weight, inward_weight, down_weight = frozen
    projection_first_factor, b_qkv, output_first_factor, output_second_factor, inward_first_factor, inward_second_factor, down_first_factor, down_second_factor = adapters
    normed_rows = low(rms_scale(hidden, gain_pair[0]))
    low_qkv = low(low_back(matmul(normed_rows, projection_first_factor))) * jnp.tile(adapter_select_mask, (1, 3))
    extra = einsum_high('tca,cad->tcd', low_qkv.reshape(GLEN, 3, AR), b_qkv).reshape(GLEN, 3 * D)
    projected = matmul(normed_rows, w_qkv) + extra
    queries = low(low_back(projected[:, :D]).reshape(GLEN, HEADS, HD) * factor)
    key_heads = low(low_back(projected[:, D:2 * D])).reshape(GLEN, HEADS, HD)
    value_heads = low(low_back(projected[:, 2 * D:])).reshape(GLEN, HEADS, HD)
    mixed_rows = low(low_back(attention(queries, key_heads, value_heads, segments)))
    low_out = low(low_back(matmul(mixed_rows, output_first_factor))) * adapter_select_mask
    middle = hidden + low_back(matmul(mixed_rows, output_weight) + matmul(low_out, output_second_factor))
    normed_feed_rows = low(rms_scale(middle, gain_pair[1]))
    low_in = low(low_back(matmul(normed_feed_rows, inward_first_factor))) * adapter_select_mask
    inner = low_back(matmul(normed_feed_rows, inward_weight) + matmul(low_in, inward_second_factor))
    active_adapter = low(jax.nn.silu(inner))
    low_down = low(low_back(matmul(active_adapter, down_first_factor))) * adapter_select_mask
    return middle + low_back(matmul(active_adapter, down_weight) + matmul(low_down, down_second_factor))

def reference(tokens, cont_lengths, adapter_ids, attn_gain, mlp_gain, query_scale, w_qkv, output_weight, inward_weight, down_weight, projection_first_factor, b_qkv, output_first_factor, output_second_factor, inward_first_factor, inward_second_factor, down_first_factor, down_second_factor, cotangent):
    frozen = [weight.astype(jnp.float32) for weight in (w_qkv, output_weight, inward_weight, down_weight)]
    factors = [1.442695041 / math.sqrt(HD) * jax.nn.softplus(query_scale[layer_index]) for layer_index in range(LAYERS)]
    start_adapters = tuple((adapter.astype(jnp.float32) for adapter in (projection_first_factor, b_qkv, output_first_factor, output_second_factor, inward_first_factor, inward_second_factor, down_first_factor, down_second_factor)))

    def forward(inputs, adapters):

        def one_group(carried, group_data):
            hidden, lengths, picked = group_data
            segments = segment_ids(lengths)
            chosen = picked[segments]
            adapter_select_mask = ((jnp.arange(AR, dtype=jnp.int32) // R)[None, :] == chosen[:, None]).astype(jnp.float32)
            for layer_index in range(LAYERS):
                hidden = apply_layer(hidden, [weight[layer_index] for weight in frozen], [adapter[layer_index] for adapter in adapters], (attn_gain[layer_index], mlp_gain[layer_index]), factors[layer_index], segments, adapter_select_mask)
            return (carried, hidden)
        unused, outputs = lax.scan(jax.checkpoint(one_group), jnp.zeros((), jnp.float32), (inputs, cont_lengths, adapter_ids))
        return outputs
    result, pullback = jax.vjp(forward, tokens.astype(jnp.float32), start_adapters)
    grad_in, grad_adapt = pullback(cotangent.astype(jnp.float32))
    return (result.astype(jnp.bfloat16), grad_in, grad_adapt[0], grad_adapt[1], grad_adapt[2], grad_adapt[3], grad_adapt[4], grad_adapt[5], grad_adapt[6], grad_adapt[7])
```

```python
from functools import partial
import math

import jax
import jax.numpy as jnp
from jax import lax
from jax.experimental import pallas as pl
from jax.experimental.pallas import tpu as pltpu
from jax.sharding import PartitionSpec as P

D = 1280
HEADS = 16
HD = 80
R = 16
LAYERS = 2
PROMPT = 2048
CONTS = 2
AR = 128
GLEN = 2560
LOG2E = 1.4426950408889634


def product(left, right):
    return jnp.dot(left, right, preferred_element_type=jnp.float32)


def backward_product(left, right):
    return lax.dot_general(
        left, right, (((1,), (1,)), ((), ())), preferred_element_type=jnp.float32
    )


def product_across(left, right):
    return lax.dot_general(
        left, right, (((0,), (0,)), ((), ())), preferred_element_type=jnp.float32
    )


def rms_scale(hidden, gain):
    return hidden * lax.rsqrt(jnp.mean(hidden * hidden, axis=-1, keepdims=True) + 1e-06) * gain


def norm_grad(hidden, gain, grad_out):
    norm_value, norm_back = jax.vjp(partial(rms_scale, gain=gain), hidden)
    return norm_back(grad_out)[0]


def segment_ids(lengths):
    seg_ends = PROMPT + jnp.cumsum(lengths)
    places = jnp.arange(GLEN, dtype=jnp.int32)
    later = jnp.sum((places[:, None] >= seg_ends[None, :-1]).astype(jnp.int32), axis=1)
    return (places >= PROMPT).astype(jnp.int32) + later


NEG=-1e30
NT=(((1,),(1,)),((),()))
NN=(((1,),(0,)),((),()))
TN=(((0,),(0,)),((),()))
def dg(a,b,d): return lax.dot_general(a,b,d,preferred_element_type=jnp.float32)

def fwd_kernel(bound_ref, heads_ref, out_ref, lse_ref, q_s, k_s, v_s, *, LH, BQ, UN):
    bound=bound_ref[0]
    lane=lax.broadcasted_iota(jnp.int32,(BQ,128),1)
    for h in range(LH):
        for i in range(GLEN//BQ):
            r=slice(i*BQ,(i+1)*BQ)
            for c,s in ((0,q_s),(1,k_s),(2,v_s)):
                x=heads_ref[c,r,h*HD:(h+1)*HD]
                pad=jnp.zeros((BQ,128-HD),jnp.bfloat16) if c<2 else jnp.ones((BQ,128-HD),jnp.bfloat16)
                s[h,r,:]=jnp.concatenate([x,pad],axis=1)
    for i in range(GLEN//BQ):
        q0=i*BQ
        nk=q0+BQ
        d0=q0 if q0<PROMPT else PROMPT
        rows=lax.broadcasted_iota(jnp.int32,(BQ,nk-d0),0)+q0
        cols=lax.broadcasted_iota(jnp.int32,(BQ,nk-d0),1)+d0
        allowed=cols<=rows
        if q0>=PROMPT:
            allowed=allowed&((cols>=bound)|(rows<bound))
        outs=[];lses=jnp.zeros((BQ,128),jnp.float32)
        for h in range(LH):
            qb=q_s[h,q0:q0+BQ,:]
            sd=jnp.where(allowed,dg(qb,k_s[h,d0:nk,:],NT),NEG)
            m=jnp.max(sd,axis=1,keepdims=True)
            if d0>0:
                sp=dg(qb,k_s[h,0:d0,:],NT)
                m=jnp.maximum(m,jnp.max(sp,axis=1,keepdims=True))
                pp=jnp.exp2(sp-m).astype(jnp.bfloat16)
            pd=jnp.exp2(sd-m).astype(jnp.bfloat16)
            acc=dg(pd,v_s[h,d0:nk,:],NN)
            if d0>0: acc=acc+dg(pp,v_s[h,0:d0,:],NN)
            l=acc[:,HD:HD+1]
            outs.append((acc/l)[:,:HD].astype(jnp.bfloat16))
            lses=jnp.where(lane==h,m+jnp.log2(l),lses)
        out_ref[q0:q0+BQ,:]=jnp.concatenate(outs,axis=1)
        lse_ref[q0:q0+BQ,:]=lses

def attend(heads,bound,BQ=256,UN=1):
    LH=heads.shape[2]//HD
    return pl.pallas_call(partial(fwd_kernel,LH=LH,BQ=BQ,UN=UN),
        out_shape=(jax.ShapeDtypeStruct((GLEN,LH*HD),jnp.bfloat16),jax.ShapeDtypeStruct((GLEN,128),jnp.float32)),
        in_specs=[pl.BlockSpec(memory_space=pltpu.SMEM),pl.BlockSpec(memory_space=pltpu.VMEM)],
        out_specs=(pl.BlockSpec(memory_space=pltpu.VMEM),)*2,
        scratch_shapes=[pltpu.VMEM((LH,GLEN,128),jnp.bfloat16)]*3,
        compiler_params=pltpu.CompilerParams(vmem_limit_bytes=56<<20),
        name="attend")(bound,heads)

def split3(x):
    hi=x.astype(jnp.bfloat16); r=x-hi.astype(jnp.float32)
    mid=r.astype(jnp.bfloat16); lo=(r-mid.astype(jnp.float32)).astype(jnp.bfloat16)
    return hi,mid,lo

def bwd_kernel(bound_ref, factor_ref, heads_ref, o_ref, do_ref, lse_ref, out_ref, q_s,k_s,v_s,d_s,kt_s,dqt_s,dq_s, *, LH,BK,QC):
    bound=bound_ref[0]
    BQ=256
    hlane=lax.broadcasted_iota(jnp.int32,(BQ,128),1)
    W=128-HD
    zl=lax.broadcasted_iota(jnp.int32,(BQ,W),1)
    for h in range(LH):
        for i in range(GLEN//BQ):
            r=slice(i*BQ,(i+1)*BQ); cs=slice(h*HD,(h+1)*HD)
            lse=-jnp.sum(jnp.where(hlane==h,lse_ref[r,:],0.0),axis=1,keepdims=True)
            hi,mid,lo=[t.astype(jnp.float32) for t in split3(lse)]
            ext=jnp.where(zl==0,hi,jnp.where(zl==1,mid,jnp.where(zl==2,lo,0.0))).astype(jnp.bfloat16)
            q_s[h,r,:]=jnp.concatenate([heads_ref[0,r,cs],ext],axis=1)
            k_s[h,r,:]=jnp.concatenate([heads_ref[1,r,cs],jnp.ones((BQ,W),jnp.bfloat16)],axis=1)
            v_s[h,r,:]=jnp.concatenate([heads_ref[2,r,cs],jnp.ones((BQ,W),jnp.bfloat16)],axis=1)
            do=do_ref[r,cs]
            delta=-jnp.sum(do.astype(jnp.float32)*o_ref[r,cs].astype(jnp.float32),axis=1,keepdims=True)
            hi,mid,lo=[t.astype(jnp.float32) for t in split3(delta)]
            ext=jnp.where(zl==0,hi,jnp.where(zl==1,mid,jnp.where(zl==2,lo,0.0))).astype(jnp.bfloat16)
            d_s[h,r,:]=jnp.concatenate([do,ext],axis=1)
    for h in range(LH):
        kt_s[...]=k_s[h].T
        for j in range(GLEN//BK):
            k0=j*BK
            kb=k_s[h,k0:k0+BK,:]; vb=v_s[h,k0:k0+BK,:]; ktb=kt_s[:,k0:k0+BK]
            dk=jnp.zeros((BK,128),jnp.float32); dv=jnp.zeros((BK,128),jnp.float32)
            q0=k0
            while q0<GLEN:
                n=BK if q0==k0 else min(QC,GLEN-q0)
                qs=slice(q0,q0+n)
                qb=q_s[h,qs,:]; db=d_s[h,qs,:]
                st=dg(kb,qb,NT)
                p=jnp.exp2(st)
                if q0==k0 or k0>=PROMPT:
                    krow=lax.broadcasted_iota(jnp.int32,(BK,n),0)+k0
                    qcol=lax.broadcasted_iota(jnp.int32,(BK,n),1)+q0
                    al=krow<=qcol
                    if k0>=PROMPT: al=al&((krow>=bound)|(qcol<bound))
                    p=jnp.where(al,p,0.0)
                dp=dg(vb,db,NT)
                ds=(p*dp).astype(jnp.bfloat16)
                dv=dv+dg(p.astype(jnp.bfloat16),db,NN)
                dk=dk+dg(ds,qb,NN)
                dqt=dg(ktb,ds,NN)
                if j==0: dqt_s[:,qs]=dqt
                else: dqt_s[:,qs]+=dqt
                q0+=n
            out_ref[1,k0:k0+BK,h*HD:(h+1)*HD]=(dk[:,:HD]*0.6931471805599453).astype(jnp.bfloat16)
            out_ref[2,k0:k0+BK,h*HD:(h+1)*HD]=dv[:,:HD].astype(jnp.bfloat16)
        for i in range(GLEN//256):
            out_ref[0,i*256:(i+1)*256,h*HD:(h+1)*HD]=(dqt_s[:,i*256:(i+1)*256].T[:,:HD]*factor_ref[0:1,:HD]).astype(jnp.bfloat16)

def attend_back(heads,mixed,grad_heads,lse,bound,factor,BK=256,QC=512):
    LH=heads.shape[2]//HD
    f=jnp.pad(factor.reshape(1,HD),((0,0),(0,128-HD)))
    return pl.pallas_call(partial(bwd_kernel,LH=LH,BK=BK,QC=QC),
        out_shape=jax.ShapeDtypeStruct((3,GLEN,LH*HD),jnp.bfloat16),
        in_specs=[pl.BlockSpec(memory_space=pltpu.SMEM)]+[pl.BlockSpec(memory_space=pltpu.VMEM)]*5,
        out_specs=pl.BlockSpec(memory_space=pltpu.VMEM),
        scratch_shapes=[pltpu.VMEM((LH,GLEN,128),jnp.bfloat16)]*4+[pltpu.VMEM((128,GLEN),jnp.bfloat16),pltpu.VMEM((128,GLEN),jnp.float32),pltpu.VMEM((8,128),jnp.float32)],
        compiler_params=pltpu.CompilerParams(vmem_limit_bytes=60<<20),
        name="attend_back")(bound,f,heads,mixed,grad_heads,lse)


def forward_layer(hidden, pieces, gain_pair, factor, segments, mask_low):
    (
        w_qkv,
        output_weight,
        inward_weight,
        down_weight,
        projection_first_factor,
        output_first_factor,
        inward_first_factor,
        down_first_factor,
        b_qkv,
        output_second_factor,
        inward_second_factor,
        down_second_factor,
    ) = pieces
    row_count = hidden.shape[0]
    normed_rows = rms_scale(hidden, gain_pair[0]).astype(jnp.bfloat16)
    low_qkv = product(normed_rows, projection_first_factor).astype(jnp.bfloat16) * jnp.tile(
        mask_low, (1, 3)
    )
    projected = jnp.einsum(
        "td,dce->cte", normed_rows, w_qkv.reshape(D, 3, D), preferred_element_type=jnp.float32
    )
    projected = projected + jnp.einsum(
        "tca,cae->cte", low_qkv.reshape(row_count, 3, AR), b_qkv, preferred_element_type=jnp.float32
    )
    scaling = jnp.concatenate([jnp.tile(factor * LOG2E, HEADS), jnp.ones((2 * D,), jnp.float32)]).reshape(
        3, 1, D
    )
    heads = lax.all_to_all(
        (projected * scaling).astype(jnp.bfloat16), "seq", split_axis=2, concat_axis=1, tiled=True
    )
    mixed_heads, log_sums = attend(heads, segments)
    mixed_rows = lax.all_to_all(mixed_heads, "seq", split_axis=0, concat_axis=1, tiled=True)
    low_out = product(mixed_rows, output_first_factor).astype(jnp.bfloat16) * mask_low
    middle = hidden + product(mixed_rows, output_weight) + product(low_out, output_second_factor)
    normed_feed_rows = rms_scale(middle, gain_pair[1]).astype(jnp.bfloat16)
    low_in = product(normed_feed_rows, inward_first_factor).astype(jnp.bfloat16) * mask_low
    inner = product(normed_feed_rows, inward_weight) + product(low_in, inward_second_factor)
    active_adapter = jax.nn.silu(inner).astype(jnp.bfloat16)
    low_down = product(active_adapter, down_first_factor).astype(jnp.bfloat16) * mask_low
    result = middle + product(active_adapter, down_weight) + product(low_down, down_second_factor)
    return (
        result,
        (
            hidden,
            normed_rows,
            low_qkv,
            heads,
            mixed_heads,
            log_sums,
            mixed_rows,
            low_out,
            middle,
            normed_feed_rows,
            low_in,
            inner,
            active_adapter,
            low_down,
        ),
    )


def backward_layer(grad_flow, stored, pieces, gain_pair, factor, segments, adapter_select_mask):
    (
        w_qkv,
        output_weight,
        inward_weight,
        down_weight,
        projection_first_factor,
        output_first_factor,
        inward_first_factor,
        down_first_factor,
        b_qkv,
        output_second_factor,
        inward_second_factor,
        down_second_factor,
    ) = pieces
    (
        hidden,
        normed_rows,
        low_qkv,
        heads,
        mixed_heads,
        log_sums,
        mixed_rows,
        low_out,
        middle,
        normed_feed_rows,
        low_in,
        inner,
        active_adapter,
        low_down,
    ) = stored
    row_count = hidden.shape[0]
    low_rank_gradient = grad_flow.astype(jnp.bfloat16)
    down_adapter_term = (
        adapter_select_mask * backward_product(low_rank_gradient, down_second_factor)
    ).astype(jnp.bfloat16)
    active_adapter_gradient = backward_product(low_rank_gradient, down_weight) + backward_product(
        down_adapter_term, down_first_factor
    )
    grad_b_down = product_across(low_down, low_rank_gradient)
    down_first_gradient = product_across(active_adapter, down_adapter_term)
    silu_value, silu_back = jax.vjp(jax.nn.silu, inner)
    inner_gradient = silu_back(active_adapter_gradient)[0].astype(jnp.bfloat16)
    inward_adapter_term = (
        adapter_select_mask * backward_product(inner_gradient, inward_second_factor)
    ).astype(jnp.bfloat16)
    normed_feed_gradient = backward_product(inner_gradient, inward_weight) + backward_product(
        inward_adapter_term, inward_first_factor
    )
    grad_b_in = product_across(low_in, inner_gradient)
    inward_first_gradient = product_across(normed_feed_rows, inward_adapter_term)
    grad_flow = grad_flow + norm_grad(middle, gain_pair[1], normed_feed_gradient)
    low_rank_gradient = grad_flow.astype(jnp.bfloat16)
    output_adapter_term = (
        adapter_select_mask * backward_product(low_rank_gradient, output_second_factor)
    ).astype(jnp.bfloat16)
    mixed_gradient = (
        backward_product(low_rank_gradient, output_weight)
        + backward_product(output_adapter_term, output_first_factor)
    ).astype(jnp.bfloat16)
    grad_b_out = product_across(low_out, low_rank_gradient)
    output_first_gradient = product_across(mixed_rows, output_adapter_term)
    grad_heads = lax.all_to_all(mixed_gradient, "seq", split_axis=1, concat_axis=0, tiled=True)
    head_grads = attend_back(heads, mixed_heads, grad_heads, log_sums, segments, factor)
    grad_proj = lax.all_to_all(head_grads, "seq", split_axis=1, concat_axis=2, tiled=True)
    adapter_terms = jnp.einsum(
        "ctd,cad->tca", grad_proj, b_qkv, preferred_element_type=jnp.float32
    ).reshape(row_count, 3 * AR)
    projection_adapter_term = (jnp.tile(adapter_select_mask, (1, 3)) * adapter_terms).astype(
        jnp.bfloat16
    )
    normed_gradient = lax.dot_general(
        grad_proj,
        w_qkv.reshape(D, 3, D),
        (((0, 2), (1, 2)), ((), ())),
        preferred_element_type=jnp.float32,
    )
    normed_gradient = normed_gradient + backward_product(
        projection_adapter_term, projection_first_factor
    )
    grad_b_qkv = jnp.einsum(
        "tca,ctd->cad",
        low_qkv.reshape(row_count, 3, AR),
        grad_proj,
        preferred_element_type=jnp.float32,
    )
    projection_first_gradient = product_across(normed_rows, projection_adapter_term)
    grad_flow = grad_flow + norm_grad(hidden, gain_pair[0], normed_gradient)
    return (
        grad_flow,
        (
            projection_first_gradient,
            grad_b_qkv,
            output_first_gradient,
            grad_b_out,
            inward_first_gradient,
            grad_b_in,
            down_first_gradient,
            grad_b_down,
        ),
    )


def reduce_layer(grads):
    shared = (
        lax.psum_scatter(
            grads[0].astype(jnp.bfloat16), "fsdp", scatter_dimension=0, tiled=True
        ).astype(jnp.float32),
        lax.psum_scatter(
            grads[1].astype(jnp.bfloat16), "fsdp", scatter_dimension=2, tiled=True
        ).astype(jnp.float32),
        lax.psum_scatter(
            grads[2].astype(jnp.bfloat16), "fsdp", scatter_dimension=0, tiled=True
        ).astype(jnp.float32),
        lax.psum_scatter(
            grads[3].astype(jnp.bfloat16), "fsdp", scatter_dimension=1, tiled=True
        ).astype(jnp.float32),
        lax.psum_scatter(
            grads[4].astype(jnp.bfloat16), "fsdp", scatter_dimension=0, tiled=True
        ).astype(jnp.float32),
        lax.psum_scatter(
            grads[5].astype(jnp.bfloat16), "fsdp", scatter_dimension=1, tiled=True
        ).astype(jnp.float32),
        lax.psum_scatter(
            grads[6].astype(jnp.bfloat16), "fsdp", scatter_dimension=0, tiled=True
        ).astype(jnp.float32),
        lax.psum_scatter(
            grads[7].astype(jnp.bfloat16), "fsdp", scatter_dimension=1, tiled=True
        ).astype(jnp.float32),
    )
    return (
        lax.psum(shared[0].astype(jnp.bfloat16), "seq").astype(jnp.float32),
        lax.psum(shared[1].astype(jnp.bfloat16), "seq").astype(jnp.float32),
        lax.psum(shared[2].astype(jnp.bfloat16), "seq").astype(jnp.float32),
        lax.psum(shared[3].astype(jnp.bfloat16), "seq").astype(jnp.float32),
        lax.psum(shared[4].astype(jnp.bfloat16), "seq").astype(jnp.float32),
        lax.psum(shared[5].astype(jnp.bfloat16), "seq").astype(jnp.float32),
        lax.psum(shared[6].astype(jnp.bfloat16), "seq").astype(jnp.float32),
        lax.psum(shared[7].astype(jnp.bfloat16), "seq").astype(jnp.float32),
    )


def local(
    tokens,
    cont_lengths,
    adapter_ids,
    attn_gain,
    mlp_gain,
    query_scale,
    w_qkv,
    output_weight,
    inward_weight,
    down_weight,
    projection_first_factor,
    b_qkv,
    output_first_factor,
    output_second_factor,
    inward_first_factor,
    inward_second_factor,
    down_first_factor,
    down_second_factor,
    cotangent,
):
    row_count = tokens.shape[1]
    bound = PROMPT + cont_lengths[0, :1]
    segments = segment_ids(cont_lengths[0])
    local_segments = lax.dynamic_slice_in_dim(
        segments, lax.axis_index("seq") * row_count, row_count
    )
    matches = local_segments[:, None] == jnp.arange(CONTS + 1, dtype=jnp.int32)[None, :]
    chosen = jnp.sum(jnp.where(matches, adapter_ids[0][None, :], 0), axis=1)
    adapter_select_mask = (
        (jnp.arange(AR, dtype=jnp.int32) // R)[None, :] == chosen[:, None]
    ).astype(jnp.float32)
    mask_low = adapter_select_mask.astype(jnp.bfloat16)
    hidden = tokens[0].astype(jnp.float32)
    kept_pieces = []
    stored_all = []
    factors = []
    for layer_index in range(LAYERS):
        pieces = (
            lax.all_gather(w_qkv[layer_index], "fsdp", axis=0, tiled=True),
            lax.all_gather(output_weight[layer_index], "fsdp", axis=0, tiled=True),
            lax.all_gather(inward_weight[layer_index], "fsdp", axis=0, tiled=True),
            lax.all_gather(down_weight[layer_index], "fsdp", axis=0, tiled=True),
            lax.all_gather(projection_first_factor[layer_index], "fsdp", axis=0, tiled=True),
            lax.all_gather(output_first_factor[layer_index], "fsdp", axis=0, tiled=True),
            lax.all_gather(inward_first_factor[layer_index], "fsdp", axis=0, tiled=True),
            lax.all_gather(down_first_factor[layer_index], "fsdp", axis=0, tiled=True),
            lax.all_gather(b_qkv[layer_index], "fsdp", axis=2, tiled=True),
            lax.all_gather(output_second_factor[layer_index], "fsdp", axis=1, tiled=True),
            lax.all_gather(inward_second_factor[layer_index], "fsdp", axis=1, tiled=True),
            lax.all_gather(down_second_factor[layer_index], "fsdp", axis=1, tiled=True),
        )
        factor = 1.442695041 / math.sqrt(HD) * jax.nn.softplus(query_scale[layer_index])
        hidden, stored = forward_layer(
            hidden,
            pieces,
            (attn_gain[layer_index], mlp_gain[layer_index]),
            factor,
            bound,
            mask_low,
        )
        kept_pieces.append(pieces)
        stored_all.append(stored)
        factors.append(factor)
    layer_output = hidden.astype(jnp.bfloat16)[None]
    grad_flow = cotangent[0].astype(jnp.float32)
    layer_sums = [None] * LAYERS
    for layer_index in reversed(range(LAYERS)):
        pieces = (
            lax.all_gather(w_qkv[layer_index], "fsdp", axis=0, tiled=True),
            lax.all_gather(output_weight[layer_index], "fsdp", axis=0, tiled=True),
            lax.all_gather(inward_weight[layer_index], "fsdp", axis=0, tiled=True),
            lax.all_gather(down_weight[layer_index], "fsdp", axis=0, tiled=True),
            lax.all_gather(projection_first_factor[layer_index], "fsdp", axis=0, tiled=True),
            lax.all_gather(output_first_factor[layer_index], "fsdp", axis=0, tiled=True),
            lax.all_gather(inward_first_factor[layer_index], "fsdp", axis=0, tiled=True),
            lax.all_gather(down_first_factor[layer_index], "fsdp", axis=0, tiled=True),
            lax.all_gather(b_qkv[layer_index], "fsdp", axis=2, tiled=True),
            lax.all_gather(output_second_factor[layer_index], "fsdp", axis=1, tiled=True),
            lax.all_gather(inward_second_factor[layer_index], "fsdp", axis=1, tiled=True),
            lax.all_gather(down_second_factor[layer_index], "fsdp", axis=1, tiled=True),
        )
        grad_flow, grads = backward_layer(
            grad_flow,
            stored_all[layer_index],
            pieces,
            (attn_gain[layer_index], mlp_gain[layer_index]),
            factors[layer_index],
            bound,
            adapter_select_mask,
        )
        layer_sums[layer_index] = reduce_layer(grads)
    stacked = [
        jnp.stack([layer_sums[depth_index][member] for depth_index in range(LAYERS)])
        for member in range(8)
    ]
    return (
        layer_output,
        grad_flow[None],
        stacked[0],
        stacked[1],
        stacked[2],
        stacked[3],
        stacked[4],
        stacked[5],
        stacked[6],
        stacked[7],
    )


def solution(mesh):
    return jax.shard_map(
        local,
        mesh=mesh,
        in_specs=(
            P("fsdp", "seq", None),
            P("fsdp", None),
            P("fsdp", None),
            P(),
            P(),
            P(),
            P(None, "fsdp", None),
            P(None, "fsdp", None),
            P(None, "fsdp", None),
            P(None, "fsdp", None),
            P(None, "fsdp", None),
            P(None, None, None, "fsdp"),
            P(None, "fsdp", None),
            P(None, None, "fsdp"),
            P(None, "fsdp", None),
            P(None, None, "fsdp"),
            P(None, "fsdp", None),
            P(None, None, "fsdp"),
            P("fsdp", "seq", None),
        ),
        out_specs=(
            P("fsdp", "seq", None),
            P("fsdp", "seq", None),
            P(None, "fsdp", None),
            P(None, None, None, "fsdp"),
            P(None, "fsdp", None),
            P(None, None, "fsdp"),
            P(None, "fsdp", None),
            P(None, None, "fsdp"),
            P(None, "fsdp", None),
            P(None, None, "fsdp"),
        ),
        check_vma=False,
    )
```

```python
from functools import partial
import math

import jax
import jax.numpy as jnp
from jax import lax
from jax.experimental import pallas as pl
from jax.experimental.pallas import tpu as pltpu
from jax.sharding import PartitionSpec as P

D = 1280
HEADS = 16
HD = 80
R = 16
LAYERS = 2
PROMPT = 2048
AR = 128
GLEN = 2560
LOG2E = 1.4426950408889634
LN2 = 0.6931471805599453
ROFF = 8
NEG = -1e30
BLOCK = 256
CHUNK = 512
WIDE = D + AR
PART = D + 2 * AR
SIDE = 3 * PART
BF = jnp.bfloat16
F32 = jnp.float32
NN = (((1,), (0,)), ((), ()))
NT = (((1,), (1,)), ((), ()))
VMEM = pl.BlockSpec(memory_space=pltpu.VMEM)
SMEM = pl.BlockSpec(memory_space=pltpu.SMEM)
HBM = pl.BlockSpec(memory_space=pl.ANY)


def dot(left, right, dims=NN):
    return lax.dot_general(left, right, dims, preferred_element_type=F32)


def call(kernel, name, outs, specs, scratch, expected, out_specs=None):
    return pl.pallas_call(
        kernel,
        out_shape=outs,
        in_specs=specs,
        out_specs=tuple(VMEM for _ in outs) if out_specs is None else out_specs,
        scratch_shapes=scratch,
        compiler_params=pltpu.CompilerParams(vmem_limit_bytes=60 << 20),
        cost_estimate=pl.CostEstimate(
            flops=int(expected * 1.15e9), bytes_accessed=1024, transcendentals=0
        ),
        name=name,
    )


def shape(dims, kind=BF):
    return jax.ShapeDtypeStruct(dims, kind)


def sigmoid(v):
    return 1.0 / (1.0 + jnp.exp(-v))


def row_mask(meta, base, count):
    rows = lax.broadcasted_iota(jnp.int32, (count, AR), 0) + base
    lane = lax.broadcasted_iota(jnp.int32, (count, AR), 1)
    chosen = jnp.where(rows < PROMPT, meta[0], jnp.where(rows < meta[3], meta[1], meta[2]))
    low = chosen * R
    return jnp.where((lane >= low) & (lane < low + R), 1.0, 0.0).astype(F32)


def columns_of(ref, at, width):
    return ref if width == ref.shape[1] else ref.at[:, pl.ds(at, width)]


def head_copies(meta, pieces, wq_s, cb_s, sems):
    core, both = meta[5], 3 * AR
    n = len(pieces) // 2
    single = n == 1 and pieces[0].shape[0] == 1
    copies, block_at = [], 0
    for own, other in zip(pieces[:n], pieces[n:]):
        blocks, rows, columns = own.shape
        for block in range(blocks):
            at = 0 if single else pl.multiple_of(meta[ROFF + block_at], math.gcd(rows, 256))
            into = pl.ds(at, rows)
            for source, target in (
                (own.at[block, :, :both], cb_s.at[into, pl.ds(pl.multiple_of(core * both, both), both)]),
                (other.at[block], cb_s.at[into, pl.ds(pl.multiple_of((1 - core) * both, both), both)]),
                (own.at[block, :, both:], wq_s.at[into]),
            ):
                copies.append(pltpu.make_async_copy(source, target, sems.at[len(copies)]))
            block_at += 1
    return copies


def side_copies(meta, own, other, which, r_s, sems):
    half = PART // 2
    return [
        pltpu.make_async_copy(
            columns_of(ref, which * half, half),
            columns_of(r_s, pl.multiple_of(which * PART + side * half, half), half),
            sems.at[which, k],
        )
        for k, (ref, side) in enumerate(((own, meta[5]), (other, 1 - meta[5])))
    ]


def start_all(copies):
    for copy in copies:
        copy.start()
    return copies


def wait_all(copies):
    for copy in copies:
        copy.wait()


def run_copies(copies):
    wait_all(start_all(copies))


def fill_second(meta, cb_s, bd_s, width, group):
    bd_s[...] = jnp.zeros_like(bd_s)
    for p in range(width // group):
        start = pl.multiple_of(meta[4] * width + p * group, math.gcd(group, 256))
        for c in range(3):
            at = (p * 3 + c) * group
            bd_s[at : at + group, c * AR : (c + 1) * AR] = cb_s[
                pl.ds(start, group), (3 + c) * AR : (4 + c) * AR
            ]


def project_kernel(*refs, arrays, pieces, parts, block):
    meta, scale = refs[:2]
    tokens = refs[2 : 2 + arrays]
    weights = refs[2 + arrays : 2 + arrays + pieces]
    heads = refs[2 + arrays + pieces : 2 + arrays + pieces + parts]
    low_out, wq_s, cb_s, bd_s, sems = refs[2 + arrays + pieces + parts :]
    run_copies(head_copies(meta, weights, wq_s, cb_s, sems))
    columns = wq_s.shape[1]
    each = columns // parts
    fill_second(meta, cb_s, bd_s, columns // 3, each // 3)
    for k in range(arrays):
        rows = tokens[k].shape[0]
        local = 0 if arrays == 1 else (meta[5] if k == 0 else 1 - meta[5]) * rows

        def step(i, carry, k=k, local=local):
            x = tokens[k][pl.ds(pl.multiple_of(i * block, 64), block), :]
            place = pl.multiple_of(local + i * block, 64)
            mask = row_mask(meta, meta[7] + place, block)
            low = dot(x, cb_s[:, : 3 * AR]) * jnp.concatenate([mask] * 3, axis=1)
            low = low.astype(BF)
            low_out[pl.ds(place, block), :] = low
            both = ((dot(x, wq_s[...]) + dot(low, bd_s[...], NT)) * scale[...]).astype(BF)
            for p in range(parts):
                heads[p][pl.ds(place, block), :] = both[:, p * each : (p + 1) * each]
            return carry

        lax.fori_loop(0, rows // block, step, 0)


def project(meta, scale, tokens, weights, base, parts):
    arrays = len(tokens)
    rows = tokens[0].shape[0]
    count = rows * arrays
    columns = scale.shape[1]
    return call(
        partial(
            project_kernel, arrays=arrays, pieces=len(weights), parts=parts, block=320
        ),
        "project",
        (shape((count, columns // parts)),) * parts + (shape((count, 3 * AR)),),
        [SMEM, VMEM] + [VMEM] * arrays + [HBM] * len(weights),
        [
            pltpu.VMEM((D, columns), BF),
            pltpu.VMEM((D, 6 * AR), BF),
            pltpu.VMEM((columns, 3 * AR), BF),
            pltpu.SemaphoreType.DMA((3 * sum(w.shape[0] for w in weights),)),
        ],
        13,
    )(meta.at[7].set(base), scale, *tokens, *weights)


def load_rows(meta, sources, target, sems):
    copies = []
    for index, ref in enumerate(sources):
        rows = ref.shape[0]
        if len(sources) == 1:
            into = target
        else:
            into = target.at[pl.ds(pl.multiple_of(meta[6] * rows if index == 0 else (1 - meta[6]) * rows, 256), rows)]
        copies.append(pltpu.make_async_copy(ref, into, sems.at[index]))
    run_copies(copies)


def allowed_pairs(meta, queries, keys, query_at, key_at):
    same = (keys >= meta[3]) | (queries < meta[3])
    causal = keys <= queries
    return causal & same if key_at >= PROMPT else causal


def attend_kernel(*refs, groups, local_heads):
    meta = refs[0]
    sources = refs[1 : 1 + groups]
    out, lse, hs, q_s, k_s, v_s, sems = refs[1 + groups :]
    load_rows(meta, sources, hs, sems)
    width = local_heads * HD
    span = out.shape[2]
    lane = lax.broadcasted_iota(jnp.int32, (BLOCK, 128), 1)
    for h in range(local_heads):
        for i in range(GLEN // BLOCK):
            r = slice(i * BLOCK, (i + 1) * BLOCK)
            for c, ref in ((0, q_s), (1, k_s), (2, v_s)):
                x = hs[r, c * width + h * HD : c * width + (h + 1) * HD]
                fill = jnp.ones if c == 2 else jnp.zeros
                ref[h, r, :] = jnp.concatenate([x, fill((BLOCK, 128 - HD), BF)], axis=1)

    def head(h, carry):
        place = pl.multiple_of(h * HD, 16)
        for i in range(GLEN // BLOCK):
            q0 = i * BLOCK
            nk = q0 + BLOCK
            d0 = min(q0, PROMPT)
            rows = lax.broadcasted_iota(jnp.int32, (BLOCK, nk - d0), 0) + q0
            cols = lax.broadcasted_iota(jnp.int32, (BLOCK, nk - d0), 1) + d0
            qb = q_s[h, q0 : q0 + BLOCK, :]
            sd = jnp.where(
                allowed_pairs(meta, rows, cols, q0, d0), dot(qb, k_s[h, d0:nk, :], NT), NEG
            )
            peak = jnp.max(sd, axis=1, keepdims=True)
            if d0 > 0:
                sp = dot(qb, k_s[h, 0:d0, :], NT)
                peak = jnp.maximum(peak, jnp.max(sp, axis=1, keepdims=True))
            total = dot(jnp.exp2(sd - peak).astype(BF), v_s[h, d0:nk, :])
            if d0 > 0:
                total = total + dot(jnp.exp2(sp - peak).astype(BF), v_s[h, 0:d0, :])
            turned = jnp.where(lane == HD + 1, peak, total).T
            rowsum = turned[HD : HD + 1, :]
            lse[pl.ds(h, 1), q0 : q0 + BLOCK] = turned[HD + 1 : HD + 2, :] + jnp.log2(rowsum)
            result = (turned[:HD, :] * (1.0 / rowsum)).astype(BF)
            for part in range(BLOCK // 128):
                t = q0 + part * 128
                out[t // span, pl.ds(place, HD), t % span : t % span + 128] = result[
                    :, part * 128 : (part + 1) * 128
                ]
        return carry

    lax.fori_loop(0, local_heads, head, 0)


def attend(meta, heads, span):
    width = heads[0].shape[1]
    local_heads = width // (3 * HD)
    return call(
        partial(attend_kernel, groups=len(heads), local_heads=local_heads),
        "attend",
        (shape((GLEN // span, local_heads * HD, span)), shape((8, GLEN), F32)),
        [SMEM] + [HBM] * len(heads),
        [pltpu.VMEM((GLEN, width), BF)]
        + [pltpu.VMEM((local_heads, GLEN, 128), BF)] * 3
        + [pltpu.SemaphoreType.DMA((len(heads),))],
        16,
    )(meta, *heads)


def three_parts(x):
    high = x.astype(BF).astype(F32)
    rest = x - high
    middle = rest.astype(BF).astype(F32)
    return high, middle, (rest - middle).astype(BF).astype(F32)


def attend_back_kernel(*refs, groups, local_heads):
    meta, factor = refs[:2]
    sources = refs[2 : 2 + groups]
    o_ref, do_ref, lse = refs[2 + groups : 5 + groups]
    out, hs, q_s, k_s, v_s, d_s, qt_s, dt_s, kt_s, dqt_s, dq_s, dk_s, dv_s, sems = refs[5 + groups :]
    load_rows(meta, sources, hs, sems)
    width = local_heads * HD
    span = o_ref.shape[2]
    zero_row = lax.broadcasted_iota(jnp.int32, (128 - HD, 128), 0)

    def extra_rows(value):
        a, b, c = three_parts(value)
        return jnp.where(
            zero_row == 0, a, jnp.where(zero_row == 1, b, jnp.where(zero_row == 2, c, 0.0))
        ).astype(BF)

    for h in range(local_heads):
        cs = slice(h * HD, (h + 1) * HD)
        for i in range(GLEN // 128):
            r = slice(i * 128, (i + 1) * 128)
            t, inner = (i * 128) // span, slice((i * 128) % span, (i * 128) % span + 128)
            ones = jnp.ones((128, 128 - HD), BF)
            q = jnp.concatenate([hs[r, h * HD : (h + 1) * HD], jnp.zeros_like(ones)], axis=1)
            q_s[h, r, :] = q
            k_s[h, r, :] = jnp.concatenate(
                [hs[r, width + h * HD : width + (h + 1) * HD], ones], axis=1
            )
            v_s[h, r, :] = jnp.concatenate(
                [hs[r, 2 * width + h * HD : 2 * width + (h + 1) * HD], ones], axis=1
            )
            qt_s[h, :HD, r] = q.T[:HD, :]
            qt_s[h, HD:, r] = extra_rows(-lse[h : h + 1, r])
            do = do_ref[t, cs, inner]
            delta = jnp.sum(do.astype(F32) * o_ref[t, cs, inner].astype(F32), axis=0, keepdims=True)
            dt = jnp.concatenate([do, extra_rows(-delta)], axis=0)
            dt_s[h, :, r] = dt
            d_s[h, r, :] = dt.T

    def head(h, carry):
        for i in range(GLEN // BLOCK):
            kt_s[:, i * BLOCK : (i + 1) * BLOCK] = k_s[h, i * BLOCK : (i + 1) * BLOCK, :].T
        for j in range(GLEN // BLOCK):
            k0 = j * BLOCK
            kb = k_s[h, k0 : k0 + BLOCK, :]
            vb = v_s[h, k0 : k0 + BLOCK, :]
            dk = jnp.zeros((BLOCK, 128), F32)
            dv = jnp.zeros((BLOCK, 128), F32)
            q0 = k0
            while q0 < GLEN:
                n = BLOCK if q0 == k0 else min(CHUNK, GLEN - q0)
                qs = slice(q0, q0 + n)
                probs = jnp.exp2(dot(kb, qt_s[h, :, qs]))
                if q0 == k0 or k0 >= PROMPT:
                    keys = lax.broadcasted_iota(jnp.int32, (BLOCK, n), 0) + k0
                    queries = lax.broadcasted_iota(jnp.int32, (BLOCK, n), 1) + q0
                    probs = jnp.where(allowed_pairs(meta, queries, keys, q0, k0), probs, 0.0)
                dscore = (probs * dot(vb, dt_s[h, :, qs])).astype(BF)
                dv = dv + dot(probs.astype(BF), d_s[h, qs, :])
                dk = dk + dot(dscore, q_s[h, qs, :])
                dq = dot(kt_s[:, k0 : k0 + BLOCK], dscore)
                if j == 0:
                    dqt_s[:, qs] = dq
                else:
                    dqt_s[:, qs] += dq
                q0 += n
            dk_s[h, k0 : k0 + BLOCK, :] = (dk * LN2).astype(BF)
            dv_s[h, k0 : k0 + BLOCK, :] = dv.astype(BF)
        for i in range(GLEN // BLOCK):
            r = slice(i * BLOCK, (i + 1) * BLOCK)
            dq_s[h, r, :] = (dqt_s[:, r].T * factor[...]).astype(BF)
        return carry

    lax.fori_loop(0, local_heads, head, 0)
    for i in range(GLEN // BLOCK):
        r = slice(i * BLOCK, (i + 1) * BLOCK)
        out[r, :] = jnp.concatenate(
            [ref[h, r, :HD] for ref in (dq_s, dk_s, dv_s) for h in range(local_heads)], axis=1
        )


def attend_back(meta, factor, heads, mixed, grad_mixed, lse):
    width = heads[0].shape[1]
    local_heads = width // (3 * HD)
    rows = pltpu.VMEM((local_heads, GLEN, 128), BF)
    turned = pltpu.VMEM((local_heads, 128, GLEN), BF)
    return call(
        partial(attend_back_kernel, groups=len(heads), local_heads=local_heads),
        "attend_back",
        (shape((GLEN, width)),),
        [SMEM, VMEM] + [HBM] * len(heads) + [VMEM] * 3,
        [pltpu.VMEM((GLEN, width), BF)]
        + [rows] * 4
        + [turned] * 2
        + [pltpu.VMEM((128, GLEN), BF), pltpu.VMEM((128, GLEN), F32)]
        + [rows] * 3
        + [pltpu.SemaphoreType.DMA((len(heads),))],
        0.05,
    )(meta, factor, *heads, mixed, grad_mixed, lse)[0]


def rms_of(value):
    return lax.rsqrt(jnp.mean(value * value, axis=-1, keepdims=True) + 1e-06)


def feed_kernel(*refs, parts, pieces, block, last):
    meta, gain_mlp, gain_next, hidden_in = refs[:4]
    mixed = refs[4 : 4 + parts]
    weights = refs[4 + parts : 4 + parts + pieces]
    refs = refs[4 + parts + pieces :]
    middle_out, inner_out, low_out, result = refs[:4]
    normed_out = None if last else refs[4]
    hidden, middle_s, inner_s, r_s, mt_s, mx_s, sems, io_sems = refs[4 if last else 5 :]
    rows = hidden.shape[0]
    loads, slot = [], 0
    for p in range(parts):
        sources, group, _ = mixed[p].shape
        for source in range(sources):
            at = (source * parts + p) * group
            loads.append(
                pltpu.make_async_copy(
                    mixed[p].at[source], mt_s.at[at : at + group], io_sems.at[len(loads)]
                )
            )
    start_all(loads)
    load_hidden = pltpu.make_async_copy(hidden_in, hidden, io_sems.at[len(loads)])
    load_hidden.start()
    copies = [start_all(side_copies(meta, *weights, which, r_s, sems)) for which in range(3)]
    wait_all(loads)
    for i in range(0, rows, 128):
        n = min(128, rows - i)
        mx_s[i : i + n, :] = mt_s[:, i : i + n].T
    load_hidden.wait()

    def stage(which, body):
        wait_all(copies[which])

        def step(i, carry):
            r = pl.ds(pl.multiple_of(i * block, 64), block)
            mask = row_mask(meta, meta[4] * rows + i * block, block)

            def adapted(x):
                both = dot(x, r_s[:, which * PART : which * PART + WIDE])
                low = (both[:, D:] * mask).astype(BF)
                low_out[r, which * AR : (which + 1) * AR] = low
                return both[:, :D] + dot(low, r_s[:, which * PART + WIDE : (which + 1) * PART], NT)

            body(r, adapted)
            return carry

        lax.fori_loop(0, rows // block, step, 0)

    def out_stage(r, adapted):
        middle_s[r, :] = hidden[r, :] + adapted(mx_s[r, :])

    def in_stage(r, adapted):
        middle = middle_s[r, :]
        inner_s[r, :] = adapted((middle * rms_of(middle) * gain_mlp[...]).astype(BF))

    def down_stage(r, adapted):
        inner = inner_s[r, :]
        value = middle_s[r, :] + adapted((inner * sigmoid(inner)).astype(BF))
        result[r, :] = value.astype(result.dtype)
        if not last:
            normed_out[r, :] = (value * rms_of(value) * gain_next[...]).astype(BF)

    stage(0, out_stage)
    store_middle = pltpu.make_async_copy(middle_s, middle_out, io_sems.at[len(loads) + 1])
    store_middle.start()
    stage(1, in_stage)
    store_inner = pltpu.make_async_copy(inner_s, inner_out, io_sems.at[len(loads) + 2])
    store_inner.start()
    stage(2, down_stage)
    store_middle.wait()
    store_inner.wait()


def feed(meta, gain_mlp, gain_next, mixed, hidden, weights, last):
    rows = hidden.shape[0]
    row = pltpu.VMEM((rows, D), F32)
    outs = (shape((rows, D), F32), shape((rows, D), F32), shape((rows, 3 * AR)))
    outs += (shape((rows, D), BF),) if last else (shape((rows, D), F32), shape((rows, D), BF))
    return call(
        partial(
            feed_kernel,
            parts=len(mixed),
            pieces=2,
            block=math.gcd(rows, 320),
            last=last,
        ),
        "feed",
        outs,
        [SMEM] + [VMEM] * 2 + [HBM] * (1 + len(mixed) + 2),
        [
            row,
            row,
            row,
            pltpu.VMEM((D, SIDE), BF),
            pltpu.VMEM((D, rows), BF),
            pltpu.VMEM((rows, D), BF),
            pltpu.SemaphoreType.DMA((3, 2)),
            pltpu.SemaphoreType.DMA((sum(m.shape[0] for m in mixed) + 3,)),
        ],
        17,
        out_specs=(HBM, HBM) + (VMEM,) * (len(outs) - 2),
    )(meta, gain_mlp, gain_next, hidden, *mixed, *weights)


def rms_back(grad, value, gain, grad_normed):
    r = rms_of(value)
    e = gain * grad_normed
    return grad + r * e - value * (r * r * r) * jnp.mean(value * e, axis=-1, keepdims=True)


def feed_back_kernel(*refs, parts, pieces, block):
    meta, gain_mlp, grad_hbm, middle_hbm, inner_hbm = refs[:5]
    weights = refs[5 : 5 + pieces]
    refs = refs[5 + pieces :]
    grad_out, gi_s, gm_s, dl_s, il_s = refs[:5]
    mixed_grad = refs[5 : 5 + parts]
    grad_in, middle_s, inner_s, r_s, sems, io_sems = refs[5 + parts :]
    rows = grad_in.shape[0]
    loads = start_all(
        [
            pltpu.make_async_copy(source, target, io_sems.at[k])
            for k, (source, target) in enumerate(
                ((grad_hbm, grad_in), (inner_hbm, inner_s), (middle_hbm, middle_s))
            )
        ]
    )
    copies = {which: start_all(side_copies(meta, *weights, which, r_s, sems)) for which in (2, 1, 0)}

    def rows_of(i):
        return pl.ds(pl.multiple_of(i * block, 64), block)

    def narrow(g, which, i):
        mask = row_mask(meta, meta[4] * rows + i * block, block)
        return (dot(g, r_s[:, which * PART + WIDE : (which + 1) * PART]) * mask).astype(BF)

    def across(g, low, which):
        both = jnp.concatenate([g, low], axis=1)
        return dot(both, r_s[:, which * PART : which * PART + WIDE], NT)

    def down_stage(i, carry):
        r = rows_of(i)
        gl = grad_in[r, :].astype(BF)
        dl = narrow(gl, 2, i)
        dl_s[r, :] = dl
        inner = inner_s[r, :]
        s = sigmoid(inner)
        gi_s[r, :] = (across(gl, dl, 2) * (s * (1.0 + inner * (1.0 - s)))).astype(BF)
        return carry

    def in_stage(i, carry):
        r = rows_of(i)
        gi = gi_s[r, :]
        il = narrow(gi, 1, i)
        il_s[r, :] = il
        grad = rms_back(grad_in[r, :].astype(F32), middle_s[r, :], gain_mlp[...], across(gi, il, 1))
        grad_out[r, :] = grad
        gm_s[r, :D] = grad.astype(BF)
        return carry

    def out_stage(i, carry):
        r = rows_of(i)
        gm_s[r, D:] = narrow(gm_s[r, :D], 0, i)
        return carry

    wait_all(copies[2])
    loads[0].wait()
    loads[1].wait()
    lax.fori_loop(0, rows // block, down_stage, 0)
    wait_all(copies[1])
    loads[2].wait()
    lax.fori_loop(0, rows // block, in_stage, 0)
    wait_all(copies[0])
    lax.fori_loop(0, rows // block, out_stage, 0)
    sources, group, _ = mixed_grad[0].shape
    for source in range(sources):
        for p in range(parts):
            at = (source * parts + p) * group
            mixed_grad[p][source] = dot(r_s[at : at + group, :WIDE], gm_s[...], NT).astype(BF)


def feed_back(meta, gain_mlp, grad, middle, inner, weights, parts, sources):
    rows = grad.shape[0]
    narrow = shape((rows, AR))
    return call(
        partial(
            feed_back_kernel,
            parts=parts,
            pieces=2,
            block=math.gcd(rows, 320),
        ),
        "feed_back",
        (shape((rows, D), F32), shape((rows, D)), shape((rows, WIDE)), narrow, narrow)
        + (shape((sources, D // sources // parts, rows)),) * parts,
        [SMEM, VMEM] + [HBM] * (3 + 2),
        [
            pltpu.VMEM((rows, D), grad.dtype),
            pltpu.VMEM((rows, D), F32),
            pltpu.VMEM((rows, D), F32),
            pltpu.VMEM((D, SIDE), BF),
            pltpu.SemaphoreType.DMA((3, 2)),
            pltpu.SemaphoreType.DMA((3,)),
        ],
        0.05,
    )(meta, gain_mlp, grad, middle, inner, *weights)


def feed_sums_kernel(*refs, parts):
    gain_mlp, grad, middle_ref, inner_ref, gi, gm, dl, il, low = refs[:9]
    mixed = refs[9 : 9 + parts]
    sums = refs[9 + parts]
    for p in range(parts):
        sources, group, _ = mixed[p].shape
        for source in range(sources):
            at = (source * parts + p) * group
            sums[at : at + group, :AR] = dot(mixed[p][source], gm[:, D:]).astype(BF)
    inner = inner_ref[...]
    act = (inner * sigmoid(inner)).astype(BF)
    middle = middle_ref[...]
    nf = (middle * rms_of(middle) * gain_mlp[...]).astype(BF)
    pairs = (
        (1, low[:, :AR], gm[:, :D]),
        (2, il[...], nf),
        (3, low[:, AR : 2 * AR], gi[...]),
        (4, dl[...], act),
        (5, low[:, 2 * AR :], grad[...].astype(BF)),
    )
    for slot, few, wide in pairs:
        turned = few.T
        for i in range(0, D, BLOCK):
            part = dot(turned, wide[:, i : i + BLOCK])
            sums[i : i + BLOCK, slot * AR : (slot + 1) * AR] = part.T.astype(BF)


def feed_sums(gain_mlp, grad, middle, inner, gi, gm, dl, il, low, mixed):
    return call(
        partial(feed_sums_kernel, parts=len(mixed)),
        "feed_sums",
        (shape((D, 6 * AR)),),
        [VMEM] * (9 + len(mixed)),
        [],
        0.05,
    )(gain_mlp, grad, middle, inner, gi, gm, dl, il, low, *mixed)[0]


def norm_back_kernel(gain, grad, hidden, *refs, cut):
    total = refs[0][...].astype(F32)
    out = refs[-1]
    for ref in refs[1 : -3 if cut else -1]:
        total = total + ref[...].astype(F32)
    if cut:
        first = pl.program_id(0) < cut
        total = total + jnp.where(first, refs[-3][...], refs[-2][...]).astype(F32)
    out[...] = rms_back(grad[...], hidden[...], gain[...], total)


def norm_back(gain, grad, hidden, terms):
    rows = grad.shape[0]
    block = math.gcd(rows, 128)
    cut = terms[-2].shape[0] // block if terms[-1].shape[0] < rows else 0
    row = pl.BlockSpec((block, D), lambda i: (i, 0))
    specs = [row] * (2 + len(terms))
    if cut:
        specs[-2] = pl.BlockSpec((block, D), lambda i: (jnp.minimum(i, cut - 1), 0))
        specs[-1] = pl.BlockSpec((block, D), lambda i: (jnp.maximum(i - cut, 0), 0))
    return pl.pallas_call(
        partial(norm_back_kernel, cut=cut),
        grid=(rows // block,),
        out_shape=shape((rows, D), F32),
        in_specs=[pl.BlockSpec((1, D), lambda i: (0, 0))] + specs,
        out_specs=row,
        cost_estimate=pl.CostEstimate(flops=int(5e7), bytes_accessed=1024, transcendentals=0),
        name="norm_back",
    )(gain, grad, hidden, *terms)


def project_back_kernel(*refs, arrays, pieces, parts, block, mode):
    meta = refs[0]
    grads = refs[1 : 1 + parts]
    weights = refs[1 + parts : 1 + parts + pieces]
    refs = refs[1 + parts + pieces :]
    if mode == "own":
        lora_in, refs = refs[0], refs[1:]
    outs, refs = refs[:arrays], refs[arrays:]
    if mode != "own":
        lora_out, refs = refs[0], refs[1:]
    if mode == "far":
        lora_own, refs = refs[0], refs[1:]
    wq_s, cb_s, bd_s = refs[:3]
    g_s = refs[3 : 3 + parts]
    sems, row_sems = refs[3 + parts :]
    count = g_s[0].shape[0]
    rows_at = pl.ds(pl.multiple_of(meta[7], 256), count)
    loads = start_all(
        [
            pltpu.make_async_copy(
                grads[p] if count == GLEN else grads[p].at[rows_at], g_s[p], row_sems.at[p]
            )
            for p in range(parts)
        ]
    )
    copies = start_all(head_copies(meta, weights, wq_s, cb_s, sems))
    wait_all(copies)
    wait_all(loads)
    columns = wq_s.shape[1]
    each = columns // parts
    fill_second(meta, cb_s, bd_s, columns // 3, each // 3)
    base = meta[7] if mode == "far" else 0

    def rows_of(place):
        at = pl.ds(pl.multiple_of(base + place, 64), block)
        return jnp.concatenate([g_s[p][at, :] for p in range(parts)], axis=1)

    def narrow(g, place):
        mask = row_mask(meta, meta[7] + place, block)
        return (dot(g, bd_s[...]) * jnp.concatenate([mask] * 3, axis=1)).astype(BF)

    for k in range(arrays):
        rows = outs[k].shape[0]
        local = 0 if arrays == 1 else (meta[5] if k == 0 else 1 - meta[5]) * rows

        def step(i, carry, k=k, local=local):
            place = pl.multiple_of(local + i * block, 64)
            g = rows_of(place)
            if mode == "own":
                lora = lora_in[pl.ds(place, block), :]
            else:
                lora = narrow(g, place)
                lora_out[pl.ds(place, block), :] = lora
            outs[k][pl.ds(pl.multiple_of(i * block, 64), block), :] = (
                dot(g, wq_s[...], NT) + dot(lora, cb_s[:, : 3 * AR], NT)
            ).astype(BF)
            return carry

        lax.fori_loop(0, rows // block, step, 0)
    if mode == "far":
        half = GLEN // 2
        own = half - meta[7]

        def own_step(i, carry):
            place = pl.multiple_of(i * block, 64)
            at = pl.multiple_of(own + place, 64)
            g = jnp.concatenate([g_s[p][pl.ds(at, block), :] for p in range(parts)], axis=1)
            mask = row_mask(meta, at, block)
            lora_own[pl.ds(place, block), :] = (
                dot(g, bd_s[...]) * jnp.concatenate([mask] * 3, axis=1)
            ).astype(BF)
            return carry

        lax.fori_loop(0, half // block, own_step, 0)


def project_back(meta, grads, weights, base, arrays, rows, mode, lora=None):
    columns = sum(g.shape[1] for g in grads)
    count = rows * arrays
    low = (shape((count, 3 * AR)),)
    held = count if mode == "own" else GLEN
    return call(
        partial(
            project_back_kernel,
            arrays=arrays,
            pieces=len(weights),
            parts=len(grads),
            block=320,
            mode=mode,
        ),
        "project_back",
        tuple(shape((rows, D)) for _ in range(arrays)) + low * {"own": 0, "far": 2, "all": 1}[mode],
        [SMEM] + [HBM] * (len(grads) + len(weights)) + [VMEM] * (mode == "own"),
        [
            pltpu.VMEM((D, columns), BF),
            pltpu.VMEM((D, 6 * AR), BF),
            pltpu.VMEM((columns, 3 * AR), BF),
        ]
        + [pltpu.VMEM((held, g.shape[1]), BF) for g in grads]
        + [
            pltpu.SemaphoreType.DMA((3 * sum(w.shape[0] for w in weights),)),
            pltpu.SemaphoreType.DMA((len(grads),)),
        ],
        0.05,
    )(meta.at[7].set(base), *grads, *weights, *(() if lora is None else (lora,)))


def project_sums_kernel(*refs, parts, groups, arrays):
    meta = refs[0]
    grads = refs[1 : 1 + parts]
    lows = refs[1 + parts : 1 + parts + groups]
    loras = refs[1 + parts + groups : 1 + parts + 2 * groups]
    tokens = refs[1 + parts + 2 * groups : 1 + parts + 2 * groups + groups * arrays]
    sums, turned = refs[1 + parts + 2 * groups + groups * arrays :]
    sections = []
    for index in range(groups):
        for k in range(arrays):
            ref = tokens[index * arrays + k]
            rows = ref.shape[0]
            at = 0 if arrays == 1 else (meta[5] if k == 0 else 1 - meta[5]) * rows
            slot = index * arrays + k
            turned[slot] = loras[index][pl.ds(at if arrays == 1 else pl.multiple_of(at, 64), rows), :].T
            sections.append((slot, ref))
    for i in range(0, D, BLOCK):
        total = None
        for slot, ref in sections:
            piece = dot(turned[slot], ref[:, i : i + BLOCK])
            total = piece if total is None else total + piece
        sums[i : i + BLOCK, : 3 * AR] = total.T.astype(BF)
    sums[:, 3 * AR :] = jnp.zeros((D, 3 * AR), BF)
    each = grads[0].shape[1]
    group = each // 3
    for c in range(3):
        few = [low[:, c * AR : (c + 1) * AR].T for low in lows]
        for p in range(parts):
            total = None
            for index in range(groups):
                rows = lows[index].shape[0]
                if groups == 1:
                    at = pl.ds(0, rows)
                else:
                    chip = meta[6] if index == 0 else 1 - meta[6]
                    at = pl.ds(pl.multiple_of(chip * rows, 256), rows)
                piece = dot(few[index], grads[p][at, c * group : (c + 1) * group])
                total = piece if total is None else total + piece
            own = pl.multiple_of(meta[4] * group * parts + p * group, math.gcd(group, 256))
            sums[pl.ds(own, group), (3 + c) * AR : (4 + c) * AR] = total.T.astype(BF)


def project_sums(meta, grads, lows, loras, tokens):
    flat = [t for arrays in tokens for t in arrays]
    rows = flat[0].shape[0]
    return call(
        partial(
            project_sums_kernel, parts=len(grads), groups=len(lows), arrays=len(tokens[0])
        ),
        "project_sums",
        (shape((D, 6 * AR)),),
        [SMEM] + [VMEM] * (len(grads) + 2 * len(lows) + len(flat)),
        [pltpu.VMEM((len(flat), 3 * AR, rows), BF)],
        0.05,
    )(meta, *grads, *lows, *loras, *flat)[0]


def swap(value, axis, count, step):
    return lax.ppermute(value, axis, [(i, i ^ step) for i in range(count)])


def fence(*values):
    return lax.optimization_barrier(values)


def after(value, *earlier):
    return lax.optimization_barrier((value, *earlier))[0]


def reduce_quarter(value, core, chip, seq_count, fsdp_count):
    def halves(v, index, step):
        v = v.reshape(fsdp_count, 2, v.shape[1] // 2, v.shape[2])
        keep = jnp.where(index == 0, v[:, 0], v[:, 1])
        give = jnp.where(index == 0, v[:, 1], v[:, 0])
        return (keep.astype(F32) + swap(give, "seq", seq_count, step).astype(F32)).astype(BF)

    value = value.reshape(fsdp_count, value.shape[0] // fsdp_count, value.shape[1])
    return halves(halves(value, core, 1), chip, 2)


def owned(value):
    return lax.all_to_all(value, "fsdp", split_axis=0, concat_axis=0, tiled=True)


def reduce_owner(value, core, chip, seq_count):
    def join(v, index, step):
        far = swap(v, "seq", seq_count, step)
        return jnp.where(index == 0, jnp.concatenate([v, far]), jnp.concatenate([far, v]))

    value = jnp.sum(value.astype(F32), axis=0).astype(BF)
    return join(join(value, chip, 2), core, 1)


def reduce_rows(value):
    return lax.psum_scatter(value, "fsdp", scatter_dimension=0, tiled=True)


def local(
    tokens,
    cont_lengths,
    adapter_ids,
    attn_gain,
    mlp_gain,
    query_scale,
    w_qkv,
    output_weight,
    inward_weight,
    down_weight,
    projection_first_factor,
    b_qkv,
    output_first_factor,
    output_second_factor,
    inward_first_factor,
    inward_second_factor,
    down_first_factor,
    down_second_factor,
    cotangent,
    seq_count,
    fsdp_count,
):
    rows = tokens.shape[1]
    shard = w_qkv.shape[1]
    width = D // seq_count
    paired = seq_count == 4
    place = lax.axis_index("seq")
    core = place % 2
    chip = place // 2 if paired else place * 0
    span = rows if rows % 128 == 0 else GLEN
    meta = jnp.concatenate(
        [
            adapter_ids[0],
            PROMPT + cont_lengths[0, :1],
            jnp.stack([place, core, chip, place * 0]),
        ]
    ).astype(jnp.int32)

    parts = 2 if paired else 1
    group = width // parts

    def heads_part(layer):
        return jnp.concatenate(
            [
                lax.dynamic_slice(
                    w_qkv, (layer, 0, c * D + place * width + p * group), (1, shard, group)
                )[0]
                for p in range(parts)
                for c in range(3)
            ],
            axis=1,
        )

    def both_part(layer):
        turned = jnp.concatenate([b_qkv[layer, c].T for c in range(3)], axis=1)
        return jnp.where(core == 0, projection_first_factor[layer], turned)

    def side_part(layer):
        whole = jnp.concatenate(
            [
                output_weight[layer],
                output_first_factor[layer],
                output_second_factor[layer].T,
                inward_weight[layer],
                inward_first_factor[layer],
                inward_second_factor[layer].T,
                down_weight[layer],
                down_first_factor[layer],
                down_second_factor[layer].T,
            ],
            axis=1,
        )
        half = PART // 2
        return jnp.where(
            core == 0,
            jnp.concatenate([whole[:, k * PART : k * PART + half] for k in range(3)], axis=1),
            jnp.concatenate([whole[:, k * PART + half : (k + 1) * PART] for k in range(3)], axis=1),
        )

    def gathered(value):
        return lax.all_gather(value, "fsdp", axis=0, tiled=True)

    def other_core(own, columns):
        return swap(own[:, :columns], "seq", seq_count, 1)

    def to_rows(mixed):
        if span != rows:
            mixed = mixed[0].reshape(group, seq_count, rows).transpose(1, 0, 2)
        return lax.all_to_all(mixed, "seq", split_axis=0, concat_axis=0, tiled=True)

    def to_heads(value):
        value = lax.all_to_all(value, "seq", split_axis=0, concat_axis=0, tiled=True)
        if span != rows:
            value = value.transpose(1, 0, 2).reshape(1, group, GLEN)
        return value

    both = 3 * AR
    head_weights, side_weights, kept = [], [], []

    def gather_head(layer, *earlier):
        value = jnp.concatenate([both_part(layer), heads_part(layer)], axis=1)
        return gathered(after(value, *earlier) if earlier else value)

    head_gathered = gather_head(0)
    side_gathered = gathered(after(side_part(0), head_gathered))
    hidden = tokens[0].astype(F32)
    normed = (hidden * rms_of(hidden) * attn_gain[0]).astype(BF)
    if paired:
        far = swap(normed, "seq", seq_count, 2)
        head_gathered, far = fence(head_gathered, far)
    for layer in range(LAYERS):
        last = layer == LAYERS - 1
        factor = 1.442695041 / math.sqrt(HD) * jax.nn.softplus(query_scale[layer])
        tiled = jnp.concatenate([jnp.tile(factor * LOG2E, group // HD), jnp.ones((2 * group,), F32)])
        scale = jnp.tile(tiled, parts).reshape(1, 3 * width)
        if layer > 0 and paired:
            far = swap(normed, "seq", seq_count, 2)
            head_gathered, far = fence(head_gathered, far)
        head_weights.append((head_gathered[None], other_core(head_gathered, both)[None]))
        if layer > 0:
            side_gathered = gathered(after(side_part(layer), head_gathered))
        if paired:
            own = ([normed, swap(normed, "seq", seq_count, 1)], chip * 2 * rows)
            projected = [project(meta, scale, own[0], head_weights[layer], own[1], parts)]
            far = after(far, projected[0][-1])
            far = ([far, swap(far, "seq", seq_count, 1)], (1 - chip) * 2 * rows)
            projected.append(project(meta, scale, far[0], head_weights[layer], far[1], parts))
            groups = [own, far]
        else:
            groups = [([lax.all_gather(normed, "seq", axis=0, tiled=True)], place * 0)]
            projected = [project(meta, scale, groups[0][0], head_weights[layer], place * 0, parts)]
        heads = [[p[k] for p in projected] for k in range(parts)]
        attended, mixed = [], []
        for p in range(parts):
            inputs = heads[p] if p == 0 else [after(h, attended[-1][1]) for h in heads[p]]
            attended.append(attend(meta, inputs, span))
            if p < parts - 1:
                mixed.append(to_rows(attended[-1][0]))
        attended, mixed = fence(attended, mixed)
        side_gathered = after(side_gathered, attended[-1][1])
        mixed = mixed + [to_rows(attended[-1][0])]
        side_weights.append((side_gathered, other_core(side_gathered, SIDE // 2)))
        if not last:
            head_gathered = gather_head(layer + 1, attended[-1][1], side_gathered)
        results = feed(
            meta,
            mlp_gain[layer][None],
            attn_gain[(layer + 1) % LAYERS][None],
            mixed,
            hidden,
            side_weights[layer],
            last,
        )
        kept.append(
            (hidden, groups, heads, [p[-1] for p in projected], attended, mixed, factor)
            + tuple(results[:3])
        )
        if last:
            layer_output = results[3]
        else:
            hidden, normed = results[3:]

    grad = cotangent[0]
    sums = [None] * LAYERS
    for layer in reversed(range(LAYERS)):
        hidden, groups, heads, lows, attended, mixed, factor, middle, inner, low = kept[layer]
        gain = mlp_gain[layer][None]
        grad_in = grad
        results = feed_back(
            meta, gain, grad_in, middle, inner, side_weights[layer], parts, seq_count
        )
        results = fence(*results)
        grad, gi, gm, dl, il = results[:5]
        mixed_grads = [to_heads(results[5])]
        side_sum = feed_sums(gain, grad_in, middle, inner, gi, gm, dl, il, low, mixed)
        mixed_grads, side_sum = fence(mixed_grads, side_sum)
        side_total = reduce_rows(side_sum)
        if layer == 0 and paired:
            side_reduced = after(side_total, sums[1][1])
            side_reduced = lax.psum(side_reduced, "seq")
            sums[1] = tuple(lax.psum(v, "seq") for v in sums[1])
        factor_row = jnp.pad(factor, (0, 128 - HD)).reshape(1, 128)
        head_grads = []
        for p in range(parts):
            if p < parts - 1:
                mixed_grads.append(to_heads(after(results[6 + p], side_sum)))
            head_grads.append(
                attend_back(meta, factor_row, heads[p], attended[p][0], mixed_grads[p], attended[p][1])
            )
            head_grads, mixed_grads = fence(head_grads, mixed_grads)
        if paired:
            own, far = groups
            far_back = project_back(
                meta, head_grads, head_weights[layer], far[1], 2, rows, "far"
            )
            far_sum = (
                far_back[0].astype(F32) + swap(far_back[1], "seq", seq_count, 1).astype(F32)
            ).astype(BF)
            if layer > 0:
                far_sum, head_grads, side_total = fence(far_sum, head_grads, side_total)
            else:
                far_sum, head_grads = fence(far_sum, head_grads)
            loras = [far_back[3], far_back[2]]
            cut = rows * 3 // 5
            crossed = swap(far_sum[:cut], "seq", seq_count, 2)
            head_sum = project_sums(meta, head_grads, lows, loras, [g[0] for g in groups])
            if layer == 0:
                side_total = side_reduced
            head_sum, crossed, head_grads, rest, sums[1], side_total = fence(
                head_sum, crossed, head_grads, far_sum[cut:], sums[1], side_total
            )
            if layer > 0:
                head_total = reduce_rows(head_sum)
                rest = swap(rest, "seq", seq_count, 2)
            else:
                head_total = reduce_quarter(head_sum, core, chip, seq_count, fsdp_count)
            own_back = project_back(
                meta, head_grads, head_weights[layer], own[1], 2, rows, "own", loras[0]
            )
            if layer > 0:
                own_back, rest = fence(own_back, rest)
            else:
                own_back, head_total, rest = fence(own_back, head_total, rest)
                rest = swap(rest, "seq", seq_count, 2)
                head_total = owned(head_total)
                head_total, rest = fence(head_total, rest)
                head_total = reduce_owner(head_total, core, chip, seq_count)
            near = swap(own_back[1], "seq", seq_count, 1)
            sums[layer] = (side_total, head_total)
            terms = [own_back[0], near, crossed, rest]
        else:
            back = project_back(
                meta, head_grads, head_weights[layer], place * 0, 1, GLEN, "all"
            )
            terms = [lax.psum_scatter(back[0], "seq", scatter_dimension=0, tiled=True)]
            head_sum = project_sums(meta, head_grads, lows, [back[1]], [g[0] for g in groups])
            sums[layer] = tuple(lax.psum(v, "seq") for v in (side_total, reduce_rows(head_sum)))
        grad = norm_back(attn_gain[layer][None], grad, hidden, terms)

    side = jnp.stack([s[0] for s in sums]).astype(F32)
    head = jnp.stack([s[1] for s in sums]).astype(F32)

    def columns(slot):
        return side[:, :, slot * AR : (slot + 1) * AR]

    return (
        layer_output[None],
        grad[None],
        head[:, :, : 3 * AR],
        head[:, :, 3 * AR :].reshape(LAYERS, shard, 3, AR).transpose(0, 2, 3, 1),
        columns(0),
        columns(1).transpose(0, 2, 1),
        columns(2),
        columns(3).transpose(0, 2, 1),
        columns(4),
        columns(5).transpose(0, 2, 1),
    )


def solution(mesh):
    rows = P("fsdp", "seq", None)
    first = P(None, "fsdp", None)
    second = P(None, None, "fsdp")
    return jax.shard_map(
        partial(local, seq_count=mesh.shape["seq"], fsdp_count=mesh.shape["fsdp"]),
        mesh=mesh,
        in_specs=(
            rows,
            P("fsdp", None),
            P("fsdp", None),
            P(),
            P(),
            P(),
            first,
            first,
            first,
            first,
            first,
            P(None, None, None, "fsdp"),
            first,
            second,
            first,
            second,
            first,
            second,
            rows,
        ),
        out_specs=(
            rows,
            rows,
            first,
            P(None, None, None, "fsdp"),
            first,
            second,
            first,
            second,
            first,
            second,
        ),
        check_vma=False,
    )
```

```python
from functools import partial
import math

import jax
import jax.numpy as jnp
from jax import lax
from jax.experimental import pallas as pl
from jax.experimental.pallas import tpu as pltpu
from jax.sharding import PartitionSpec as P

D = 1280
HEADS = 16
HD = 80
R = 16
LAYERS = 2
PROMPT = 2048
AR = 128
GLEN = 2560
LOG2E = 1.4426950408889634
LN2 = 0.6931471805599453
ROFF = 8
NEG = -1e30
BLOCK = 256
CHUNK = 512
WIDE = D + AR
PART = D + 2 * AR
SIDE = 3 * PART
BF = jnp.bfloat16
F32 = jnp.float32
NN = (((1,), (0,)), ((), ()))
NT = (((1,), (1,)), ((), ()))
VMEM = pl.BlockSpec(memory_space=pltpu.VMEM)
SMEM = pl.BlockSpec(memory_space=pltpu.SMEM)
HBM = pl.BlockSpec(memory_space=pl.ANY)


def dot(left, right, dims=NN):
    return lax.dot_general(left, right, dims, preferred_element_type=F32)


def call(kernel, name, outs, specs, scratch, expected, out_specs=None):
    return pl.pallas_call(
        kernel,
        out_shape=outs,
        in_specs=specs,
        out_specs=tuple(VMEM for _ in outs) if out_specs is None else out_specs,
        scratch_shapes=scratch,
        compiler_params=pltpu.CompilerParams(vmem_limit_bytes=60 << 20),
        cost_estimate=pl.CostEstimate(
            flops=int(expected * 1.15e9), bytes_accessed=1024, transcendentals=0
        ),
        name=name,
    )


def shape(dims, kind=BF):
    return jax.ShapeDtypeStruct(dims, kind)


def sigmoid(v):
    return 1.0 / (1.0 + jnp.exp(-v))


def row_mask(meta, base, count):
    rows = lax.broadcasted_iota(jnp.int32, (count, AR), 0) + base
    lane = lax.broadcasted_iota(jnp.int32, (count, AR), 1)
    chosen = jnp.where(rows < PROMPT, meta[0], jnp.where(rows < meta[3], meta[1], meta[2]))
    low = chosen * R
    return jnp.where((lane >= low) & (lane < low + R), 1.0, 0.0).astype(F32)


def columns_of(ref, at, width):
    return ref if width == ref.shape[1] else ref.at[:, pl.ds(at, width)]


def head_copies(meta, pieces, wq_s, cb_s, sems):
    core, both = meta[5], 3 * AR
    n = len(pieces) // 2
    single = n == 1 and pieces[0].shape[0] == 1
    copies, block_at = [], 0
    for own, other in zip(pieces[:n], pieces[n:]):
        blocks, rows, columns = own.shape
        for block in range(blocks):
            at = 0 if single else pl.multiple_of(meta[ROFF + block_at], math.gcd(rows, 256))
            into = pl.ds(at, rows)
            for source, target in (
                (own.at[block, :, :both], cb_s.at[into, pl.ds(pl.multiple_of(core * both, both), both)]),
                (other.at[block], cb_s.at[into, pl.ds(pl.multiple_of((1 - core) * both, both), both)]),
                (own.at[block, :, both:], None if wq_s is None else wq_s.at[into]),
            ):
                if target is not None:
                    copies.append(pltpu.make_async_copy(source, target, sems.at[len(copies)]))
            block_at += 1
    return copies


def side_copies(meta, own, other, which, r_s, sems):
    half = PART // 2
    return [
        pltpu.make_async_copy(
            columns_of(ref, which * half, half),
            columns_of(r_s, pl.multiple_of(which * PART + side * half, half), half),
            sems.at[which, k],
        )
        for k, (ref, side) in enumerate(((own, meta[5]), (other, 1 - meta[5])))
    ]


def start_all(copies):
    for copy in copies:
        copy.start()
    return copies


def wait_all(copies):
    for copy in copies:
        copy.wait()


def run_copies(copies):
    wait_all(start_all(copies))


def fill_second(meta, cb_s, bd_s, width, group):
    bd_s[...] = jnp.zeros_like(bd_s)
    for p in range(width // group):
        start = pl.multiple_of(meta[4] * width + p * group, math.gcd(group, 256))
        for c in range(3):
            at = (p * 3 + c) * group
            bd_s[at : at + group, c * AR : (c + 1) * AR] = cb_s[
                pl.ds(start, group), (3 + c) * AR : (4 + c) * AR
            ]


def project_kernel(*refs, arrays, pieces, parts, block):
    meta, scale = refs[:2]
    tokens = refs[2 : 2 + arrays]
    weights = refs[2 + arrays : 2 + arrays + pieces]
    heads = refs[2 + arrays + pieces : 2 + arrays + pieces + parts]
    low_out, wq_s, cb_s, bd_s, sems = refs[2 + arrays + pieces + parts :]
    run_copies(head_copies(meta, weights, wq_s, cb_s, sems))
    columns = wq_s.shape[1]
    each = columns // parts
    fill_second(meta, cb_s, bd_s, columns // 3, each // 3)
    for k in range(arrays):
        rows = tokens[k].shape[0]
        local = 0 if arrays == 1 else (meta[5] if k == 0 else 1 - meta[5]) * rows

        def step(i, carry, k=k, local=local):
            x = tokens[k][pl.ds(pl.multiple_of(i * block, 64), block), :]
            place = pl.multiple_of(local + i * block, 64)
            mask = row_mask(meta, meta[7] + place, block)
            low = dot(x, cb_s[:, : 3 * AR]) * jnp.concatenate([mask] * 3, axis=1)
            low = low.astype(BF)
            low_out[pl.ds(place, block), :] = low
            both = ((dot(x, wq_s[...]) + dot(low, bd_s[...], NT)) * scale[...]).astype(BF)
            for p in range(parts):
                heads[p][pl.ds(place, block), :] = both[:, p * each : (p + 1) * each]
            return carry

        lax.fori_loop(0, rows // block, step, 0)


def project(meta, scale, tokens, weights, base, parts):
    arrays = len(tokens)
    rows = tokens[0].shape[0]
    count = rows * arrays
    columns = scale.shape[1]
    return call(
        partial(
            project_kernel, arrays=arrays, pieces=len(weights), parts=parts, block=320
        ),
        "project",
        (shape((count, columns // parts)),) * parts + (shape((count, 3 * AR)),),
        [SMEM, VMEM] + [VMEM] * arrays + [HBM] * len(weights),
        [
            pltpu.VMEM((D, columns), BF),
            pltpu.VMEM((D, 6 * AR), BF),
            pltpu.VMEM((columns, 3 * AR), BF),
            pltpu.SemaphoreType.DMA((3 * sum(w.shape[0] for w in weights),)),
        ],
        13,
    )(meta.at[7].set(base), scale, *tokens, *weights)


def load_rows(meta, sources, target, sems):
    copies = []
    for index, ref in enumerate(sources):
        rows = ref.shape[0]
        if len(sources) == 1:
            into = target
        else:
            into = target.at[pl.ds(pl.multiple_of(meta[6] * rows if index == 0 else (1 - meta[6]) * rows, 256), rows)]
        copies.append(pltpu.make_async_copy(ref, into, sems.at[index]))
    run_copies(copies)


def allowed_pairs(meta, queries, keys, query_at, key_at):
    same = (keys >= meta[3]) | (queries < meta[3])
    causal = keys <= queries
    return causal & same if key_at >= PROMPT else causal


def three_parts(x):
    high = x.astype(BF).astype(F32)
    rest = x - high
    middle = rest.astype(BF).astype(F32)
    return high, middle, (rest - middle).astype(BF).astype(F32)


def with_parts(base, place, value):
    a, b, c = three_parts(value)
    return jnp.where(place == 0, a, jnp.where(place == 1, b, jnp.where(place == 2, c, base)))


def attend_kernel(*refs, groups, local_heads):
    meta = refs[0]
    sources = refs[1 : 1 + groups]
    out, saved, hs, q_s, k_s, v_s, sems, out_sems = refs[1 + groups :]
    load_rows(meta, sources, hs, sems)
    width = local_heads * HD
    span = out.shape[2]
    lane = lax.broadcasted_iota(jnp.int32, (BLOCK, 128), 1)
    for h in range(local_heads):
        for i in range(GLEN // BLOCK):
            r = slice(i * BLOCK, (i + 1) * BLOCK)
            for c, ref in ((0, q_s), (1, k_s), (2, v_s)):
                x = hs[r, c * width + h * HD : c * width + (h + 1) * HD]
                fill = jnp.ones if c > 0 else jnp.zeros
                ref[h, r, :] = jnp.concatenate([x, fill((BLOCK, 128 - HD), BF)], axis=1)
    stores = [
        pltpu.make_async_copy(ref, saved.at[c], out_sems.at[c])
        for c, ref in ((0, q_s), (1, k_s), (2, v_s))
    ]
    stores[1].start()
    stores[2].start()

    def head(h, carry):
        place = pl.multiple_of(h * HD, 16)
        for i in range(GLEN // BLOCK):
            q0 = i * BLOCK
            nk = q0 + BLOCK
            d0 = min(q0, PROMPT)
            rows = lax.broadcasted_iota(jnp.int32, (BLOCK, nk - d0), 0) + q0
            cols = lax.broadcasted_iota(jnp.int32, (BLOCK, nk - d0), 1) + d0
            qb = q_s[h, q0 : q0 + BLOCK, :]
            sd = jnp.where(
                allowed_pairs(meta, rows, cols, q0, d0), dot(qb, k_s[h, d0:nk, :], NT), NEG
            )
            peak = jnp.max(sd, axis=1, keepdims=True)
            if d0 > 0:
                sp = dot(qb, k_s[h, 0:d0, :], NT)
                peak = jnp.maximum(peak, jnp.max(sp, axis=1, keepdims=True))
            total = dot(jnp.exp2(sd - peak).astype(BF), v_s[h, d0:nk, :])
            if d0 > 0:
                total = total + dot(jnp.exp2(sp - peak).astype(BF), v_s[h, 0:d0, :])
            lse = peak + jnp.log2(total[:, HD : HD + 1])
            q_s[h, q0 : q0 + BLOCK, :] = with_parts(qb.astype(F32), lane - HD, -lse).astype(BF)
            turned = total.T
            result = (turned[:HD, :] * (1.0 / turned[HD : HD + 1, :])).astype(BF)
            for part in range(BLOCK // 128):
                t = q0 + part * 128
                out[t // span, pl.ds(place, HD), t % span : t % span + 128] = result[
                    :, part * 128 : (part + 1) * 128
                ]
        return carry

    lax.fori_loop(0, local_heads, head, 0)
    stores[0].start()
    wait_all(stores)


def attend(meta, heads, span):
    width = heads[0].shape[1]
    local_heads = width // (3 * HD)
    return call(
        partial(attend_kernel, groups=len(heads), local_heads=local_heads),
        "attend",
        (shape((GLEN // span, local_heads * HD, span)), shape((3, local_heads, GLEN, 128))),
        [SMEM] + [HBM] * len(heads),
        [pltpu.VMEM((GLEN, width), BF)]
        + [pltpu.VMEM((local_heads, GLEN, 128), BF)] * 3
        + [pltpu.SemaphoreType.DMA((len(heads),)), pltpu.SemaphoreType.DMA((3,))],
        16,
        out_specs=(VMEM, HBM),
    )(meta, *heads)


def attend_back_kernel(meta, factor, saved, o_ref, do_ref, out, q_s, k_s, v_s, dt_s, kt_s, dqt_s, sems):
    local_heads = saved.shape[1]
    width = local_heads * HD
    span = o_ref.shape[2]
    loads = [
        start_all(
            [
                pltpu.make_async_copy(saved.at[c, h], ref.at[h], sems.at[c, h])
                for c, ref in ((0, q_s), (1, k_s), (2, v_s))
            ]
        )
        for h in range(local_heads)
    ]
    extra = lax.broadcasted_iota(jnp.int32, (128 - HD, 128), 0)
    for h in range(local_heads):
        cs = slice(h * HD, (h + 1) * HD)
        for i in range(GLEN // 128):
            t, inner = (i * 128) // span, slice((i * 128) % span, (i * 128) % span + 128)
            do = do_ref[t, cs, inner]
            delta = jnp.sum(do.astype(F32) * o_ref[t, cs, inner].astype(F32), axis=0, keepdims=True)
            dt_s[h, :HD, i * 128 : (i + 1) * 128] = do
            dt_s[h, HD:, i * 128 : (i + 1) * 128] = with_parts(0.0, extra, -delta).astype(BF)
    for h in range(local_heads):
        wait_all(loads[h])
        for i in range(GLEN // BLOCK):
            kt_s[:, i * BLOCK : (i + 1) * BLOCK] = k_s[h, i * BLOCK : (i + 1) * BLOCK, :].T
        for j in range(GLEN // BLOCK):
            k0 = j * BLOCK
            kb = k_s[h, k0 : k0 + BLOCK, :]
            vb = v_s[h, k0 : k0 + BLOCK, :]
            dk = jnp.zeros((BLOCK, 128), F32)
            dv = jnp.zeros((BLOCK, 128), F32)
            q0 = k0
            while q0 < GLEN:
                n = BLOCK if q0 == k0 else min(CHUNK, GLEN - q0)
                qs = slice(q0, q0 + n)
                probs = jnp.exp2(dot(kb, q_s[h, qs, :], NT))
                if q0 == k0 or k0 >= PROMPT:
                    keys = lax.broadcasted_iota(jnp.int32, (BLOCK, n), 0) + k0
                    queries = lax.broadcasted_iota(jnp.int32, (BLOCK, n), 1) + q0
                    probs = jnp.where(allowed_pairs(meta, queries, keys, q0, k0), probs, 0.0)
                dscore = (probs * dot(vb, dt_s[h, :, qs])).astype(BF)
                dv = dv + dot(probs.astype(BF), dt_s[h, :, qs], NT)
                dk = dk + dot(dscore, q_s[h, qs, :])
                dq = dot(kt_s[:, k0 : k0 + BLOCK], dscore)
                if j == 0:
                    dqt_s[:, qs] = dq
                else:
                    dqt_s[:, qs] += dq
                q0 += n
            r = slice(k0, k0 + BLOCK)
            out[r, width + h * HD : width + (h + 1) * HD] = (dk[:, :HD] * LN2).astype(BF)
            out[r, 2 * width + h * HD : 2 * width + (h + 1) * HD] = dv[:, :HD].astype(BF)
            out[r, h * HD : (h + 1) * HD] = (dqt_s[:, r].T * factor[...]).astype(BF)[:, :HD]


def attend_back(meta, factor, saved, mixed, grad_mixed):
    local_heads = saved.shape[1]
    rows = pltpu.VMEM((local_heads, GLEN, 128), BF)
    return call(
        attend_back_kernel,
        "attend_back",
        (shape((GLEN, 3 * local_heads * HD)),),
        [SMEM, VMEM, HBM] + [VMEM] * 2,
        [rows] * 3
        + [
            pltpu.VMEM((local_heads, 128, GLEN), BF),
            pltpu.VMEM((128, GLEN), BF),
            pltpu.VMEM((128, GLEN), F32),
            pltpu.SemaphoreType.DMA((3, local_heads)),
        ],
        0.05,
    )(meta, factor, saved, mixed, grad_mixed)[0]


def rms_of(value):
    return lax.rsqrt(jnp.mean(value * value, axis=-1, keepdims=True) + 1e-06)


def feed_kernel(*refs, parts, pieces, block, last):
    meta, gain_mlp, gain_next, hidden_in = refs[:4]
    mixed = refs[4 : 4 + parts]
    weights = refs[4 + parts : 4 + parts + pieces]
    refs = refs[4 + parts + pieces :]
    middle_out, inner_out, low_out, result = refs[:4]
    normed_out = None if last else refs[4]
    hidden, middle_s, inner_s, r_s, mt_s, mx_s, sems, io_sems = refs[4 if last else 5 :]
    rows = hidden.shape[0]
    loads, slot = [], 0
    for p in range(parts):
        sources, group, _ = mixed[p].shape
        for source in range(sources):
            at = (source * parts + p) * group
            loads.append(
                pltpu.make_async_copy(
                    mixed[p].at[source], mt_s.at[at : at + group], io_sems.at[len(loads)]
                )
            )
    start_all(loads)
    load_hidden = pltpu.make_async_copy(hidden_in, hidden, io_sems.at[len(loads)])
    load_hidden.start()
    copies = [start_all(side_copies(meta, *weights, which, r_s, sems)) for which in range(3)]
    wait_all(loads)
    for i in range(0, rows, 128):
        n = min(128, rows - i)
        mx_s[i : i + n, :] = mt_s[:, i : i + n].T
    load_hidden.wait()

    def stage(which, body):
        wait_all(copies[which])

        def step(i, carry):
            r = pl.ds(pl.multiple_of(i * block, 64), block)
            mask = row_mask(meta, meta[4] * rows + i * block, block)

            def adapted(x):
                both = dot(x, r_s[:, which * PART : which * PART + WIDE])
                low = (both[:, D:] * mask).astype(BF)
                low_out[r, which * AR : (which + 1) * AR] = low
                return both[:, :D] + dot(low, r_s[:, which * PART + WIDE : (which + 1) * PART], NT)

            body(r, adapted)
            return carry

        lax.fori_loop(0, rows // block, step, 0)

    def out_stage(r, adapted):
        middle_s[r, :] = hidden[r, :] + adapted(mx_s[r, :])

    def in_stage(r, adapted):
        middle = middle_s[r, :]
        inner_s[r, :] = adapted((middle * rms_of(middle) * gain_mlp[...]).astype(BF))

    def down_stage(r, adapted):
        inner = inner_s[r, :]
        value = middle_s[r, :] + adapted((inner * sigmoid(inner)).astype(BF))
        result[r, :] = value.astype(result.dtype)
        if not last:
            normed_out[r, :] = (value * rms_of(value) * gain_next[...]).astype(BF)

    stage(0, out_stage)
    store_middle = pltpu.make_async_copy(middle_s, middle_out, io_sems.at[len(loads) + 1])
    store_middle.start()
    stage(1, in_stage)
    store_inner = pltpu.make_async_copy(inner_s, inner_out, io_sems.at[len(loads) + 2])
    store_inner.start()
    stage(2, down_stage)
    store_middle.wait()
    store_inner.wait()


def feed(meta, gain_mlp, gain_next, mixed, hidden, weights, last):
    rows = hidden.shape[0]
    row = pltpu.VMEM((rows, D), F32)
    outs = (shape((rows, D), F32), shape((rows, D), F32), shape((rows, 3 * AR)))
    outs += (shape((rows, D), BF),) if last else (shape((rows, D), F32), shape((rows, D), BF))
    return call(
        partial(
            feed_kernel,
            parts=len(mixed),
            pieces=2,
            block=math.gcd(rows, 320),
            last=last,
        ),
        "feed",
        outs,
        [SMEM] + [VMEM] * 2 + [HBM] * (1 + len(mixed) + 2),
        [
            row,
            row,
            row,
            pltpu.VMEM((D, SIDE), BF),
            pltpu.VMEM((D, rows), BF),
            pltpu.VMEM((rows, D), BF),
            pltpu.SemaphoreType.DMA((3, 2)),
            pltpu.SemaphoreType.DMA((sum(m.shape[0] for m in mixed) + 3,)),
        ],
        17,
        out_specs=(HBM, HBM) + (VMEM,) * (len(outs) - 2),
    )(meta, gain_mlp, gain_next, hidden, *mixed, *weights)


def rms_back(grad, value, gain, grad_normed):
    r = rms_of(value)
    e = gain * grad_normed
    return grad + r * e - value * (r * r * r) * jnp.mean(value * e, axis=-1, keepdims=True)


def feed_back_kernel(*refs, parts, pieces, block, terms):
    meta, gain_mlp, grad_hbm, middle_hbm, inner_hbm = refs[:5]
    weights = refs[5 : 5 + pieces]
    refs = refs[5 + pieces :]
    if terms:
        gain_next, hidden_hbm, term_hbm = refs[0], refs[1], refs[2 : 2 + terms]
        refs = refs[2 + terms :]
    grad_out, gi_s, gm_s, dl_s, il_s = refs[:5]
    mixed_grad = refs[5 : 5 + parts]
    refs = refs[5 + parts :]
    if terms:
        gl_out, refs = refs[0], refs[1:]
    grad_in, middle_s, inner_s, r_s, sems, io_sems = refs[:6]
    rows = grad_in.shape[0]
    early = []
    if terms:
        hidden_s, term_s, term_sems = refs[6], refs[7 : 7 + terms - 1], refs[7 + terms - 1]
        early.append(pltpu.make_async_copy(hidden_hbm, hidden_s, term_sems.at[terms]))
        for k in range(terms - 2):
            early.append(pltpu.make_async_copy(term_hbm[k], term_s[k], term_sems.at[k]))
        cut = term_hbm[-2].shape[0]
        early.append(
            pltpu.make_async_copy(term_hbm[-2], term_s[-1].at[:cut], term_sems.at[terms - 2])
        )
        early.append(
            pltpu.make_async_copy(term_hbm[-1], term_s[-1].at[cut:], term_sems.at[terms - 1])
        )
        start_all(early)
    loads = start_all(
        [
            pltpu.make_async_copy(source, target, io_sems.at[k])
            for k, (source, target) in enumerate(
                ((grad_hbm, grad_in), (inner_hbm, inner_s), (middle_hbm, middle_s))
            )
        ]
    )
    copies = {which: start_all(side_copies(meta, *weights, which, r_s, sems)) for which in (2, 1, 0)}

    def rows_of(i):
        return pl.ds(pl.multiple_of(i * block, 64), block)

    def narrow(g, which, i):
        mask = row_mask(meta, meta[4] * rows + i * block, block)
        return (dot(g, r_s[:, which * PART + WIDE : (which + 1) * PART]) * mask).astype(BF)

    def across(g, low, which):
        both = jnp.concatenate([g, low], axis=1)
        return dot(both, r_s[:, which * PART : which * PART + WIDE], NT)

    def down_stage(i, carry):
        r = rows_of(i)
        gl = grad_in[r, :].astype(BF)
        dl = narrow(gl, 2, i)
        dl_s[r, :] = dl
        inner = inner_s[r, :]
        s = sigmoid(inner)
        gi_s[r, :] = (across(gl, dl, 2) * (s * (1.0 + inner * (1.0 - s)))).astype(BF)
        return carry

    def in_stage(i, carry):
        r = rows_of(i)
        gi = gi_s[r, :]
        il = narrow(gi, 1, i)
        il_s[r, :] = il
        grad = rms_back(grad_in[r, :].astype(F32), middle_s[r, :], gain_mlp[...], across(gi, il, 1))
        grad_out[r, :] = grad
        gm_s[r, :D] = grad.astype(BF)
        return carry

    def out_stage(i, carry):
        r = rows_of(i)
        gm_s[r, D:] = narrow(gm_s[r, :D], 0, i)
        return carry

    loads[0].wait()
    if terms:
        wait_all(early)

        def norm_stage(i, carry):
            r = rows_of(i)
            total = term_s[0][r, :].astype(F32)
            for ref in term_s[1:]:
                total = total + ref[r, :].astype(F32)
            grad = rms_back(grad_in[r, :], hidden_s[r, :], gain_next[...], total)
            grad_in[r, :] = grad
            gl_out[r, :] = grad.astype(BF)
            return carry

        lax.fori_loop(0, rows // block, norm_stage, 0)
    wait_all(copies[2])
    loads[1].wait()
    lax.fori_loop(0, rows // block, down_stage, 0)
    wait_all(copies[1])
    loads[2].wait()
    lax.fori_loop(0, rows // block, in_stage, 0)
    wait_all(copies[0])
    lax.fori_loop(0, rows // block, out_stage, 0)
    sources, group, _ = mixed_grad[0].shape
    for source in range(sources):
        for p in range(parts):
            at = (source * parts + p) * group
            mixed_grad[p][source] = dot(r_s[at : at + group, :WIDE], gm_s[...], NT).astype(BF)


def feed_back(meta, gain_mlp, grad, middle, inner, weights, parts, sources, norm=None):
    rows = grad.shape[0]
    narrow = shape((rows, AR))
    return call(
        partial(
            feed_back_kernel,
            parts=parts,
            pieces=2,
            block=math.gcd(rows, 320),
            terms=0 if norm is None else len(norm[2]),
        ),
        "feed_back",
        (shape((rows, D), F32), shape((rows, D)), shape((rows, WIDE)), narrow, narrow)
        + (shape((sources, D // sources // parts, rows)),) * parts
        + (() if norm is None else (shape((rows, D)),)),
        [SMEM, VMEM]
        + [HBM] * (3 + 2)
        + ([] if norm is None else [VMEM] + [HBM] * (1 + len(norm[2]))),
        [
            pltpu.VMEM((rows, D), grad.dtype),
            pltpu.VMEM((rows, D), F32),
            pltpu.VMEM((rows, D), F32),
            pltpu.VMEM((D, SIDE), BF),
            pltpu.SemaphoreType.DMA((3, 2)),
            pltpu.SemaphoreType.DMA((3,)),
        ]
        + (
            []
            if norm is None
            else [pltpu.VMEM((rows, D), F32)]
            + [pltpu.VMEM((rows, D), BF)] * (len(norm[2]) - 1)
            + [pltpu.SemaphoreType.DMA((len(norm[2]) + 1,))]
        ),
        0.05,
    )(
        meta,
        gain_mlp,
        grad,
        middle,
        inner,
        *weights,
        *(() if norm is None else (norm[0], norm[1], *norm[2])),
    )


def feed_sums_kernel(*refs, parts):
    gain_mlp, grad, middle_ref, inner_ref, gi, gm, dl, il, low = refs[:9]
    mixed = refs[9 : 9 + parts]
    sums = refs[9 + parts]
    for p in range(parts):
        sources, group, _ = mixed[p].shape
        for source in range(sources):
            at = (source * parts + p) * group
            sums[at : at + group, :AR] = dot(mixed[p][source], gm[:, D:]).astype(BF)
    inner = inner_ref[...]
    act = (inner * sigmoid(inner)).astype(BF)
    middle = middle_ref[...]
    nf = (middle * rms_of(middle) * gain_mlp[...]).astype(BF)
    pairs = (
        (1, low[:, :AR], gm[:, :D]),
        (2, il[...], nf),
        (3, low[:, AR : 2 * AR], gi[...]),
        (4, dl[...], act),
        (5, low[:, 2 * AR :], grad[...].astype(BF)),
    )
    for slot, few, wide in pairs:
        turned = few.T
        for i in range(0, D, BLOCK):
            part = dot(turned, wide[:, i : i + BLOCK])
            sums[i : i + BLOCK, slot * AR : (slot + 1) * AR] = part.T.astype(BF)


def feed_sums(gain_mlp, grad, middle, inner, gi, gm, dl, il, low, mixed):
    return call(
        partial(feed_sums_kernel, parts=len(mixed)),
        "feed_sums",
        (shape((D, 6 * AR)),),
        [VMEM] * (9 + len(mixed)),
        [],
        0.05,
    )(gain_mlp, grad, middle, inner, gi, gm, dl, il, low, *mixed)[0]


def norm_back_kernel(gain, grad, hidden, *refs, cut):
    total = refs[0][...].astype(F32)
    out = refs[-1]
    for ref in refs[1 : -3 if cut else -1]:
        total = total + ref[...].astype(F32)
    if cut:
        first = pl.program_id(0) < cut
        total = total + jnp.where(first, refs[-3][...], refs[-2][...]).astype(F32)
    out[...] = rms_back(grad[...], hidden[...], gain[...], total)


def norm_back(gain, grad, hidden, terms):
    rows = grad.shape[0]
    block = math.gcd(rows, 128)
    cut = terms[-2].shape[0] // block if terms[-1].shape[0] < rows else 0
    row = pl.BlockSpec((block, D), lambda i: (i, 0))
    specs = [row] * (2 + len(terms))
    if cut:
        specs[-2] = pl.BlockSpec((block, D), lambda i: (jnp.minimum(i, cut - 1), 0))
        specs[-1] = pl.BlockSpec((block, D), lambda i: (jnp.maximum(i - cut, 0), 0))
    return pl.pallas_call(
        partial(norm_back_kernel, cut=cut),
        grid=(rows // block,),
        out_shape=shape((rows, D), F32),
        in_specs=[pl.BlockSpec((1, D), lambda i: (0, 0))] + specs,
        out_specs=row,
        cost_estimate=pl.CostEstimate(flops=int(5e7), bytes_accessed=1024, transcendentals=0),
        name="norm_back",
    )(gain, grad, hidden, *terms)


def project_back_kernel(*refs, arrays, pieces, parts, block, mode):
    meta = refs[0]
    grads = refs[1 : 1 + parts]
    weights = refs[1 + parts : 1 + parts + pieces]
    refs = refs[1 + parts + pieces :]
    if mode == "own":
        lora_in, refs = refs[0], refs[1:]
    outs, refs = refs[:arrays], refs[arrays:]
    if mode != "own":
        lora_out, refs = refs[0], refs[1:]
    wq_s, cb_s, bd_s = refs[:3]
    g_s = refs[3 : 3 + parts]
    sems, row_sems = refs[3 + parts :]
    count = g_s[0].shape[0]
    rows_at = pl.ds(pl.multiple_of(meta[7], 256), count)
    loads = start_all(
        [
            pltpu.make_async_copy(
                grads[p] if count == GLEN else grads[p].at[rows_at], g_s[p], row_sems.at[p]
            )
            for p in range(parts)
        ]
    )
    copies = start_all(head_copies(meta, weights, wq_s, cb_s, sems))
    wait_all(copies)
    wait_all(loads)
    columns = wq_s.shape[1]
    each = columns // parts
    fill_second(meta, cb_s, bd_s, columns // 3, each // 3)

    def rows_of(place):
        at = pl.ds(pl.multiple_of(place, 64), block)
        return jnp.concatenate([g_s[p][at, :] for p in range(parts)], axis=1)

    def narrow(g, place):
        mask = row_mask(meta, meta[7] + place, block)
        return (dot(g, bd_s[...]) * jnp.concatenate([mask] * 3, axis=1)).astype(BF)

    for k in range(arrays):
        rows = outs[k].shape[0]
        local = 0 if arrays == 1 else (meta[5] if k == 0 else 1 - meta[5]) * rows

        def step(i, carry, k=k, local=local):
            place = pl.multiple_of(local + i * block, 64)
            g = rows_of(place)
            if mode == "own":
                lora = lora_in[pl.ds(place, block), :]
            else:
                lora = narrow(g, place)
                lora_out[pl.ds(place, block), :] = lora
            outs[k][pl.ds(pl.multiple_of(i * block, 64), block), :] = (
                dot(g, wq_s[...], NT) + dot(lora, cb_s[:, : 3 * AR], NT)
            ).astype(BF)
            return carry

        lax.fori_loop(0, rows // block, step, 0)


def project_back(meta, grads, weights, base, arrays, rows, mode, lora=None):
    columns = sum(g.shape[1] for g in grads)
    count = rows * arrays
    low = (shape((count, 3 * AR)),)
    return call(
        partial(
            project_back_kernel,
            arrays=arrays,
            pieces=len(weights),
            parts=len(grads),
            block=320,
            mode=mode,
        ),
        "project_back",
        tuple(shape((rows, D)) for _ in range(arrays)) + low * (mode != "own"),
        [SMEM] + [HBM] * (len(grads) + len(weights)) + [VMEM] * (mode == "own"),
        [
            pltpu.VMEM((D, columns), BF),
            pltpu.VMEM((D, 6 * AR), BF),
            pltpu.VMEM((columns, 3 * AR), BF),
        ]
        + [pltpu.VMEM((count, g.shape[1]), BF) for g in grads]
        + [
            pltpu.SemaphoreType.DMA((3 * sum(w.shape[0] for w in weights),)),
            pltpu.SemaphoreType.DMA((len(grads),)),
        ],
        0.05,
    )(meta.at[7].set(base), *grads, *weights, *(() if lora is None else (lora,)))


def project_sums_kernel(*refs, parts, groups, arrays, block):
    meta = refs[0]
    grads, refs = refs[1 : 1 + parts], refs[1 + parts :]
    lows, refs = refs[:groups], refs[groups:]
    lora_far, refs = refs[0], refs[1:]
    tokens, refs = refs[: groups * arrays], refs[groups * arrays :]
    if groups == 1:
        loras = [lora_far]
        sums, turned = refs
    else:
        weights, refs = refs[:2], refs[2:]
        sums, lora_own, turned, cb_s, bd_s, sems = refs
        loras = [lora_own, lora_far]
        run_copies(head_copies(meta, weights, None, cb_s, sems))
        each = grads[0].shape[1]
        fill_second(meta, cb_s, bd_s, each * parts // 3, each // 3)
        count = lora_own.shape[0]

        def step(i, carry):
            place = pl.multiple_of(i * block, 64)
            at = pl.multiple_of(meta[6] * count + place, 64)
            g = jnp.concatenate([ref[pl.ds(at, block), :] for ref in grads], axis=1)
            mask = row_mask(meta, at, block)
            lora_own[pl.ds(place, block), :] = (
                dot(g, bd_s[...]) * jnp.concatenate([mask] * 3, axis=1)
            ).astype(BF)
            return carry

        lax.fori_loop(0, count // block, step, 0)
    sections = []
    for index in range(groups):
        for k in range(arrays):
            ref = tokens[index * arrays + k]
            rows = ref.shape[0]
            at = 0 if arrays == 1 else (meta[5] if k == 0 else 1 - meta[5]) * rows
            slot = index * arrays + k
            turned[slot] = loras[index][pl.ds(at if arrays == 1 else pl.multiple_of(at, 64), rows), :].T
            sections.append((slot, ref))
    for i in range(0, D, BLOCK):
        total = None
        for slot, ref in sections:
            piece = dot(turned[slot], ref[:, i : i + BLOCK])
            total = piece if total is None else total + piece
        sums[i : i + BLOCK, : 3 * AR] = total.T.astype(BF)
    sums[:, 3 * AR :] = jnp.zeros((D, 3 * AR), BF)
    each = grads[0].shape[1]
    group = each // 3
    for c in range(3):
        few = [low[:, c * AR : (c + 1) * AR].T for low in lows]
        for p in range(parts):
            total = None
            for index in range(groups):
                rows = lows[index].shape[0]
                if groups == 1:
                    at = pl.ds(0, rows)
                else:
                    chip = meta[6] if index == 0 else 1 - meta[6]
                    at = pl.ds(pl.multiple_of(chip * rows, 256), rows)
                piece = dot(few[index], grads[p][at, c * group : (c + 1) * group])
                total = piece if total is None else total + piece
            own = pl.multiple_of(meta[4] * group * parts + p * group, math.gcd(group, 256))
            sums[pl.ds(own, group), (3 + c) * AR : (4 + c) * AR] = total.T.astype(BF)


def project_sums(meta, grads, lows, lora_far, tokens, weights):
    flat = [t for arrays in tokens for t in arrays]
    rows = flat[0].shape[0]
    columns = sum(g.shape[1] for g in grads)
    outs = (shape((D, 6 * AR)),)
    scratch = [pltpu.VMEM((len(flat), 3 * AR, rows), BF)]
    if len(lows) > 1:
        outs += (shape(lows[0].shape),)
        scratch += [
            pltpu.VMEM((D, 6 * AR), BF),
            pltpu.VMEM((columns, 3 * AR), BF),
            pltpu.SemaphoreType.DMA((3,)),
        ]
    else:
        weights = ()
    return call(
        partial(
            project_sums_kernel,
            parts=len(grads),
            groups=len(lows),
            arrays=len(tokens[0]),
            block=320,
        ),
        "project_sums",
        outs,
        [SMEM] + [VMEM] * (len(grads) + len(lows) + 1 + len(flat)) + [HBM] * len(weights),
        scratch,
        0.05,
    )(meta, *grads, *lows, lora_far, *flat, *weights)


def swap(value, axis, count, step):
    return lax.ppermute(value, axis, [(i, i ^ step) for i in range(count)])


def fence(*values):
    return lax.optimization_barrier(values)


def after(value, *earlier):
    return lax.optimization_barrier((value, *earlier))[0]


def sum_over_seq(value, seq_count):
    for step in (1, 2):
        value = (value.astype(F32) + swap(value, "seq", seq_count, step).astype(F32)).astype(BF)
    return value


def reduce_quarter(value, core, chip, seq_count, fsdp_count):
    def halves(v, index, step):
        v = v.reshape(fsdp_count, 2, v.shape[1] // 2, v.shape[2])
        keep = jnp.where(index == 0, v[:, 0], v[:, 1])
        give = jnp.where(index == 0, v[:, 1], v[:, 0])
        return (keep.astype(F32) + swap(give, "seq", seq_count, step).astype(F32)).astype(BF)

    value = value.reshape(fsdp_count, value.shape[0] // fsdp_count, value.shape[1])
    return halves(halves(value, core, 1), chip, 2)


def owned(value):
    return lax.all_to_all(value, "fsdp", split_axis=0, concat_axis=0, tiled=True)


def joined(value, index, seq_count, step):
    far = swap(value, "seq", seq_count, step)
    return jnp.where(index == 0, jnp.concatenate([value, far]), jnp.concatenate([far, value]))


def reduce_rows(value):
    return lax.psum_scatter(value, "fsdp", scatter_dimension=0, tiled=True)


def local(
    tokens,
    cont_lengths,
    adapter_ids,
    attn_gain,
    mlp_gain,
    query_scale,
    w_qkv,
    output_weight,
    inward_weight,
    down_weight,
    projection_first_factor,
    b_qkv,
    output_first_factor,
    output_second_factor,
    inward_first_factor,
    inward_second_factor,
    down_first_factor,
    down_second_factor,
    cotangent,
    seq_count,
    fsdp_count,
):
    rows = tokens.shape[1]
    shard = w_qkv.shape[1]
    width = D // seq_count
    paired = seq_count == 4
    place = lax.axis_index("seq")
    core = place % 2
    chip = place // 2 if paired else place * 0
    span = rows if rows % 128 == 0 else GLEN
    meta = jnp.concatenate(
        [
            adapter_ids[0],
            PROMPT + cont_lengths[0, :1],
            jnp.stack([place, core, chip, place * 0]),
        ]
    ).astype(jnp.int32)

    parts = 2 if paired else 1
    group = width // parts

    def heads_part(layer):
        return jnp.concatenate(
            [
                lax.dynamic_slice(
                    w_qkv, (layer, 0, c * D + place * width + p * group), (1, shard, group)
                )[0]
                for p in range(parts)
                for c in range(3)
            ],
            axis=1,
        )

    def both_part(layer):
        turned = jnp.concatenate([b_qkv[layer, c].T for c in range(3)], axis=1)
        return jnp.where(core == 0, projection_first_factor[layer], turned)

    def side_part(layer):
        whole = jnp.concatenate(
            [
                output_weight[layer],
                output_first_factor[layer],
                output_second_factor[layer].T,
                inward_weight[layer],
                inward_first_factor[layer],
                inward_second_factor[layer].T,
                down_weight[layer],
                down_first_factor[layer],
                down_second_factor[layer].T,
            ],
            axis=1,
        )
        half = PART // 2
        return jnp.where(
            core == 0,
            jnp.concatenate([whole[:, k * PART : k * PART + half] for k in range(3)], axis=1),
            jnp.concatenate([whole[:, k * PART + half : (k + 1) * PART] for k in range(3)], axis=1),
        )

    def gathered(value):
        return lax.all_gather(value, "fsdp", axis=0, tiled=True)

    def other_core(own, columns):
        return swap(own[:, :columns], "seq", seq_count, 1)

    def to_rows(mixed):
        if span != rows:
            mixed = mixed[0].reshape(group, seq_count, rows).transpose(1, 0, 2)
        return lax.all_to_all(mixed, "seq", split_axis=0, concat_axis=0, tiled=True)

    def to_heads(value):
        value = lax.all_to_all(value, "seq", split_axis=0, concat_axis=0, tiled=True)
        if span != rows:
            value = value.transpose(1, 0, 2).reshape(1, group, GLEN)
        return value

    both = 3 * AR
    head_weights, side_weights, kept = [], [], []

    def gather_head(layer, *earlier):
        value = jnp.concatenate([both_part(layer), heads_part(layer)], axis=1)
        return gathered(after(value, *earlier) if earlier else value)

    head_gathered = gather_head(0)
    side_gathered = gathered(after(side_part(0), head_gathered))
    hidden = tokens[0].astype(F32)
    normed = (hidden * rms_of(hidden) * attn_gain[0]).astype(BF)
    if paired:
        far = swap(normed, "seq", seq_count, 2)
        head_gathered, far = fence(head_gathered, far)
    for layer in range(LAYERS):
        last = layer == LAYERS - 1
        factor = 1.442695041 / math.sqrt(HD) * jax.nn.softplus(query_scale[layer])
        tiled = jnp.concatenate([jnp.tile(factor * LOG2E, group // HD), jnp.ones((2 * group,), F32)])
        scale = jnp.tile(tiled, parts).reshape(1, 3 * width)
        if layer > 0 and paired:
            cut = rows * 3 // 5
            far = swap(normed[:cut], "seq", seq_count, 2)
            head_gathered, far, rest = fence(head_gathered, far, normed[cut:])
            next_side = gathered(after(side_part(layer), head_gathered))
            far = [far, swap(rest, "seq", seq_count, 2)]
        head_weights.append((head_gathered[None], other_core(head_gathered, both)[None]))
        if layer > 0:
            side_gathered = (
                next_side if paired else gathered(after(side_part(layer), head_gathered))
            )
        if paired:
            own = ([normed, swap(normed, "seq", seq_count, 1)], chip * 2 * rows)
            projected = [project(meta, scale, own[0], head_weights[layer], own[1], parts)]
            if layer > 0:
                far[0], far[1], projected[0] = fence(far[0], far[1], projected[0])
                far = jnp.concatenate(far)
            else:
                far = after(far, projected[0][-1])
            far = ([far, swap(far, "seq", seq_count, 1)], (1 - chip) * 2 * rows)
            projected.append(project(meta, scale, far[0], head_weights[layer], far[1], parts))
            groups = [own, far]
        else:
            groups = [([lax.all_gather(normed, "seq", axis=0, tiled=True)], place * 0)]
            projected = [project(meta, scale, groups[0][0], head_weights[layer], place * 0, parts)]
        heads = [[p[k] for p in projected] for k in range(parts)]
        attended, mixed = [], []
        for p in range(parts):
            inputs = heads[p] if p == 0 else [after(h, attended[-1][1]) for h in heads[p]]
            attended.append(attend(meta, inputs, span))
            if p < parts - 1:
                mixed.append(to_rows(attended[-1][0]))
        attended, mixed = fence(attended, mixed)
        side_gathered = after(side_gathered, attended[-1][1])
        mixed = mixed + [to_rows(attended[-1][0])]
        side_weights.append((side_gathered, other_core(side_gathered, SIDE // 2)))
        if not last:
            head_gathered = gather_head(layer + 1, attended[-1][1], side_gathered)
        results = feed(
            meta,
            mlp_gain[layer][None],
            attn_gain[(layer + 1) % LAYERS][None],
            mixed,
            hidden,
            side_weights[layer],
            last,
        )
        kept.append(
            (hidden, groups, heads, [p[-1] for p in projected], attended, mixed, factor)
            + tuple(results[:3])
        )
        if last:
            layer_output = results[3]
        else:
            hidden, normed = results[3:]

    grad = cotangent[0]
    pending = None
    sums = [None] * LAYERS
    for layer in reversed(range(LAYERS)):
        hidden, groups, heads, lows, attended, mixed, factor, middle, inner, low = kept[layer]
        gain = mlp_gain[layer][None]
        results = feed_back(
            meta, gain, grad, middle, inner, side_weights[layer], parts, seq_count, pending
        )
        results = fence(*results)
        grad_in = grad if pending is None else results[5 + parts]
        grad, gi, gm, dl, il = results[:5]
        mixed_grads = [to_heads(results[5])]
        side_sum = feed_sums(gain, grad_in, middle, inner, gi, gm, dl, il, low, mixed)
        mixed_grads, side_sum = fence(mixed_grads, side_sum)
        side_total = reduce_rows(side_sum)
        factor_row = jnp.pad(factor, (0, 128 - HD)).reshape(1, 128)
        head_grads = []
        for p in range(parts):
            if p < parts - 1:
                mixed_grads.append(to_heads(after(results[6 + p], side_sum)))
            head_grads.append(
                attend_back(meta, factor_row, attended[p][1], attended[p][0], mixed_grads[p])
            )
            if p == parts - 1 and layer < LAYERS - 1 and paired:
                whole = sum_over_seq(jnp.stack(sums[layer + 1]), seq_count)
                head_grads, mixed_grads, whole = fence(head_grads, mixed_grads, whole)
                sums[layer + 1] = (whole[0], whole[1])
            else:
                head_grads, mixed_grads = fence(head_grads, mixed_grads)
        if paired:
            own, far = groups
            far_back = project_back(
                meta, head_grads, head_weights[layer], far[1], 2, rows, "far"
            )
            far_sum = (
                far_back[0].astype(F32) + swap(far_back[1], "seq", seq_count, 1).astype(F32)
            ).astype(BF)
            far_sum, head_grads, side_total = fence(far_sum, head_grads, side_total)
            cut = rows * (3 if layer > 0 else 2) // 5
            crossed = swap(far_sum[:cut], "seq", seq_count, 2)
            head_sum, lora_own = project_sums(
                meta, head_grads, lows, far_back[2], [g[0] for g in groups], head_weights[layer]
            )
            if layer == 0:
                side_total = sum_over_seq(side_total, seq_count)
            head_sum, lora_own, crossed, head_grads, rest, side_total = fence(
                head_sum, lora_own, crossed, head_grads, far_sum[cut:], side_total
            )
            if layer > 0:
                head_total = reduce_rows(head_sum)
            else:
                head_total = reduce_quarter(head_sum, core, chip, seq_count, fsdp_count)
            if layer > 0:
                rest = swap(rest, "seq", seq_count, 2)
            own_back = project_back(
                meta, head_grads, head_weights[layer], own[1], 2, rows, "own", lora_own
            )
            if layer > 0:
                own_back, rest = fence(own_back, rest)
            else:
                own_back, head_total, rest = fence(own_back, head_total, rest)
                rest = swap(rest, "seq", seq_count, 2)
                head_total = owned(head_total)
                head_total, rest = fence(head_total, rest)
            near = swap(own_back[1], "seq", seq_count, 1)
            sums[layer] = (side_total, head_total)
            terms = [own_back[0], near, crossed, rest]
        else:
            back = project_back(
                meta, head_grads, head_weights[layer], place * 0, 1, GLEN, "all"
            )
            terms = [lax.psum_scatter(back[0], "seq", scatter_dimension=0, tiled=True)]
            head_sum = project_sums(
                meta, head_grads, lows, back[1], [g[0] for g in groups], head_weights[layer]
            )[0]
            sums[layer] = tuple(lax.psum(v, "seq") for v in (side_total, reduce_rows(head_sum)))
        if layer > 0 and paired:
            pending = (attn_gain[layer][None], hidden, terms)
        else:
            grad = norm_back(attn_gain[layer][None], grad, hidden, terms)
            if paired:
                head_total = joined(jnp.sum(head_total.astype(F32), axis=0).astype(BF), chip, seq_count, 2)
                grad, head_total = fence(grad, head_total)
                sums[0] = (sums[0][0], joined(head_total, core, seq_count, 1))

    side = jnp.stack([s[0] for s in sums]).astype(F32)
    head = jnp.stack([s[1] for s in sums]).astype(F32)

    def columns(slot):
        return side[:, :, slot * AR : (slot + 1) * AR]

    return (
        layer_output[None],
        grad[None],
        head[:, :, : 3 * AR],
        head[:, :, 3 * AR :].reshape(LAYERS, shard, 3, AR).transpose(0, 2, 3, 1),
        columns(0),
        columns(1).transpose(0, 2, 1),
        columns(2),
        columns(3).transpose(0, 2, 1),
        columns(4),
        columns(5).transpose(0, 2, 1),
    )


def solution(mesh):
    rows = P("fsdp", "seq", None)
    first = P(None, "fsdp", None)
    second = P(None, None, "fsdp")
    return jax.shard_map(
        partial(local, seq_count=mesh.shape["seq"], fsdp_count=mesh.shape["fsdp"]),
        mesh=mesh,
        in_specs=(
            rows,
            P("fsdp", None),
            P("fsdp", None),
            P(),
            P(),
            P(),
            first,
            first,
            first,
            first,
            first,
            P(None, None, None, "fsdp"),
            first,
            second,
            first,
            second,
            first,
            second,
            rows,
        ),
        out_specs=(
            rows,
            rows,
            first,
            P(None, None, None, "fsdp"),
            first,
            second,
            first,
            second,
            first,
            second,
        ),
        check_vma=False,
    )
```

```python
from functools import partial
import math

import jax
import jax.numpy as jnp
from jax import lax
from jax.experimental import pallas as pl
from jax.experimental.pallas import tpu as pltpu
from jax.sharding import PartitionSpec as P

D = 1280
HEADS = 16
HD = 80
R = 16
LAYERS = 2
PROMPT = 2048
AR = 128
GLEN = 2560
LOG2E = 1.4426950408889634
LN2 = 0.6931471805599453
ROFF = 8
NEG = -1e30
BLOCK = 256
KEYS = 512
CHUNK = 1024
WIDE = D + AR
PART = D + 2 * AR
SIDE = 3 * PART
BF = jnp.bfloat16
F32 = jnp.float32
NN = (((1,), (0,)), ((), ()))
NT = (((1,), (1,)), ((), ()))
VMEM = pl.BlockSpec(memory_space=pltpu.VMEM)
SMEM = pl.BlockSpec(memory_space=pltpu.SMEM)
HBM = pl.BlockSpec(memory_space=pl.ANY)


def dot(left, right, dims=NN):
    return lax.dot_general(left, right, dims, preferred_element_type=F32)


def call(kernel, name, outs, specs, scratch, expected, out_specs=None):
    return pl.pallas_call(
        kernel,
        out_shape=outs,
        in_specs=specs,
        out_specs=tuple(VMEM for _ in outs) if out_specs is None else out_specs,
        scratch_shapes=scratch,
        compiler_params=pltpu.CompilerParams(vmem_limit_bytes=60 << 20),
        cost_estimate=pl.CostEstimate(
            flops=int(expected * 1.15e9), bytes_accessed=1024, transcendentals=0
        ),
        name=name,
    )


def shape(dims, kind=BF):
    return jax.ShapeDtypeStruct(dims, kind)


def sigmoid(v):
    return 1.0 / (1.0 + jnp.exp(-v))


def row_mask(meta, base, count):
    rows = lax.broadcasted_iota(jnp.int32, (count, AR), 0) + base
    lane = lax.broadcasted_iota(jnp.int32, (count, AR), 1)
    chosen = jnp.where(rows < PROMPT, meta[0], jnp.where(rows < meta[3], meta[1], meta[2]))
    low = chosen * R
    return jnp.where((lane >= low) & (lane < low + R), 1.0, 0.0).astype(F32)


def columns_of(ref, at, width):
    return ref if width == ref.shape[1] else ref.at[:, pl.ds(at, width)]


def head_copies(meta, pieces, wq_s, cb_s, sems):
    core, both = meta[5], 3 * AR
    n = len(pieces) // 2
    single = n == 1 and pieces[0].shape[0] == 1
    copies, block_at = [], 0
    for own, other in zip(pieces[:n], pieces[n:]):
        blocks, rows, columns = own.shape
        for block in range(blocks):
            at = 0 if single else pl.multiple_of(meta[ROFF + block_at], math.gcd(rows, 256))
            into = pl.ds(at, rows)
            for source, target in (
                (own.at[block, :, :both], cb_s.at[into, pl.ds(pl.multiple_of(core * both, both), both)]),
                (other.at[block], cb_s.at[into, pl.ds(pl.multiple_of((1 - core) * both, both), both)]),
                (own.at[block, :, both:], None if wq_s is None else wq_s.at[into]),
            ):
                if target is not None:
                    copies.append(pltpu.make_async_copy(source, target, sems.at[len(copies)]))
            block_at += 1
    return copies


def side_copies(meta, own, other, which, r_s, sems):
    half = PART // 2
    return [
        pltpu.make_async_copy(
            columns_of(ref, which * half, half),
            columns_of(r_s, pl.multiple_of(which * PART + side * half, half), half),
            sems.at[which, k],
        )
        for k, (ref, side) in enumerate(((own, meta[5]), (other, 1 - meta[5])))
    ]


def start_all(copies):
    for copy in copies:
        copy.start()
    return copies


def wait_all(copies):
    for copy in copies:
        copy.wait()


def run_copies(copies):
    wait_all(start_all(copies))


def fill_second(meta, cb_s, bd_s, width, group):
    bd_s[...] = jnp.zeros_like(bd_s)
    for p in range(width // group):
        start = pl.multiple_of(meta[4] * width + p * group, math.gcd(group, 256))
        for c in range(3):
            at = (p * 3 + c) * group
            bd_s[at : at + group, c * AR : (c + 1) * AR] = cb_s[
                pl.ds(start, group), (3 + c) * AR : (4 + c) * AR
            ]


def project_kernel(*refs, arrays, pieces, parts, block):
    meta, scale = refs[:2]
    tokens = refs[2 : 2 + arrays]
    weights = refs[2 + arrays : 2 + arrays + pieces]
    heads = refs[2 + arrays + pieces : 2 + arrays + pieces + parts]
    low_out, wq_s, cb_s, bd_s, sems = refs[2 + arrays + pieces + parts :]
    run_copies(head_copies(meta, weights, wq_s, cb_s, sems))
    columns = wq_s.shape[1]
    each = columns // parts
    fill_second(meta, cb_s, bd_s, columns // 3, each // 3)
    for k in range(arrays):
        rows = tokens[k].shape[0]
        local = 0 if arrays == 1 else (meta[5] if k == 0 else 1 - meta[5]) * rows

        def step(i, carry, k=k, local=local):
            x = tokens[k][pl.ds(pl.multiple_of(i * block, 64), block), :]
            place = pl.multiple_of(local + i * block, 64)
            mask = row_mask(meta, meta[7] + place, block)
            low = dot(x, cb_s[:, : 3 * AR]) * jnp.concatenate([mask] * 3, axis=1)
            low = low.astype(BF)
            low_out[pl.ds(place, block), :] = low
            both = ((dot(x, wq_s[...]) + dot(low, bd_s[...], NT)) * scale[...]).astype(BF)
            for p in range(parts):
                heads[p][pl.ds(place, block), :] = both[:, p * each : (p + 1) * each]
            return carry

        lax.fori_loop(0, rows // block, step, 0)


def project(meta, scale, tokens, weights, base, parts):
    arrays = len(tokens)
    rows = tokens[0].shape[0]
    count = rows * arrays
    columns = scale.shape[1]
    return call(
        partial(
            project_kernel, arrays=arrays, pieces=len(weights), parts=parts, block=320
        ),
        "project",
        (shape((count, columns // parts)),) * parts + (shape((count, 3 * AR)),),
        [SMEM, VMEM] + [VMEM] * arrays + [HBM] * len(weights),
        [
            pltpu.VMEM((D, columns), BF),
            pltpu.VMEM((D, 6 * AR), BF),
            pltpu.VMEM((columns, 3 * AR), BF),
            pltpu.SemaphoreType.DMA((3 * sum(w.shape[0] for w in weights),)),
        ],
        13,
    )(meta.at[7].set(base), scale, *tokens, *weights)


def load_rows(meta, sources, target, sems):
    copies = []
    for index, ref in enumerate(sources):
        rows = ref.shape[0]
        if len(sources) == 1:
            into = target
        else:
            into = target.at[pl.ds(pl.multiple_of(meta[6] * rows if index == 0 else (1 - meta[6]) * rows, 256), rows)]
        copies.append(pltpu.make_async_copy(ref, into, sems.at[index]))
    run_copies(copies)


def allowed_pairs(meta, queries, keys, query_at, key_at):
    same = (keys >= meta[3]) | (queries < meta[3])
    causal = keys <= queries
    return causal & same if key_at >= PROMPT else causal


def three_parts(x):
    high = x.astype(BF).astype(F32)
    rest = x - high
    middle = rest.astype(BF).astype(F32)
    return high, middle, (rest - middle).astype(BF).astype(F32)


def with_parts(base, place, value):
    a, b, c = three_parts(value)
    return jnp.where(place == 0, a, jnp.where(place == 1, b, jnp.where(place == 2, c, base)))


def attend_kernel(*refs, groups, local_heads):
    meta = refs[0]
    sources = refs[1 : 1 + groups]
    out, saved, hs, q_s, k_s, v_s, sems, out_sems = refs[1 + groups :]
    load_rows(meta, sources, hs, sems)
    width = local_heads * HD
    span = out.shape[2]
    lane = lax.broadcasted_iota(jnp.int32, (BLOCK, 128), 1)
    for h in range(local_heads):
        for i in range(GLEN // BLOCK):
            r = slice(i * BLOCK, (i + 1) * BLOCK)
            for c, ref in ((0, q_s), (1, k_s), (2, v_s)):
                x = hs[r, c * width + h * HD : c * width + (h + 1) * HD]
                fill = jnp.ones if c > 0 else jnp.zeros
                ref[h, r, :] = jnp.concatenate([x, fill((BLOCK, 128 - HD), BF)], axis=1)
    stores = [
        pltpu.make_async_copy(ref, saved.at[c], out_sems.at[c])
        for c, ref in ((0, q_s), (1, k_s), (2, v_s))
    ]
    stores[1].start()
    stores[2].start()

    def head(h, carry):
        place = pl.multiple_of(h * HD, 16)
        for i in range(GLEN // BLOCK):
            q0 = i * BLOCK
            nk = q0 + BLOCK
            d0 = min(q0, PROMPT)
            rows = lax.broadcasted_iota(jnp.int32, (BLOCK, nk - d0), 0) + q0
            cols = lax.broadcasted_iota(jnp.int32, (BLOCK, nk - d0), 1) + d0
            qb = q_s[h, q0 : q0 + BLOCK, :]
            sd = jnp.where(
                allowed_pairs(meta, rows, cols, q0, d0), dot(qb, k_s[h, d0:nk, :], NT), NEG
            )
            peak = jnp.max(sd, axis=1, keepdims=True)
            if d0 > 0:
                sp = dot(qb, k_s[h, 0:d0, :], NT)
                peak = jnp.maximum(peak, jnp.max(sp, axis=1, keepdims=True))
            total = dot(jnp.exp2(sd - peak).astype(BF), v_s[h, d0:nk, :])
            if d0 > 0:
                total = total + dot(jnp.exp2(sp - peak).astype(BF), v_s[h, 0:d0, :])
            lse = peak + jnp.log2(total[:, HD : HD + 1])
            q_s[h, q0 : q0 + BLOCK, :] = with_parts(qb.astype(F32), lane - HD, -lse).astype(BF)
            turned = total.T
            result = (turned[:HD, :] * (1.0 / turned[HD : HD + 1, :])).astype(BF)
            for part in range(BLOCK // 128):
                t = q0 + part * 128
                out[t // span, pl.ds(place, HD), t % span : t % span + 128] = result[
                    :, part * 128 : (part + 1) * 128
                ]
        return carry

    lax.fori_loop(0, local_heads, head, 0)
    stores[0].start()
    wait_all(stores)


def attend(meta, heads, span):
    width = heads[0].shape[1]
    local_heads = width // (3 * HD)
    return call(
        partial(attend_kernel, groups=len(heads), local_heads=local_heads),
        "attend",
        (shape((GLEN // span, local_heads * HD, span)), shape((3, local_heads, GLEN, 128))),
        [SMEM] + [HBM] * len(heads),
        [pltpu.VMEM((GLEN, width), BF)]
        + [pltpu.VMEM((local_heads, GLEN, 128), BF)] * 3
        + [pltpu.SemaphoreType.DMA((len(heads),)), pltpu.SemaphoreType.DMA((3,))],
        16,
        out_specs=(VMEM, HBM),
    )(meta, *heads)


def attend_back_kernel(meta, factor, saved, o_ref, do_ref, out, q_s, k_s, v_s, dt_s, kt_s, dqt_s, sems):
    local_heads = saved.shape[1]
    width = local_heads * HD
    span = o_ref.shape[2]
    loads = [
        start_all(
            [
                pltpu.make_async_copy(saved.at[c, h], ref.at[h], sems.at[c, h])
                for c, ref in ((0, q_s), (1, k_s), (2, v_s))
            ]
        )
        for h in range(local_heads)
    ]
    extra = lax.broadcasted_iota(jnp.int32, (128 - HD, 128), 0)
    for h in range(local_heads):
        cs = slice(h * HD, (h + 1) * HD)
        for i in range(GLEN // 128):
            t, inner = (i * 128) // span, slice((i * 128) % span, (i * 128) % span + 128)
            do = do_ref[t, cs, inner]
            delta = jnp.sum(do.astype(F32) * o_ref[t, cs, inner].astype(F32), axis=0, keepdims=True)
            dt_s[h, :HD, i * 128 : (i + 1) * 128] = do
            dt_s[h, HD:, i * 128 : (i + 1) * 128] = with_parts(0.0, extra, -delta).astype(BF)
    for h in range(local_heads):
        wait_all(loads[h])
        for i in range(GLEN // KEYS):
            kt_s[:, i * KEYS : (i + 1) * KEYS] = k_s[h, i * KEYS : (i + 1) * KEYS, :].T
        for j in range(GLEN // KEYS):
            k0 = j * KEYS
            kb = k_s[h, k0 : k0 + KEYS, :]
            vb = v_s[h, k0 : k0 + KEYS, :]
            dk = jnp.zeros((KEYS, 128), F32)
            dv = jnp.zeros((KEYS, 128), F32)
            q0 = k0
            while q0 < GLEN:
                n = KEYS if q0 == k0 else min(CHUNK, GLEN - q0)
                qs = slice(q0, q0 + n)
                probs = jnp.exp2(dot(kb, q_s[h, qs, :], NT))
                if q0 == k0 or k0 >= PROMPT:
                    keys = lax.broadcasted_iota(jnp.int32, (KEYS, n), 0) + k0
                    queries = lax.broadcasted_iota(jnp.int32, (KEYS, n), 1) + q0
                    probs = jnp.where(allowed_pairs(meta, queries, keys, q0, k0), probs, 0.0)
                dscore = (probs * dot(vb, dt_s[h, :, qs])).astype(BF)
                dv = dv + dot(probs.astype(BF), dt_s[h, :, qs], NT)
                dk = dk + dot(dscore, q_s[h, qs, :])
                dq = dot(kt_s[:, k0 : k0 + KEYS], dscore)
                if j == 0:
                    dqt_s[:, qs] = dq
                else:
                    dqt_s[:, qs] += dq
                q0 += n
            r = slice(k0, k0 + KEYS)
            out[r, width + h * HD : width + (h + 1) * HD] = (dk[:, :HD] * LN2).astype(BF)
            out[r, 2 * width + h * HD : 2 * width + (h + 1) * HD] = dv[:, :HD].astype(BF)
            out[r, h * HD : (h + 1) * HD] = (dqt_s[:, r].T * factor[...]).astype(BF)[:, :HD]


def attend_back(meta, factor, saved, mixed, grad_mixed):
    local_heads = saved.shape[1]
    rows = pltpu.VMEM((local_heads, GLEN, 128), BF)
    return call(
        attend_back_kernel,
        "attend_back",
        (shape((GLEN, 3 * local_heads * HD)),),
        [SMEM, VMEM, HBM] + [VMEM] * 2,
        [rows] * 3
        + [
            pltpu.VMEM((local_heads, 128, GLEN), BF),
            pltpu.VMEM((128, GLEN), BF),
            pltpu.VMEM((128, GLEN), F32),
            pltpu.SemaphoreType.DMA((3, local_heads)),
        ],
        0.05,
    )(meta, factor, saved, mixed, grad_mixed)[0]


def rms_of(value):
    return lax.rsqrt(jnp.mean(value * value, axis=-1, keepdims=True) + 1e-06)


def feed_kernel(*refs, parts, pieces, block, last):
    meta, gain_mlp, gain_next, hidden_in = refs[:4]
    mixed = refs[4 : 4 + parts]
    weights = refs[4 + parts : 4 + parts + pieces]
    refs = refs[4 + parts + pieces :]
    middle_out, inner_out, low_out, result = refs[:4]
    normed_out = None if last else refs[4]
    hidden, middle_s, inner_s, r_s, mt_s, mx_s, sems, io_sems = refs[4 if last else 5 :]
    rows = hidden.shape[0]
    loads, slot = [], 0
    for p in range(parts):
        sources, group, _ = mixed[p].shape
        for source in range(sources):
            at = (source * parts + p) * group
            loads.append(
                pltpu.make_async_copy(
                    mixed[p].at[source], mt_s.at[at : at + group], io_sems.at[len(loads)]
                )
            )
    start_all(loads)
    load_hidden = pltpu.make_async_copy(hidden_in, hidden, io_sems.at[len(loads)])
    load_hidden.start()
    copies = [start_all(side_copies(meta, *weights, which, r_s, sems)) for which in range(3)]
    wait_all(loads)
    for i in range(0, rows, 128):
        n = min(128, rows - i)
        mx_s[i : i + n, :] = mt_s[:, i : i + n].T
    load_hidden.wait()

    def stage(which, body):
        wait_all(copies[which])

        def step(i, carry):
            r = pl.ds(pl.multiple_of(i * block, 64), block)
            mask = row_mask(meta, meta[4] * rows + i * block, block)

            def adapted(x):
                both = dot(x, r_s[:, which * PART : which * PART + WIDE])
                low = (both[:, D:] * mask).astype(BF)
                low_out[r, which * AR : (which + 1) * AR] = low
                return both[:, :D] + dot(low, r_s[:, which * PART + WIDE : (which + 1) * PART], NT)

            body(r, adapted)
            return carry

        lax.fori_loop(0, rows // block, step, 0)

    def out_stage(r, adapted):
        middle_s[r, :] = hidden[r, :] + adapted(mx_s[r, :])

    def in_stage(r, adapted):
        middle = middle_s[r, :]
        inner_s[r, :] = adapted((middle * rms_of(middle) * gain_mlp[...]).astype(BF))

    def down_stage(r, adapted):
        inner = inner_s[r, :]
        value = middle_s[r, :] + adapted((inner * sigmoid(inner)).astype(BF))
        result[r, :] = value.astype(result.dtype)
        if not last:
            normed_out[r, :] = (value * rms_of(value) * gain_next[...]).astype(BF)

    stage(0, out_stage)
    store_middle = pltpu.make_async_copy(middle_s, middle_out, io_sems.at[len(loads) + 1])
    store_middle.start()
    stage(1, in_stage)
    store_inner = pltpu.make_async_copy(inner_s, inner_out, io_sems.at[len(loads) + 2])
    store_inner.start()
    stage(2, down_stage)
    store_middle.wait()
    store_inner.wait()


def feed(meta, gain_mlp, gain_next, mixed, hidden, weights, last):
    rows = hidden.shape[0]
    row = pltpu.VMEM((rows, D), F32)
    outs = (shape((rows, D), F32), shape((rows, D), F32), shape((rows, 3 * AR)))
    outs += (shape((rows, D), BF),) if last else (shape((rows, D), F32), shape((rows, D), BF))
    return call(
        partial(
            feed_kernel,
            parts=len(mixed),
            pieces=2,
            block=math.gcd(rows, 320),
            last=last,
        ),
        "feed",
        outs,
        [SMEM] + [VMEM] * 2 + [HBM] * (1 + len(mixed) + 2),
        [
            row,
            row,
            row,
            pltpu.VMEM((D, SIDE), BF),
            pltpu.VMEM((D, rows), BF),
            pltpu.VMEM((rows, D), BF),
            pltpu.SemaphoreType.DMA((3, 2)),
            pltpu.SemaphoreType.DMA((sum(m.shape[0] for m in mixed) + 3,)),
        ],
        17,
        out_specs=(HBM, HBM) + (VMEM,) * (len(outs) - 2),
    )(meta, gain_mlp, gain_next, hidden, *mixed, *weights)


def rms_back(grad, value, gain, grad_normed):
    r = rms_of(value)
    e = gain * grad_normed
    return grad + r * e - value * (r * r * r) * jnp.mean(value * e, axis=-1, keepdims=True)


def feed_back_kernel(*refs, parts, pieces, block, terms):
    meta, gain_mlp, grad_hbm, middle_hbm, inner_hbm = refs[:5]
    weights = refs[5 : 5 + pieces]
    refs = refs[5 + pieces :]
    if terms:
        gain_next, hidden_hbm, term_hbm = refs[0], refs[1], refs[2 : 2 + terms]
        refs = refs[2 + terms :]
    grad_out, gi_s, gm_s, dl_s, il_s = refs[:5]
    mixed_grad = refs[5 : 5 + parts]
    refs = refs[5 + parts :]
    if terms:
        gl_out, refs = refs[0], refs[1:]
    grad_in, middle_s, inner_s, r_s, sems, io_sems = refs[:6]
    rows = grad_in.shape[0]
    early = []
    if terms:
        hidden_s, term_s, term_sems = refs[6], refs[7 : 7 + terms - 1], refs[7 + terms - 1]
        early.append(pltpu.make_async_copy(hidden_hbm, hidden_s, term_sems.at[terms]))
        for k in range(terms - 2):
            early.append(pltpu.make_async_copy(term_hbm[k], term_s[k], term_sems.at[k]))
        cut = term_hbm[-2].shape[0]
        early.append(
            pltpu.make_async_copy(term_hbm[-2], term_s[-1].at[:cut], term_sems.at[terms - 2])
        )
        early.append(
            pltpu.make_async_copy(term_hbm[-1], term_s[-1].at[cut:], term_sems.at[terms - 1])
        )
        start_all(early)
    loads = start_all(
        [
            pltpu.make_async_copy(source, target, io_sems.at[k])
            for k, (source, target) in enumerate(
                ((grad_hbm, grad_in), (inner_hbm, inner_s), (middle_hbm, middle_s))
            )
        ]
    )
    copies = {which: start_all(side_copies(meta, *weights, which, r_s, sems)) for which in (2, 1, 0)}

    def rows_of(i):
        return pl.ds(pl.multiple_of(i * block, 64), block)

    def narrow(g, which, i):
        mask = row_mask(meta, meta[4] * rows + i * block, block)
        return (dot(g, r_s[:, which * PART + WIDE : (which + 1) * PART]) * mask).astype(BF)

    def across(g, low, which):
        both = jnp.concatenate([g, low], axis=1)
        return dot(both, r_s[:, which * PART : which * PART + WIDE], NT)

    def down_stage(i, carry):
        r = rows_of(i)
        gl = grad_in[r, :].astype(BF)
        dl = narrow(gl, 2, i)
        dl_s[r, :] = dl
        inner = inner_s[r, :]
        s = sigmoid(inner)
        gi_s[r, :] = (across(gl, dl, 2) * (s * (1.0 + inner * (1.0 - s)))).astype(BF)
        return carry

    def in_stage(i, carry):
        r = rows_of(i)
        gi = gi_s[r, :]
        il = narrow(gi, 1, i)
        il_s[r, :] = il
        grad = rms_back(grad_in[r, :].astype(F32), middle_s[r, :], gain_mlp[...], across(gi, il, 1))
        grad_out[r, :] = grad
        gm_s[r, :D] = grad.astype(BF)
        return carry

    def out_stage(i, carry):
        r = rows_of(i)
        gm_s[r, D:] = narrow(gm_s[r, :D], 0, i)
        return carry

    loads[0].wait()
    if terms:
        wait_all(early)

        def norm_stage(i, carry):
            r = rows_of(i)
            total = term_s[0][r, :].astype(F32)
            for ref in term_s[1:]:
                total = total + ref[r, :].astype(F32)
            grad = rms_back(grad_in[r, :], hidden_s[r, :], gain_next[...], total)
            grad_in[r, :] = grad
            gl_out[r, :] = grad.astype(BF)
            return carry

        lax.fori_loop(0, rows // block, norm_stage, 0)
    wait_all(copies[2])
    loads[1].wait()
    lax.fori_loop(0, rows // block, down_stage, 0)
    wait_all(copies[1])
    loads[2].wait()
    lax.fori_loop(0, rows // block, in_stage, 0)
    wait_all(copies[0])
    lax.fori_loop(0, rows // block, out_stage, 0)
    sources, group, _ = mixed_grad[0].shape
    for source in range(sources):
        for p in range(parts):
            at = (source * parts + p) * group
            mixed_grad[p][source] = dot(r_s[at : at + group, :WIDE], gm_s[...], NT).astype(BF)


def feed_back(meta, gain_mlp, grad, middle, inner, weights, parts, sources, norm=None):
    rows = grad.shape[0]
    narrow = shape((rows, AR))
    return call(
        partial(
            feed_back_kernel,
            parts=parts,
            pieces=2,
            block=math.gcd(rows, 320),
            terms=0 if norm is None else len(norm[2]),
        ),
        "feed_back",
        (shape((rows, D), F32), shape((rows, D)), shape((rows, WIDE)), narrow, narrow)
        + (shape((sources, D // sources // parts, rows)),) * parts
        + (() if norm is None else (shape((rows, D)),)),
        [SMEM, VMEM]
        + [HBM] * (3 + 2)
        + ([] if norm is None else [VMEM] + [HBM] * (1 + len(norm[2]))),
        [
            pltpu.VMEM((rows, D), grad.dtype),
            pltpu.VMEM((rows, D), F32),
            pltpu.VMEM((rows, D), F32),
            pltpu.VMEM((D, SIDE), BF),
            pltpu.SemaphoreType.DMA((3, 2)),
            pltpu.SemaphoreType.DMA((3,)),
        ]
        + (
            []
            if norm is None
            else [pltpu.VMEM((rows, D), F32)]
            + [pltpu.VMEM((rows, D), BF)] * (len(norm[2]) - 1)
            + [pltpu.SemaphoreType.DMA((len(norm[2]) + 1,))]
        ),
        0.05,
    )(
        meta,
        gain_mlp,
        grad,
        middle,
        inner,
        *weights,
        *(() if norm is None else (norm[0], norm[1], *norm[2])),
    )


def feed_sums_kernel(*refs, parts):
    gain_mlp, grad, middle_ref, inner_ref, gi, gm, dl, il, low = refs[:9]
    mixed = refs[9 : 9 + parts]
    sums = refs[9 + parts]
    for p in range(parts):
        sources, group, _ = mixed[p].shape
        for source in range(sources):
            at = (source * parts + p) * group
            sums[at : at + group, :AR] = dot(mixed[p][source], gm[:, D:]).astype(BF)
    inner = inner_ref[...]
    act = (inner * sigmoid(inner)).astype(BF)
    middle = middle_ref[...]
    nf = (middle * rms_of(middle) * gain_mlp[...]).astype(BF)
    pairs = (
        (1, low[:, :AR], gm[:, :D]),
        (2, il[...], nf),
        (3, low[:, AR : 2 * AR], gi[...]),
        (4, dl[...], act),
        (5, low[:, 2 * AR :], grad[...].astype(BF)),
    )
    for slot, few, wide in pairs:
        turned = few.T
        for i in range(0, D, BLOCK):
            part = dot(turned, wide[:, i : i + BLOCK])
            sums[i : i + BLOCK, slot * AR : (slot + 1) * AR] = part.T.astype(BF)


def feed_sums(gain_mlp, grad, middle, inner, gi, gm, dl, il, low, mixed):
    return call(
        partial(feed_sums_kernel, parts=len(mixed)),
        "feed_sums",
        (shape((D, 6 * AR)),),
        [VMEM] * (9 + len(mixed)),
        [],
        0.05,
    )(gain_mlp, grad, middle, inner, gi, gm, dl, il, low, *mixed)[0]


def norm_back_kernel(gain, grad, hidden, *refs, cut):
    total = refs[0][...].astype(F32)
    out = refs[-1]
    for ref in refs[1 : -3 if cut else -1]:
        total = total + ref[...].astype(F32)
    if cut:
        first = pl.program_id(0) < cut
        total = total + jnp.where(first, refs[-3][...], refs[-2][...]).astype(F32)
    out[...] = rms_back(grad[...], hidden[...], gain[...], total)


def norm_back(gain, grad, hidden, terms):
    rows = grad.shape[0]
    block = math.gcd(rows, 128)
    cut = terms[-2].shape[0] // block if terms[-1].shape[0] < rows else 0
    row = pl.BlockSpec((block, D), lambda i: (i, 0))
    specs = [row] * (2 + len(terms))
    if cut:
        specs[-2] = pl.BlockSpec((block, D), lambda i: (jnp.minimum(i, cut - 1), 0))
        specs[-1] = pl.BlockSpec((block, D), lambda i: (jnp.maximum(i - cut, 0), 0))
    return pl.pallas_call(
        partial(norm_back_kernel, cut=cut),
        grid=(rows // block,),
        out_shape=shape((rows, D), F32),
        in_specs=[pl.BlockSpec((1, D), lambda i: (0, 0))] + specs,
        out_specs=row,
        cost_estimate=pl.CostEstimate(flops=int(5e7), bytes_accessed=1024, transcendentals=0),
        name="norm_back",
    )(gain, grad, hidden, *terms)


def project_back_kernel(*refs, arrays, pieces, parts, block, mode):
    meta = refs[0]
    grads = refs[1 : 1 + parts]
    weights = refs[1 + parts : 1 + parts + pieces]
    refs = refs[1 + parts + pieces :]
    if mode == "own":
        lora_in, refs = refs[0], refs[1:]
    outs, refs = refs[:arrays], refs[arrays:]
    if mode != "own":
        lora_out, refs = refs[0], refs[1:]
    wq_s, cb_s, bd_s = refs[:3]
    g_s = refs[3 : 3 + parts]
    sems, row_sems = refs[3 + parts :]
    count = g_s[0].shape[0]
    rows_at = pl.ds(pl.multiple_of(meta[7], 256), count)
    loads = start_all(
        [
            pltpu.make_async_copy(
                grads[p] if count == GLEN else grads[p].at[rows_at], g_s[p], row_sems.at[p]
            )
            for p in range(parts)
        ]
    )
    copies = start_all(head_copies(meta, weights, wq_s, cb_s, sems))
    wait_all(copies)
    wait_all(loads)
    columns = wq_s.shape[1]
    each = columns // parts
    fill_second(meta, cb_s, bd_s, columns // 3, each // 3)

    def rows_of(place):
        at = pl.ds(pl.multiple_of(place, 64), block)
        return jnp.concatenate([g_s[p][at, :] for p in range(parts)], axis=1)

    def narrow(g, place):
        mask = row_mask(meta, meta[7] + place, block)
        return (dot(g, bd_s[...]) * jnp.concatenate([mask] * 3, axis=1)).astype(BF)

    for k in range(arrays):
        rows = outs[k].shape[0]
        local = 0 if arrays == 1 else (meta[5] if k == 0 else 1 - meta[5]) * rows

        def step(i, carry, k=k, local=local):
            place = pl.multiple_of(local + i * block, 64)
            g = rows_of(place)
            if mode == "own":
                lora = lora_in[pl.ds(place, block), :]
            else:
                lora = narrow(g, place)
                lora_out[pl.ds(place, block), :] = lora
            outs[k][pl.ds(pl.multiple_of(i * block, 64), block), :] = (
                dot(g, wq_s[...], NT) + dot(lora, cb_s[:, : 3 * AR], NT)
            ).astype(BF)
            return carry

        lax.fori_loop(0, rows // block, step, 0)


def project_back(meta, grads, weights, base, arrays, rows, mode, lora=None):
    columns = sum(g.shape[1] for g in grads)
    count = rows * arrays
    low = (shape((count, 3 * AR)),)
    return call(
        partial(
            project_back_kernel,
            arrays=arrays,
            pieces=len(weights),
            parts=len(grads),
            block=320,
            mode=mode,
        ),
        "project_back",
        tuple(shape((rows, D)) for _ in range(arrays)) + low * (mode != "own"),
        [SMEM] + [HBM] * (len(grads) + len(weights)) + [VMEM] * (mode == "own"),
        [
            pltpu.VMEM((D, columns), BF),
            pltpu.VMEM((D, 6 * AR), BF),
            pltpu.VMEM((columns, 3 * AR), BF),
        ]
        + [pltpu.VMEM((count, g.shape[1]), BF) for g in grads]
        + [
            pltpu.SemaphoreType.DMA((3 * sum(w.shape[0] for w in weights),)),
            pltpu.SemaphoreType.DMA((len(grads),)),
        ],
        0.05,
    )(meta.at[7].set(base), *grads, *weights, *(() if lora is None else (lora,)))


def project_sums_kernel(*refs, parts, groups, arrays, block):
    meta = refs[0]
    grads, refs = refs[1 : 1 + parts], refs[1 + parts :]
    lows, refs = refs[:groups], refs[groups:]
    lora_far, refs = refs[0], refs[1:]
    tokens, refs = refs[: groups * arrays], refs[groups * arrays :]
    if groups == 1:
        loras = [lora_far]
        sums, turned = refs
    else:
        weights, refs = refs[:2], refs[2:]
        sums, lora_own, turned, cb_s, bd_s, sems = refs
        loras = [lora_own, lora_far]
        run_copies(head_copies(meta, weights, None, cb_s, sems))
        each = grads[0].shape[1]
        fill_second(meta, cb_s, bd_s, each * parts // 3, each // 3)
        count = lora_own.shape[0]

        def step(i, carry):
            place = pl.multiple_of(i * block, 64)
            at = pl.multiple_of(meta[6] * count + place, 64)
            g = jnp.concatenate([ref[pl.ds(at, block), :] for ref in grads], axis=1)
            mask = row_mask(meta, at, block)
            lora_own[pl.ds(place, block), :] = (
                dot(g, bd_s[...]) * jnp.concatenate([mask] * 3, axis=1)
            ).astype(BF)
            return carry

        lax.fori_loop(0, count // block, step, 0)
    sections = []
    for index in range(groups):
        for k in range(arrays):
            ref = tokens[index * arrays + k]
            rows = ref.shape[0]
            at = 0 if arrays == 1 else (meta[5] if k == 0 else 1 - meta[5]) * rows
            slot = index * arrays + k
            turned[slot] = loras[index][pl.ds(at if arrays == 1 else pl.multiple_of(at, 64), rows), :].T
            sections.append((slot, ref))
    for i in range(0, D, BLOCK):
        total = None
        for slot, ref in sections:
            piece = dot(turned[slot], ref[:, i : i + BLOCK])
            total = piece if total is None else total + piece
        sums[i : i + BLOCK, : 3 * AR] = total.T.astype(BF)
    sums[:, 3 * AR :] = jnp.zeros((D, 3 * AR), BF)
    each = grads[0].shape[1]
    group = each // 3
    for c in range(3):
        few = [low[:, c * AR : (c + 1) * AR].T for low in lows]
        for p in range(parts):
            total = None
            for index in range(groups):
                rows = lows[index].shape[0]
                if groups == 1:
                    at = pl.ds(0, rows)
                else:
                    chip = meta[6] if index == 0 else 1 - meta[6]
                    at = pl.ds(pl.multiple_of(chip * rows, 256), rows)
                piece = dot(few[index], grads[p][at, c * group : (c + 1) * group])
                total = piece if total is None else total + piece
            own = pl.multiple_of(meta[4] * group * parts + p * group, math.gcd(group, 256))
            sums[pl.ds(own, group), (3 + c) * AR : (4 + c) * AR] = total.T.astype(BF)


def project_sums(meta, grads, lows, lora_far, tokens, weights):
    flat = [t for arrays in tokens for t in arrays]
    rows = flat[0].shape[0]
    columns = sum(g.shape[1] for g in grads)
    outs = (shape((D, 6 * AR)),)
    scratch = [pltpu.VMEM((len(flat), 3 * AR, rows), BF)]
    if len(lows) > 1:
        outs += (shape(lows[0].shape),)
        scratch += [
            pltpu.VMEM((D, 6 * AR), BF),
            pltpu.VMEM((columns, 3 * AR), BF),
            pltpu.SemaphoreType.DMA((3,)),
        ]
    else:
        weights = ()
    return call(
        partial(
            project_sums_kernel,
            parts=len(grads),
            groups=len(lows),
            arrays=len(tokens[0]),
            block=320,
        ),
        "project_sums",
        outs,
        [SMEM] + [VMEM] * (len(grads) + len(lows) + 1 + len(flat)) + [HBM] * len(weights),
        scratch,
        0.05,
    )(meta, *grads, *lows, lora_far, *flat, *weights)


def swap(value, axis, count, step):
    return lax.ppermute(value, axis, [(i, i ^ step) for i in range(count)])


def fence(*values):
    return lax.optimization_barrier(values)


def after(value, *earlier):
    return lax.optimization_barrier((value, *earlier))[0]


def sum_over_seq(value, seq_count):
    for step in (1, 2):
        value = (value.astype(F32) + swap(value, "seq", seq_count, step).astype(F32)).astype(BF)
    return value


def reduce_quarter(value, core, chip, seq_count, fsdp_count):
    def halves(v, index, step):
        v = v.reshape(fsdp_count, 2, v.shape[1] // 2, v.shape[2])
        keep = jnp.where(index == 0, v[:, 0], v[:, 1])
        give = jnp.where(index == 0, v[:, 1], v[:, 0])
        return (keep.astype(F32) + swap(give, "seq", seq_count, step).astype(F32)).astype(BF)

    value = value.reshape(fsdp_count, value.shape[0] // fsdp_count, value.shape[1])
    return halves(halves(value, core, 1), chip, 2)


def owned(value):
    return lax.all_to_all(value, "fsdp", split_axis=0, concat_axis=0, tiled=True)


def joined(value, index, seq_count, step):
    far = swap(value, "seq", seq_count, step)
    return jnp.where(index == 0, jnp.concatenate([value, far]), jnp.concatenate([far, value]))


def reduce_rows(value):
    return lax.psum_scatter(value, "fsdp", scatter_dimension=0, tiled=True)


def local(
    tokens,
    cont_lengths,
    adapter_ids,
    attn_gain,
    mlp_gain,
    query_scale,
    w_qkv,
    output_weight,
    inward_weight,
    down_weight,
    projection_first_factor,
    b_qkv,
    output_first_factor,
    output_second_factor,
    inward_first_factor,
    inward_second_factor,
    down_first_factor,
    down_second_factor,
    cotangent,
    seq_count,
    fsdp_count,
):
    rows = tokens.shape[1]
    shard = w_qkv.shape[1]
    width = D // seq_count
    paired = seq_count == 4
    place = lax.axis_index("seq")
    core = place % 2
    chip = place // 2 if paired else place * 0
    span = rows if rows % 128 == 0 else GLEN
    meta = jnp.concatenate(
        [
            adapter_ids[0],
            PROMPT + cont_lengths[0, :1],
            jnp.stack([place, core, chip, place * 0]),
        ]
    ).astype(jnp.int32)

    parts = 2 if paired else 1
    group = width // parts

    def heads_part(layer):
        return jnp.concatenate(
            [
                lax.dynamic_slice(
                    w_qkv, (layer, 0, c * D + place * width + p * group), (1, shard, group)
                )[0]
                for p in range(parts)
                for c in range(3)
            ],
            axis=1,
        )

    def both_part(layer):
        turned = jnp.concatenate([b_qkv[layer, c].T for c in range(3)], axis=1)
        return jnp.where(core == 0, projection_first_factor[layer], turned)

    def side_part(layer):
        whole = jnp.concatenate(
            [
                output_weight[layer],
                output_first_factor[layer],
                output_second_factor[layer].T,
                inward_weight[layer],
                inward_first_factor[layer],
                inward_second_factor[layer].T,
                down_weight[layer],
                down_first_factor[layer],
                down_second_factor[layer].T,
            ],
            axis=1,
        )
        half = PART // 2
        return jnp.where(
            core == 0,
            jnp.concatenate([whole[:, k * PART : k * PART + half] for k in range(3)], axis=1),
            jnp.concatenate([whole[:, k * PART + half : (k + 1) * PART] for k in range(3)], axis=1),
        )

    def gathered(value):
        return lax.all_gather(value, "fsdp", axis=0, tiled=True)

    def other_core(own, columns):
        return swap(own[:, :columns], "seq", seq_count, 1)

    def to_rows(mixed):
        if span != rows:
            mixed = mixed[0].reshape(group, seq_count, rows).transpose(1, 0, 2)
        return lax.all_to_all(mixed, "seq", split_axis=0, concat_axis=0, tiled=True)

    def to_heads(value):
        value = lax.all_to_all(value, "seq", split_axis=0, concat_axis=0, tiled=True)
        if span != rows:
            value = value.transpose(1, 0, 2).reshape(1, group, GLEN)
        return value

    both = 3 * AR
    head_weights, side_weights, kept = [], [], []

    def gather_head(layer, *earlier):
        value = jnp.concatenate([both_part(layer), heads_part(layer)], axis=1)
        return gathered(after(value, *earlier) if earlier else value)

    head_gathered = gather_head(0)
    side_gathered = gathered(after(side_part(0), head_gathered))
    hidden = tokens[0].astype(F32)
    normed = (hidden * rms_of(hidden) * attn_gain[0]).astype(BF)
    if paired:
        far = swap(normed, "seq", seq_count, 2)
        head_gathered, far = fence(head_gathered, far)
    for layer in range(LAYERS):
        last = layer == LAYERS - 1
        factor = 1.442695041 / math.sqrt(HD) * jax.nn.softplus(query_scale[layer])
        tiled = jnp.concatenate([jnp.tile(factor * LOG2E, group // HD), jnp.ones((2 * group,), F32)])
        scale = jnp.tile(tiled, parts).reshape(1, 3 * width)
        if layer > 0 and paired:
            cut = rows * 3 // 5
            far = swap(normed[:cut], "seq", seq_count, 2)
            head_gathered, far, rest = fence(head_gathered, far, normed[cut:])
            next_side = gathered(after(side_part(layer), head_gathered))
            far = [far, swap(rest, "seq", seq_count, 2)]
        head_weights.append((head_gathered[None], other_core(head_gathered, both)[None]))
        if layer > 0:
            side_gathered = (
                next_side if paired else gathered(after(side_part(layer), head_gathered))
            )
        if paired:
            own = ([normed, swap(normed, "seq", seq_count, 1)], chip * 2 * rows)
            projected = [project(meta, scale, own[0], head_weights[layer], own[1], parts)]
            if layer > 0:
                far[0], far[1], projected[0] = fence(far[0], far[1], projected[0])
                far = jnp.concatenate(far)
            else:
                far = after(far, projected[0][-1])
            far = ([far, swap(far, "seq", seq_count, 1)], (1 - chip) * 2 * rows)
            projected.append(project(meta, scale, far[0], head_weights[layer], far[1], parts))
            groups = [own, far]
        else:
            groups = [([lax.all_gather(normed, "seq", axis=0, tiled=True)], place * 0)]
            projected = [project(meta, scale, groups[0][0], head_weights[layer], place * 0, parts)]
        heads = [[p[k] for p in projected] for k in range(parts)]
        attended, mixed = [], []
        for p in range(parts):
            inputs = heads[p] if p == 0 else [after(h, attended[-1][1]) for h in heads[p]]
            attended.append(attend(meta, inputs, span))
            if p < parts - 1:
                mixed.append(to_rows(attended[-1][0]))
        attended, mixed = fence(attended, mixed)
        side_gathered = after(side_gathered, attended[-1][1])
        mixed = mixed + [to_rows(attended[-1][0])]
        side_weights.append((side_gathered, other_core(side_gathered, SIDE // 2)))
        if not last:
            head_gathered = gather_head(layer + 1, attended[-1][1], side_gathered)
        results = feed(
            meta,
            mlp_gain[layer][None],
            attn_gain[(layer + 1) % LAYERS][None],
            mixed,
            hidden,
            side_weights[layer],
            last,
        )
        kept.append(
            (hidden, groups, heads, [p[-1] for p in projected], attended, mixed, factor)
            + tuple(results[:3])
        )
        if last:
            layer_output = results[3]
        else:
            hidden, normed = results[3:]

    grad = cotangent[0]
    pending = None
    sums = [None] * LAYERS
    for layer in reversed(range(LAYERS)):
        hidden, groups, heads, lows, attended, mixed, factor, middle, inner, low = kept[layer]
        gain = mlp_gain[layer][None]
        results = feed_back(
            meta, gain, grad, middle, inner, side_weights[layer], parts, seq_count, pending
        )
        results = fence(*results)
        grad_in = grad if pending is None else results[5 + parts]
        grad, gi, gm, dl, il = results[:5]
        mixed_grads = [to_heads(results[5])]
        side_sum = feed_sums(gain, grad_in, middle, inner, gi, gm, dl, il, low, mixed)
        mixed_grads, side_sum = fence(mixed_grads, side_sum)
        side_total = reduce_rows(side_sum)
        factor_row = jnp.pad(factor, (0, 128 - HD)).reshape(1, 128)
        head_grads = []
        for p in range(parts):
            if p < parts - 1:
                mixed_grads.append(to_heads(after(results[6 + p], side_sum)))
            head_grads.append(
                attend_back(meta, factor_row, attended[p][1], attended[p][0], mixed_grads[p])
            )
            if p == parts - 1 and layer < LAYERS - 1 and paired:
                whole = sum_over_seq(jnp.stack(sums[layer + 1]), seq_count)
                head_grads, mixed_grads, whole = fence(head_grads, mixed_grads, whole)
                sums[layer + 1] = (whole[0], whole[1])
            else:
                head_grads, mixed_grads = fence(head_grads, mixed_grads)
        if paired:
            own, far = groups
            far_back = project_back(
                meta, head_grads, head_weights[layer], far[1], 2, rows, "far"
            )
            far_sum = (
                far_back[0].astype(F32) + swap(far_back[1], "seq", seq_count, 1).astype(F32)
            ).astype(BF)
            far_sum, head_grads, side_total = fence(far_sum, head_grads, side_total)
            cut = rows * (3 if layer > 0 else 2) // 5
            crossed = swap(far_sum[:cut], "seq", seq_count, 2)
            head_sum, lora_own = project_sums(
                meta, head_grads, lows, far_back[2], [g[0] for g in groups], head_weights[layer]
            )
            if layer == 0:
                side_total = sum_over_seq(side_total, seq_count)
            head_sum, lora_own, crossed, head_grads, rest, side_total = fence(
                head_sum, lora_own, crossed, head_grads, far_sum[cut:], side_total
            )
            if layer > 0:
                head_total = reduce_rows(head_sum)
            else:
                head_total = reduce_quarter(head_sum, core, chip, seq_count, fsdp_count)
            if layer > 0:
                rest = swap(rest, "seq", seq_count, 2)
            own_back = project_back(
                meta, head_grads, head_weights[layer], own[1], 2, rows, "own", lora_own
            )
            if layer > 0:
                own_back, rest = fence(own_back, rest)
            else:
                own_back, head_total, rest = fence(own_back, head_total, rest)
                rest = swap(rest, "seq", seq_count, 2)
                head_total = owned(head_total)
                head_total, rest = fence(head_total, rest)
            near = swap(own_back[1], "seq", seq_count, 1)
            sums[layer] = (side_total, head_total)
            terms = [own_back[0], near, crossed, rest]
        else:
            back = project_back(
                meta, head_grads, head_weights[layer], place * 0, 1, GLEN, "all"
            )
            terms = [lax.psum_scatter(back[0], "seq", scatter_dimension=0, tiled=True)]
            head_sum = project_sums(
                meta, head_grads, lows, back[1], [g[0] for g in groups], head_weights[layer]
            )[0]
            sums[layer] = tuple(lax.psum(v, "seq") for v in (side_total, reduce_rows(head_sum)))
        if layer > 0 and paired:
            pending = (attn_gain[layer][None], hidden, terms)
        else:
            grad = norm_back(attn_gain[layer][None], grad, hidden, terms)
            if paired:
                head_total = joined(jnp.sum(head_total.astype(F32), axis=0).astype(BF), chip, seq_count, 2)
                grad, head_total = fence(grad, head_total)
                sums[0] = (sums[0][0], joined(head_total, core, seq_count, 1))

    side = jnp.stack([s[0] for s in sums]).astype(F32)
    head = jnp.stack([s[1] for s in sums]).astype(F32)

    def columns(slot):
        return side[:, :, slot * AR : (slot + 1) * AR]

    return (
        layer_output[None],
        grad[None],
        head[:, :, : 3 * AR],
        head[:, :, 3 * AR :].reshape(LAYERS, shard, 3, AR).transpose(0, 2, 3, 1),
        columns(0),
        columns(1).transpose(0, 2, 1),
        columns(2),
        columns(3).transpose(0, 2, 1),
        columns(4),
        columns(5).transpose(0, 2, 1),
    )


def solution(mesh):
    rows = P("fsdp", "seq", None)
    first = P(None, "fsdp", None)
    second = P(None, None, "fsdp")
    return jax.shard_map(
        partial(local, seq_count=mesh.shape["seq"], fsdp_count=mesh.shape["fsdp"]),
        mesh=mesh,
        in_specs=(
            rows,
            P("fsdp", None),
            P("fsdp", None),
            P(),
            P(),
            P(),
            first,
            first,
            first,
            first,
            first,
            P(None, None, None, "fsdp"),
            first,
            second,
            first,
            second,
            first,
            second,
            rows,
        ),
        out_specs=(
            rows,
            rows,
            first,
            P(None, None, None, "fsdp"),
            first,
            second,
            first,
            second,
            first,
            second,
        ),
        check_vma=False,
    )
```

```python
from functools import partial
import math

import jax
import jax.numpy as jnp
from jax import lax
from jax.experimental import pallas as pl
from jax.experimental.pallas import tpu as pltpu
from jax.sharding import PartitionSpec as P

D = 1280
HEADS = 16
HD = 80
R = 16
LAYERS = 2
PROMPT = 2048
AR = 128
GLEN = 2560
LOG2E = 1.4426950408889634
LN2 = 0.6931471805599453
ROFF = 8
NEG = -1e30
BLOCK = 256
KEYS = 512
CHUNK = 1024
WIDE = D + AR
PART = D + 2 * AR
SIDE = 3 * PART
BF = jnp.bfloat16
F32 = jnp.float32
NN = (((1,), (0,)), ((), ()))
NT = (((1,), (1,)), ((), ()))
VMEM = pl.BlockSpec(memory_space=pltpu.VMEM)
SMEM = pl.BlockSpec(memory_space=pltpu.SMEM)
HBM = pl.BlockSpec(memory_space=pl.ANY)


def dot(left, right, dims=NN):
    return lax.dot_general(left, right, dims, preferred_element_type=F32)


def call(kernel, name, outs, specs, scratch, expected, out_specs=None):
    return pl.pallas_call(
        kernel,
        out_shape=outs,
        in_specs=specs,
        out_specs=tuple(VMEM for _ in outs) if out_specs is None else out_specs,
        scratch_shapes=scratch,
        compiler_params=pltpu.CompilerParams(vmem_limit_bytes=60 << 20),
        cost_estimate=pl.CostEstimate(
            flops=int(expected * 1.15e9), bytes_accessed=1024, transcendentals=0
        ),
        name=name,
    )


def shape(dims, kind=BF):
    return jax.ShapeDtypeStruct(dims, kind)


def sigmoid(v):
    return 1.0 / (1.0 + jnp.exp(-v))


def row_mask(meta, base, count):
    rows = lax.broadcasted_iota(jnp.int32, (count, AR), 0) + base
    lane = lax.broadcasted_iota(jnp.int32, (count, AR), 1)
    chosen = jnp.where(rows < PROMPT, meta[0], jnp.where(rows < meta[3], meta[1], meta[2]))
    low = chosen * R
    return jnp.where((lane >= low) & (lane < low + R), 1.0, 0.0).astype(F32)


def columns_of(ref, at, width):
    return ref if width == ref.shape[1] else ref.at[:, pl.ds(at, width)]


def head_copies(meta, pieces, wq_s, cb_s, sems):
    core, both = meta[5], 3 * AR
    n = len(pieces) // 2
    single = n == 1 and pieces[0].shape[0] == 1
    copies, block_at = [], 0
    for own, other in zip(pieces[:n], pieces[n:]):
        blocks, rows, columns = own.shape
        for block in range(blocks):
            at = 0 if single else pl.multiple_of(meta[ROFF + block_at], math.gcd(rows, 256))
            into = pl.ds(at, rows)
            for source, target in (
                (own.at[block, :, :both], cb_s.at[into, pl.ds(pl.multiple_of(core * both, both), both)]),
                (other.at[block], cb_s.at[into, pl.ds(pl.multiple_of((1 - core) * both, both), both)]),
                (own.at[block, :, both:], None if wq_s is None else wq_s.at[into]),
            ):
                if target is not None:
                    copies.append(pltpu.make_async_copy(source, target, sems.at[len(copies)]))
            block_at += 1
    return copies


def side_copies(meta, own, other, which, r_s, sems):
    half = PART // 2
    return [
        pltpu.make_async_copy(
            columns_of(ref, which * half, half),
            columns_of(r_s, pl.multiple_of(which * PART + side * half, half), half),
            sems.at[which, k],
        )
        for k, (ref, side) in enumerate(((own, meta[5]), (other, 1 - meta[5])))
    ]


def start_all(copies):
    for copy in copies:
        copy.start()
    return copies


def wait_all(copies):
    for copy in copies:
        copy.wait()


def run_copies(copies):
    wait_all(start_all(copies))


def fill_second(meta, cb_s, bd_s, width, group):
    bd_s[...] = jnp.zeros_like(bd_s)
    for p in range(width // group):
        start = pl.multiple_of(meta[4] * width + p * group, math.gcd(group, 256))
        for c in range(3):
            at = (p * 3 + c) * group
            bd_s[at : at + group, c * AR : (c + 1) * AR] = cb_s[
                pl.ds(start, group), (3 + c) * AR : (4 + c) * AR
            ]


def project_kernel(*refs, arrays, pieces, parts, block):
    meta, scale = refs[:2]
    tokens = refs[2 : 2 + arrays]
    weights = refs[2 + arrays : 2 + arrays + pieces]
    heads = refs[2 + arrays + pieces : 2 + arrays + pieces + parts]
    low_out, wq_s, cb_s, bd_s, sems = refs[2 + arrays + pieces + parts :]
    run_copies(head_copies(meta, weights, wq_s, cb_s, sems))
    columns = wq_s.shape[1]
    each = columns // parts
    fill_second(meta, cb_s, bd_s, columns // 3, each // 3)
    for k in range(arrays):
        rows = tokens[k].shape[0]
        local = 0 if arrays == 1 else (meta[5] if k == 0 else 1 - meta[5]) * rows

        def step(i, carry, k=k, local=local):
            x = tokens[k][pl.ds(pl.multiple_of(i * block, 64), block), :]
            place = pl.multiple_of(local + i * block, 64)
            mask = row_mask(meta, meta[7] + place, block)
            low = dot(x, cb_s[:, : 3 * AR]) * jnp.concatenate([mask] * 3, axis=1)
            low = low.astype(BF)
            low_out[pl.ds(place, block), :] = low
            both = ((dot(x, wq_s[...]) + dot(low, bd_s[...], NT)) * scale[...]).astype(BF)
            for p in range(parts):
                heads[p][pl.ds(place, block), :] = both[:, p * each : (p + 1) * each]
            return carry

        lax.fori_loop(0, rows // block, step, 0)


def project(meta, scale, tokens, weights, base, parts):
    arrays = len(tokens)
    rows = tokens[0].shape[0]
    count = rows * arrays
    columns = scale.shape[1]
    return call(
        partial(
            project_kernel, arrays=arrays, pieces=len(weights), parts=parts, block=320
        ),
        "project",
        (shape((count, columns // parts)),) * parts + (shape((count, 3 * AR)),),
        [SMEM, VMEM] + [VMEM] * arrays + [HBM] * len(weights),
        [
            pltpu.VMEM((D, columns), BF),
            pltpu.VMEM((D, 6 * AR), BF),
            pltpu.VMEM((columns, 3 * AR), BF),
            pltpu.SemaphoreType.DMA((3 * sum(w.shape[0] for w in weights),)),
        ],
        13,
    )(meta.at[7].set(base), scale, *tokens, *weights)


def load_rows(meta, sources, target, sems):
    copies = []
    for index, ref in enumerate(sources):
        rows = ref.shape[0]
        if len(sources) == 1:
            into = target
        else:
            into = target.at[pl.ds(pl.multiple_of(meta[6] * rows if index == 0 else (1 - meta[6]) * rows, 256), rows)]
        copies.append(pltpu.make_async_copy(ref, into, sems.at[index]))
    run_copies(copies)


def allowed_pairs(meta, queries, keys, query_at, key_at):
    same = (keys >= meta[3]) | (queries < meta[3])
    causal = keys <= queries
    return causal & same if key_at >= PROMPT else causal


def three_parts(x):
    high = x.astype(BF).astype(F32)
    rest = x - high
    middle = rest.astype(BF).astype(F32)
    return high, middle, (rest - middle).astype(BF).astype(F32)


def with_parts(base, place, value):
    a, b, c = three_parts(value)
    return jnp.where(place == 0, a, jnp.where(place == 1, b, jnp.where(place == 2, c, base)))


def attend_kernel(*refs, groups, local_heads):
    meta = refs[0]
    sources = refs[1 : 1 + groups]
    out, saved, hs, q_s, k_s, v_s, sems, out_sems = refs[1 + groups :]
    load_rows(meta, sources, hs, sems)
    width = local_heads * HD
    span = out.shape[2]
    lane = lax.broadcasted_iota(jnp.int32, (BLOCK, 128), 1)
    for h in range(local_heads):
        for i in range(GLEN // BLOCK):
            r = slice(i * BLOCK, (i + 1) * BLOCK)
            for c, ref in ((0, q_s), (1, k_s), (2, v_s)):
                x = hs[r, c * width + h * HD : c * width + (h + 1) * HD]
                fill = jnp.ones if c > 0 else jnp.zeros
                ref[h, r, :] = jnp.concatenate([x, fill((BLOCK, 128 - HD), BF)], axis=1)
    stores = [
        pltpu.make_async_copy(ref, saved.at[c], out_sems.at[c])
        for c, ref in ((0, q_s), (1, k_s), (2, v_s))
    ]
    stores[1].start()
    stores[2].start()

    def head(h, carry):
        place = pl.multiple_of(h * HD, 16)
        for i in range(GLEN // BLOCK):
            q0 = i * BLOCK
            nk = q0 + BLOCK
            d0 = min(q0, PROMPT)
            rows = lax.broadcasted_iota(jnp.int32, (BLOCK, nk - d0), 0) + q0
            cols = lax.broadcasted_iota(jnp.int32, (BLOCK, nk - d0), 1) + d0
            qb = q_s[h, q0 : q0 + BLOCK, :]
            sd = jnp.where(
                allowed_pairs(meta, rows, cols, q0, d0), dot(qb, k_s[h, d0:nk, :], NT), NEG
            )
            peak = jnp.max(sd, axis=1, keepdims=True)
            if d0 > 0:
                sp = dot(qb, k_s[h, 0:d0, :], NT)
                peak = jnp.maximum(peak, jnp.max(sp, axis=1, keepdims=True))
            total = dot(jnp.exp2(sd - peak).astype(BF), v_s[h, d0:nk, :])
            if d0 > 0:
                total = total + dot(jnp.exp2(sp - peak).astype(BF), v_s[h, 0:d0, :])
            lse = peak + jnp.log2(total[:, HD : HD + 1])
            q_s[h, q0 : q0 + BLOCK, :] = with_parts(qb.astype(F32), lane - HD, -lse).astype(BF)
            turned = total.T
            result = (turned[:HD, :] * (1.0 / turned[HD : HD + 1, :])).astype(BF)
            for part in range(BLOCK // 128):
                t = q0 + part * 128
                out[t // span, pl.ds(place, HD), t % span : t % span + 128] = result[
                    :, part * 128 : (part + 1) * 128
                ]
        return carry

    lax.fori_loop(0, local_heads, head, 0)
    stores[0].start()
    wait_all(stores)


def attend(meta, heads, span):
    width = heads[0].shape[1]
    local_heads = width // (3 * HD)
    return call(
        partial(attend_kernel, groups=len(heads), local_heads=local_heads),
        "attend",
        (shape((GLEN // span, local_heads * HD, span)), shape((3, local_heads, GLEN, 128))),
        [SMEM] + [HBM] * len(heads),
        [pltpu.VMEM((GLEN, width), BF)]
        + [pltpu.VMEM((local_heads, GLEN, 128), BF)] * 3
        + [pltpu.SemaphoreType.DMA((len(heads),)), pltpu.SemaphoreType.DMA((3,))],
        16,
        out_specs=(VMEM, HBM),
    )(meta, *heads)


def attend_back_kernel(meta, factor, saved, o_ref, do_ref, out, q_s, k_s, v_s, dt_s, kt_s, dqt_s, sems):
    local_heads = saved.shape[1]
    width = local_heads * HD
    span = o_ref.shape[2]
    loads = [
        start_all(
            [
                pltpu.make_async_copy(saved.at[c, h], ref.at[h], sems.at[c, h])
                for c, ref in ((0, q_s), (1, k_s), (2, v_s))
            ]
        )
        for h in range(local_heads)
    ]
    extra = lax.broadcasted_iota(jnp.int32, (128 - HD, 128), 0)
    for h in range(local_heads):
        cs = slice(h * HD, (h + 1) * HD)
        for i in range(GLEN // 128):
            t, inner = (i * 128) // span, slice((i * 128) % span, (i * 128) % span + 128)
            do = do_ref[t, cs, inner]
            delta = jnp.sum(do.astype(F32) * o_ref[t, cs, inner].astype(F32), axis=0, keepdims=True)
            dt_s[h, :HD, i * 128 : (i + 1) * 128] = do
            dt_s[h, HD:, i * 128 : (i + 1) * 128] = with_parts(0.0, extra, -delta).astype(BF)
    for h in range(local_heads):
        wait_all(loads[h])
        for i in range(GLEN // KEYS):
            kt_s[:, i * KEYS : (i + 1) * KEYS] = k_s[h, i * KEYS : (i + 1) * KEYS, :].T
        for j in range(GLEN // KEYS):
            k0 = j * KEYS
            kb = k_s[h, k0 : k0 + KEYS, :]
            vb = v_s[h, k0 : k0 + KEYS, :]
            dk = jnp.zeros((KEYS, 128), F32)
            dv = jnp.zeros((KEYS, 128), F32)
            q0 = k0
            while q0 < GLEN:
                n = KEYS if q0 == k0 else min(CHUNK, GLEN - q0)
                qs = slice(q0, q0 + n)
                probs = jnp.exp2(dot(kb, q_s[h, qs, :], NT))
                if q0 == k0 or k0 >= PROMPT:
                    keys = lax.broadcasted_iota(jnp.int32, (KEYS, n), 0) + k0
                    queries = lax.broadcasted_iota(jnp.int32, (KEYS, n), 1) + q0
                    probs = jnp.where(allowed_pairs(meta, queries, keys, q0, k0), probs, 0.0)
                dscore = (probs * dot(vb, dt_s[h, :, qs])).astype(BF)
                dv = dv + dot(probs.astype(BF), dt_s[h, :, qs], NT)
                dk = dk + dot(dscore, q_s[h, qs, :])
                dq = dot(kt_s[:, k0 : k0 + KEYS], dscore)
                if j == 0:
                    dqt_s[:, qs] = dq
                else:
                    dqt_s[:, qs] += dq
                q0 += n
            r = slice(k0, k0 + KEYS)
            out[r, width + h * HD : width + (h + 1) * HD] = (dk[:, :HD] * LN2).astype(BF)
            out[r, 2 * width + h * HD : 2 * width + (h + 1) * HD] = dv[:, :HD].astype(BF)
            out[r, h * HD : (h + 1) * HD] = (dqt_s[:, r].T * factor[...]).astype(BF)[:, :HD]


def attend_back(meta, factor, saved, mixed, grad_mixed):
    local_heads = saved.shape[1]
    rows = pltpu.VMEM((local_heads, GLEN, 128), BF)
    return call(
        attend_back_kernel,
        "attend_back",
        (shape((GLEN, 3 * local_heads * HD)),),
        [SMEM, VMEM, HBM] + [VMEM] * 2,
        [rows] * 3
        + [
            pltpu.VMEM((local_heads, 128, GLEN), BF),
            pltpu.VMEM((128, GLEN), BF),
            pltpu.VMEM((128, GLEN), F32),
            pltpu.SemaphoreType.DMA((3, local_heads)),
        ],
        0.05,
    )(meta, factor, saved, mixed, grad_mixed)[0]


def rms_of(value):
    return lax.rsqrt(jnp.mean(value * value, axis=-1, keepdims=True) + 1e-06)


def feed_kernel(*refs, parts, pieces, block, last):
    meta, gain_mlp, gain_next, hidden_in = refs[:4]
    mixed = refs[4 : 4 + parts]
    weights = refs[4 + parts : 4 + parts + pieces]
    refs = refs[4 + parts + pieces :]
    middle_out, inner_out, low_out, result = refs[:4]
    normed_out = None if last else refs[4]
    hidden, middle_s, inner_s, r_s, mt_s, mx_s, sems, io_sems = refs[4 if last else 5 :]
    rows = hidden.shape[0]
    loads, slot = [], 0
    for p in range(parts):
        sources, group, _ = mixed[p].shape
        for source in range(sources):
            at = (source * parts + p) * group
            loads.append(
                pltpu.make_async_copy(
                    mixed[p].at[source], mt_s.at[at : at + group], io_sems.at[len(loads)]
                )
            )
    start_all(loads)
    load_hidden = pltpu.make_async_copy(hidden_in, hidden, io_sems.at[len(loads)])
    load_hidden.start()
    copies = [start_all(side_copies(meta, *weights, which, r_s, sems)) for which in range(3)]
    wait_all(loads)
    for i in range(0, rows, 128):
        n = min(128, rows - i)
        mx_s[i : i + n, :] = mt_s[:, i : i + n].T
    load_hidden.wait()

    def stage(which, body):
        wait_all(copies[which])

        def step(i, carry):
            r = pl.ds(pl.multiple_of(i * block, 64), block)
            mask = row_mask(meta, meta[4] * rows + i * block, block)

            def adapted(x):
                both = dot(x, r_s[:, which * PART : which * PART + WIDE])
                low = (both[:, D:] * mask).astype(BF)
                low_out[r, which * AR : (which + 1) * AR] = low
                return both[:, :D] + dot(low, r_s[:, which * PART + WIDE : (which + 1) * PART], NT)

            body(r, adapted)
            return carry

        lax.fori_loop(0, rows // block, step, 0)

    def out_stage(r, adapted):
        middle_s[r, :] = hidden[r, :] + adapted(mx_s[r, :])

    def in_stage(r, adapted):
        middle = middle_s[r, :]
        inner_s[r, :] = adapted((middle * rms_of(middle) * gain_mlp[...]).astype(BF))

    def down_stage(r, adapted):
        inner = inner_s[r, :]
        value = middle_s[r, :] + adapted((inner * sigmoid(inner)).astype(BF))
        result[r, :] = value.astype(result.dtype)
        if not last:
            normed_out[r, :] = (value * rms_of(value) * gain_next[...]).astype(BF)

    stage(0, out_stage)
    store_middle = pltpu.make_async_copy(middle_s, middle_out, io_sems.at[len(loads) + 1])
    store_middle.start()
    stage(1, in_stage)
    store_inner = pltpu.make_async_copy(inner_s, inner_out, io_sems.at[len(loads) + 2])
    store_inner.start()
    stage(2, down_stage)
    store_middle.wait()
    store_inner.wait()


def feed(meta, gain_mlp, gain_next, mixed, hidden, weights, last):
    rows = hidden.shape[0]
    row = pltpu.VMEM((rows, D), F32)
    outs = (shape((rows, D), F32), shape((rows, D), F32), shape((rows, 3 * AR)))
    outs += (shape((rows, D), BF),) if last else (shape((rows, D), F32), shape((rows, D), BF))
    return call(
        partial(
            feed_kernel,
            parts=len(mixed),
            pieces=2,
            block=math.gcd(rows, 320),
            last=last,
        ),
        "feed",
        outs,
        [SMEM] + [VMEM] * 2 + [HBM] * (1 + len(mixed) + 2),
        [
            row,
            row,
            row,
            pltpu.VMEM((D, SIDE), BF),
            pltpu.VMEM((D, rows), BF),
            pltpu.VMEM((rows, D), BF),
            pltpu.SemaphoreType.DMA((3, 2)),
            pltpu.SemaphoreType.DMA((sum(m.shape[0] for m in mixed) + 3,)),
        ],
        17,
        out_specs=(HBM, HBM) + (VMEM,) * (len(outs) - 2),
    )(meta, gain_mlp, gain_next, hidden, *mixed, *weights)


def rms_back(grad, value, gain, grad_normed):
    r = rms_of(value)
    e = gain * grad_normed
    return grad + r * e - value * (r * r * r) * jnp.mean(value * e, axis=-1, keepdims=True)


def feed_back_kernel(*refs, parts, pieces, block, terms):
    meta, gain_mlp, grad_hbm, middle_hbm, inner_hbm = refs[:5]
    weights = refs[5 : 5 + pieces]
    refs = refs[5 + pieces :]
    if terms:
        gain_next, hidden_hbm, term_hbm = refs[0], refs[1], refs[2 : 2 + terms]
        refs = refs[2 + terms :]
    grad_out, gi_s, gm_s, dl_s, il_s = refs[:5]
    mixed_grad = refs[5 : 5 + parts]
    refs = refs[5 + parts :]
    if terms:
        gl_out, refs = refs[0], refs[1:]
    grad_in, middle_s, inner_s, r_s, sems, io_sems = refs[:6]
    rows = grad_in.shape[0]
    early = []
    if terms:
        hidden_s, term_s, term_sems = refs[6], refs[7 : 7 + terms - 1], refs[7 + terms - 1]
        early.append(pltpu.make_async_copy(hidden_hbm, hidden_s, term_sems.at[terms]))
        for k in range(terms - 2):
            early.append(pltpu.make_async_copy(term_hbm[k], term_s[k], term_sems.at[k]))
        cut = term_hbm[-2].shape[0]
        early.append(
            pltpu.make_async_copy(term_hbm[-2], term_s[-1].at[:cut], term_sems.at[terms - 2])
        )
        early.append(
            pltpu.make_async_copy(term_hbm[-1], term_s[-1].at[cut:], term_sems.at[terms - 1])
        )
        start_all(early)
    loads = start_all(
        [
            pltpu.make_async_copy(source, target, io_sems.at[k])
            for k, (source, target) in enumerate(
                ((grad_hbm, grad_in), (inner_hbm, inner_s), (middle_hbm, middle_s))
            )
        ]
    )
    copies = {which: start_all(side_copies(meta, *weights, which, r_s, sems)) for which in (2, 1, 0)}

    def rows_of(i):
        return pl.ds(pl.multiple_of(i * block, 64), block)

    def narrow(g, which, i):
        mask = row_mask(meta, meta[4] * rows + i * block, block)
        return (dot(g, r_s[:, which * PART + WIDE : (which + 1) * PART]) * mask).astype(BF)

    def across(g, low, which):
        both = jnp.concatenate([g, low], axis=1)
        return dot(both, r_s[:, which * PART : which * PART + WIDE], NT)

    def down_stage(i, carry):
        r = rows_of(i)
        gl = grad_in[r, :].astype(BF)
        dl = narrow(gl, 2, i)
        dl_s[r, :] = dl
        inner = inner_s[r, :]
        s = sigmoid(inner)
        gi_s[r, :] = (across(gl, dl, 2) * (s * (1.0 + inner * (1.0 - s)))).astype(BF)
        return carry

    def in_stage(i, carry):
        r = rows_of(i)
        gi = gi_s[r, :]
        il = narrow(gi, 1, i)
        il_s[r, :] = il
        grad = rms_back(grad_in[r, :].astype(F32), middle_s[r, :], gain_mlp[...], across(gi, il, 1))
        grad_out[r, :] = grad
        gm_s[r, :D] = grad.astype(BF)
        return carry

    def out_stage(i, carry):
        r = rows_of(i)
        gm_s[r, D:] = narrow(gm_s[r, :D], 0, i)
        return carry

    loads[0].wait()
    if terms:
        wait_all(early)

        def norm_stage(i, carry):
            r = rows_of(i)
            total = term_s[0][r, :].astype(F32)
            for ref in term_s[1:]:
                total = total + ref[r, :].astype(F32)
            grad = rms_back(grad_in[r, :], hidden_s[r, :], gain_next[...], total)
            grad_in[r, :] = grad
            gl_out[r, :] = grad.astype(BF)
            return carry

        lax.fori_loop(0, rows // block, norm_stage, 0)
    wait_all(copies[2])
    loads[1].wait()
    lax.fori_loop(0, rows // block, down_stage, 0)
    wait_all(copies[1])
    loads[2].wait()
    lax.fori_loop(0, rows // block, in_stage, 0)
    wait_all(copies[0])
    lax.fori_loop(0, rows // block, out_stage, 0)
    sources, group, _ = mixed_grad[0].shape
    for source in range(sources):
        for p in range(parts):
            at = (source * parts + p) * group
            mixed_grad[p][source] = dot(r_s[at : at + group, :WIDE], gm_s[...], NT).astype(BF)


def feed_back(meta, gain_mlp, grad, middle, inner, weights, parts, sources, norm=None):
    rows = grad.shape[0]
    narrow = shape((rows, AR))
    return call(
        partial(
            feed_back_kernel,
            parts=parts,
            pieces=2,
            block=math.gcd(rows, 320),
            terms=0 if norm is None else len(norm[2]),
        ),
        "feed_back",
        (shape((rows, D), F32), shape((rows, D)), shape((rows, WIDE)), narrow, narrow)
        + (shape((sources, D // sources // parts, rows)),) * parts
        + (() if norm is None else (shape((rows, D)),)),
        [SMEM, VMEM]
        + [HBM] * (3 + 2)
        + ([] if norm is None else [VMEM] + [HBM] * (1 + len(norm[2]))),
        [
            pltpu.VMEM((rows, D), grad.dtype),
            pltpu.VMEM((rows, D), F32),
            pltpu.VMEM((rows, D), F32),
            pltpu.VMEM((D, SIDE), BF),
            pltpu.SemaphoreType.DMA((3, 2)),
            pltpu.SemaphoreType.DMA((3,)),
        ]
        + (
            []
            if norm is None
            else [pltpu.VMEM((rows, D), F32)]
            + [pltpu.VMEM((rows, D), BF)] * (len(norm[2]) - 1)
            + [pltpu.SemaphoreType.DMA((len(norm[2]) + 1,))]
        ),
        0.05,
    )(
        meta,
        gain_mlp,
        grad,
        middle,
        inner,
        *weights,
        *(() if norm is None else (norm[0], norm[1], *norm[2])),
    )


def feed_sums_kernel(*refs, parts):
    gain_mlp, grad, middle_ref, inner_ref, gi, gm, dl, il, low = refs[:9]
    mixed = refs[9 : 9 + parts]
    sums = refs[9 + parts]
    for p in range(parts):
        sources, group, _ = mixed[p].shape
        for source in range(sources):
            at = (source * parts + p) * group
            sums[at : at + group, :AR] = dot(mixed[p][source], gm[:, D:]).astype(BF)
    inner = inner_ref[...]
    act = (inner * sigmoid(inner)).astype(BF)
    middle = middle_ref[...]
    nf = (middle * rms_of(middle) * gain_mlp[...]).astype(BF)
    pairs = (
        (1, low[:, :AR], gm[:, :D]),
        (2, il[...], nf),
        (3, low[:, AR : 2 * AR], gi[...]),
        (4, dl[...], act),
        (5, low[:, 2 * AR :], grad[...].astype(BF)),
    )
    for slot, few, wide in pairs:
        turned = few.T
        for i in range(0, D, BLOCK):
            part = dot(turned, wide[:, i : i + BLOCK])
            sums[i : i + BLOCK, slot * AR : (slot + 1) * AR] = part.T.astype(BF)


def feed_sums(gain_mlp, grad, middle, inner, gi, gm, dl, il, low, mixed):
    return call(
        partial(feed_sums_kernel, parts=len(mixed)),
        "feed_sums",
        (shape((D, 6 * AR)),),
        [VMEM] * (9 + len(mixed)),
        [],
        0.05,
    )(gain_mlp, grad, middle, inner, gi, gm, dl, il, low, *mixed)[0]


def norm_back_kernel(gain, grad, hidden, *refs, cut):
    total = refs[0][...].astype(F32)
    out = refs[-1]
    for ref in refs[1 : -3 if cut else -1]:
        total = total + ref[...].astype(F32)
    if cut:
        first = pl.program_id(0) < cut
        total = total + jnp.where(first, refs[-3][...], refs[-2][...]).astype(F32)
    out[...] = rms_back(grad[...], hidden[...], gain[...], total)


def norm_back(gain, grad, hidden, terms):
    rows = grad.shape[0]
    block = math.gcd(rows, 128)
    cut = terms[-2].shape[0] // block if terms[-1].shape[0] < rows else 0
    row = pl.BlockSpec((block, D), lambda i: (i, 0))
    specs = [row] * (2 + len(terms))
    if cut:
        specs[-2] = pl.BlockSpec((block, D), lambda i: (jnp.minimum(i, cut - 1), 0))
        specs[-1] = pl.BlockSpec((block, D), lambda i: (jnp.maximum(i - cut, 0), 0))
    return pl.pallas_call(
        partial(norm_back_kernel, cut=cut),
        grid=(rows // block,),
        out_shape=shape((rows, D), F32),
        in_specs=[pl.BlockSpec((1, D), lambda i: (0, 0))] + specs,
        out_specs=row,
        cost_estimate=pl.CostEstimate(flops=int(5e7), bytes_accessed=1024, transcendentals=0),
        name="norm_back",
    )(gain, grad, hidden, *terms)


def project_back_kernel(*refs, arrays, pieces, parts, block, mode):
    meta = refs[0]
    grads = refs[1 : 1 + parts]
    weights = refs[1 + parts : 1 + parts + pieces]
    refs = refs[1 + parts + pieces :]
    if mode == "own":
        lora_in, refs = refs[0], refs[1:]
    outs, refs = refs[:arrays], refs[arrays:]
    if mode != "own":
        lora_out, refs = refs[0], refs[1:]
    wq_s, cb_s, bd_s = refs[:3]
    g_s = refs[3 : 3 + parts]
    sems, row_sems = refs[3 + parts :]
    count = g_s[0].shape[0]
    rows_at = pl.ds(pl.multiple_of(meta[7], 256), count)
    loads = start_all(
        [
            pltpu.make_async_copy(
                grads[p] if count == GLEN else grads[p].at[rows_at], g_s[p], row_sems.at[p]
            )
            for p in range(parts)
        ]
    )
    copies = start_all(head_copies(meta, weights, wq_s, cb_s, sems))
    wait_all(copies)
    wait_all(loads)
    columns = wq_s.shape[1]
    each = columns // parts
    fill_second(meta, cb_s, bd_s, columns // 3, each // 3)

    def rows_of(place):
        at = pl.ds(pl.multiple_of(place, 64), block)
        return jnp.concatenate([g_s[p][at, :] for p in range(parts)], axis=1)

    def narrow(g, place):
        mask = row_mask(meta, meta[7] + place, block)
        return (dot(g, bd_s[...]) * jnp.concatenate([mask] * 3, axis=1)).astype(BF)

    for k in range(arrays):
        rows = outs[k].shape[0]
        local = 0 if arrays == 1 else (meta[5] if k == 0 else 1 - meta[5]) * rows

        def step(i, carry, k=k, local=local):
            place = pl.multiple_of(local + i * block, 64)
            g = rows_of(place)
            if mode == "own":
                lora = lora_in[pl.ds(place, block), :]
            else:
                lora = narrow(g, place)
                lora_out[pl.ds(place, block), :] = lora
            outs[k][pl.ds(pl.multiple_of(i * block, 64), block), :] = (
                dot(g, wq_s[...], NT) + dot(lora, cb_s[:, : 3 * AR], NT)
            ).astype(BF)
            return carry

        lax.fori_loop(0, rows // block, step, 0)


def project_back(meta, grads, weights, base, arrays, rows, mode, lora=None):
    columns = sum(g.shape[1] for g in grads)
    count = rows * arrays
    low = (shape((count, 3 * AR)),)
    return call(
        partial(
            project_back_kernel,
            arrays=arrays,
            pieces=len(weights),
            parts=len(grads),
            block=320,
            mode=mode,
        ),
        "project_back",
        tuple(shape((rows, D)) for _ in range(arrays)) + low * (mode != "own"),
        [SMEM] + [HBM] * (len(grads) + len(weights)) + [VMEM] * (mode == "own"),
        [
            pltpu.VMEM((D, columns), BF),
            pltpu.VMEM((D, 6 * AR), BF),
            pltpu.VMEM((columns, 3 * AR), BF),
        ]
        + [pltpu.VMEM((count, g.shape[1]), BF) for g in grads]
        + [
            pltpu.SemaphoreType.DMA((3 * sum(w.shape[0] for w in weights),)),
            pltpu.SemaphoreType.DMA((len(grads),)),
        ],
        0.05,
    )(meta.at[7].set(base), *grads, *weights, *(() if lora is None else (lora,)))


def project_sums_kernel(*refs, parts, groups, arrays, block):
    meta = refs[0]
    grads, refs = refs[1 : 1 + parts], refs[1 + parts :]
    lows, refs = refs[:groups], refs[groups:]
    lora_far, refs = refs[0], refs[1:]
    tokens, refs = refs[: groups * arrays], refs[groups * arrays :]
    if groups == 1:
        loras = [lora_far]
        sums, turned = refs
    else:
        weights, refs = refs[:2], refs[2:]
        sums, lora_own, turned, cb_s, bd_s, sems = refs
        loras = [lora_own, lora_far]
        run_copies(head_copies(meta, weights, None, cb_s, sems))
        each = grads[0].shape[1]
        fill_second(meta, cb_s, bd_s, each * parts // 3, each // 3)
        count = lora_own.shape[0]

        def step(i, carry):
            place = pl.multiple_of(i * block, 64)
            at = pl.multiple_of(meta[6] * count + place, 64)
            g = jnp.concatenate([ref[pl.ds(at, block), :] for ref in grads], axis=1)
            mask = row_mask(meta, at, block)
            lora_own[pl.ds(place, block), :] = (
                dot(g, bd_s[...]) * jnp.concatenate([mask] * 3, axis=1)
            ).astype(BF)
            return carry

        lax.fori_loop(0, count // block, step, 0)
    sections = []
    for index in range(groups):
        for k in range(arrays):
            ref = tokens[index * arrays + k]
            rows = ref.shape[0]
            at = 0 if arrays == 1 else (meta[5] if k == 0 else 1 - meta[5]) * rows
            slot = index * arrays + k
            turned[slot] = loras[index][pl.ds(at if arrays == 1 else pl.multiple_of(at, 64), rows), :].T
            sections.append((slot, ref))
    for i in range(0, D, BLOCK):
        total = None
        for slot, ref in sections:
            piece = dot(turned[slot], ref[:, i : i + BLOCK])
            total = piece if total is None else total + piece
        sums[i : i + BLOCK, : 3 * AR] = total.T.astype(BF)
    sums[:, 3 * AR :] = jnp.zeros((D, 3 * AR), BF)
    each = grads[0].shape[1]
    group = each // 3
    for c in range(3):
        few = [low[:, c * AR : (c + 1) * AR].T for low in lows]
        for p in range(parts):
            total = None
            for index in range(groups):
                rows = lows[index].shape[0]
                if groups == 1:
                    at = pl.ds(0, rows)
                else:
                    chip = meta[6] if index == 0 else 1 - meta[6]
                    at = pl.ds(pl.multiple_of(chip * rows, 256), rows)
                piece = dot(few[index], grads[p][at, c * group : (c + 1) * group])
                total = piece if total is None else total + piece
            own = pl.multiple_of(meta[4] * group * parts + p * group, math.gcd(group, 256))
            sums[pl.ds(own, group), (3 + c) * AR : (4 + c) * AR] = total.T.astype(BF)


def project_sums(meta, grads, lows, lora_far, tokens, weights):
    flat = [t for arrays in tokens for t in arrays]
    rows = flat[0].shape[0]
    columns = sum(g.shape[1] for g in grads)
    outs = (shape((D, 6 * AR)),)
    scratch = [pltpu.VMEM((len(flat), 3 * AR, rows), BF)]
    if len(lows) > 1:
        outs += (shape(lows[0].shape),)
        scratch += [
            pltpu.VMEM((D, 6 * AR), BF),
            pltpu.VMEM((columns, 3 * AR), BF),
            pltpu.SemaphoreType.DMA((3,)),
        ]
    else:
        weights = ()
    return call(
        partial(
            project_sums_kernel,
            parts=len(grads),
            groups=len(lows),
            arrays=len(tokens[0]),
            block=320,
        ),
        "project_sums",
        outs,
        [SMEM] + [VMEM] * (len(grads) + len(lows) + 1 + len(flat)) + [HBM] * len(weights),
        scratch,
        0.05,
    )(meta, *grads, *lows, lora_far, *flat, *weights)


def swap(value, axis, count, step):
    return lax.ppermute(value, axis, [(i, i ^ step) for i in range(count)])


def fence(*values):
    return lax.optimization_barrier(values)


def after(value, *earlier):
    return lax.optimization_barrier((value, *earlier))[0]


def sum_over_seq(value, seq_count):
    for step in (1, 2):
        value = (value.astype(F32) + swap(value, "seq", seq_count, step).astype(F32)).astype(BF)
    return value


def reduce_quarter(value, core, chip, seq_count, fsdp_count):
    def halves(v, index, step):
        v = v.reshape(fsdp_count, 2, v.shape[1] // 2, v.shape[2])
        keep = jnp.where(index == 0, v[:, 0], v[:, 1])
        give = jnp.where(index == 0, v[:, 1], v[:, 0])
        return (keep.astype(F32) + swap(give, "seq", seq_count, step).astype(F32)).astype(BF)

    value = value.reshape(fsdp_count, value.shape[0] // fsdp_count, value.shape[1])
    return halves(halves(value, core, 1), chip, 2)


def owned(value):
    return lax.all_to_all(value, "fsdp", split_axis=0, concat_axis=0, tiled=True)


def joined(value, index, seq_count, step):
    far = swap(value, "seq", seq_count, step)
    return jnp.where(index == 0, jnp.concatenate([value, far]), jnp.concatenate([far, value]))


def reduce_rows(value):
    return lax.psum_scatter(value, "fsdp", scatter_dimension=0, tiled=True)


def local(
    tokens,
    cont_lengths,
    adapter_ids,
    attn_gain,
    mlp_gain,
    query_scale,
    w_qkv,
    output_weight,
    inward_weight,
    down_weight,
    projection_first_factor,
    b_qkv,
    output_first_factor,
    output_second_factor,
    inward_first_factor,
    inward_second_factor,
    down_first_factor,
    down_second_factor,
    cotangent,
    seq_count,
    fsdp_count,
):
    rows = tokens.shape[1]
    shard = w_qkv.shape[1]
    width = D // seq_count
    paired = seq_count == 4
    place = lax.axis_index("seq")
    core = place % 2
    chip = place // 2 if paired else place * 0
    span = rows if rows % 128 == 0 else GLEN
    meta = jnp.concatenate(
        [
            adapter_ids[0],
            PROMPT + cont_lengths[0, :1],
            jnp.stack([place, core, chip, place * 0]),
        ]
    ).astype(jnp.int32)

    parts = 2 if paired else 1
    group = width // parts

    def heads_part(layer):
        return jnp.concatenate(
            [
                lax.dynamic_slice(
                    w_qkv, (layer, 0, c * D + place * width + p * group), (1, shard, group)
                )[0]
                for p in range(parts)
                for c in range(3)
            ],
            axis=1,
        )

    def both_part(layer):
        turned = jnp.concatenate([b_qkv[layer, c].T for c in range(3)], axis=1)
        return jnp.where(core == 0, projection_first_factor[layer], turned)

    def side_part(layer):
        whole = jnp.concatenate(
            [
                output_weight[layer],
                output_first_factor[layer],
                output_second_factor[layer].T,
                inward_weight[layer],
                inward_first_factor[layer],
                inward_second_factor[layer].T,
                down_weight[layer],
                down_first_factor[layer],
                down_second_factor[layer].T,
            ],
            axis=1,
        )
        half = PART // 2
        return jnp.where(
            core == 0,
            jnp.concatenate([whole[:, k * PART : k * PART + half] for k in range(3)], axis=1),
            jnp.concatenate([whole[:, k * PART + half : (k + 1) * PART] for k in range(3)], axis=1),
        )

    def gathered(value):
        return lax.all_gather(value, "fsdp", axis=0, tiled=True)

    def other_core(own, columns):
        return swap(own[:, :columns], "seq", seq_count, 1)

    def to_rows(mixed):
        if span != rows:
            mixed = mixed[0].reshape(group, seq_count, rows).transpose(1, 0, 2)
        return lax.all_to_all(mixed, "seq", split_axis=0, concat_axis=0, tiled=True)

    def to_heads(value):
        value = lax.all_to_all(value, "seq", split_axis=0, concat_axis=0, tiled=True)
        if span != rows:
            value = value.transpose(1, 0, 2).reshape(1, group, GLEN)
        return value

    both = 3 * AR
    head_weights, side_weights, kept = [], [], []

    def gather_head(layer, *earlier):
        value = jnp.concatenate([both_part(layer), heads_part(layer)], axis=1)
        return gathered(after(value, *earlier) if earlier else value)

    head_gathered = gather_head(0)
    side_gathered = gathered(after(side_part(0), head_gathered))
    hidden = tokens[0].astype(F32)
    normed = (hidden * rms_of(hidden) * attn_gain[0]).astype(BF)
    if paired:
        far = swap(normed, "seq", seq_count, 2)
        head_gathered, far = fence(head_gathered, far)
    for layer in range(LAYERS):
        last = layer == LAYERS - 1
        factor = 1.442695041 / math.sqrt(HD) * jax.nn.softplus(query_scale[layer])
        tiled = jnp.concatenate([jnp.tile(factor * LOG2E, group // HD), jnp.ones((2 * group,), F32)])
        scale = jnp.tile(tiled, parts).reshape(1, 3 * width)
        if layer > 0 and paired:
            cut = rows * 3 // 5
            far = swap(normed[:cut], "seq", seq_count, 2)
            head_gathered, far, rest = fence(head_gathered, far, normed[cut:])
            next_side = gathered(after(side_part(layer), head_gathered))
            far = [far, swap(rest, "seq", seq_count, 2)]
        head_weights.append((head_gathered[None], other_core(head_gathered, both)[None]))
        if layer > 0:
            side_gathered = (
                next_side if paired else gathered(after(side_part(layer), head_gathered))
            )
        if paired:
            own = ([normed, swap(normed, "seq", seq_count, 1)], chip * 2 * rows)
            projected = [project(meta, scale, own[0], head_weights[layer], own[1], parts)]
            if layer > 0:
                far[0], far[1], projected[0] = fence(far[0], far[1], projected[0])
                far = jnp.concatenate(far)
            else:
                far = after(far, projected[0][-1])
            far = ([far, swap(far, "seq", seq_count, 1)], (1 - chip) * 2 * rows)
            projected.append(project(meta, scale, far[0], head_weights[layer], far[1], parts))
            groups = [own, far]
        else:
            groups = [([lax.all_gather(normed, "seq", axis=0, tiled=True)], place * 0)]
            projected = [project(meta, scale, groups[0][0], head_weights[layer], place * 0, parts)]
        heads = [[p[k] for p in projected] for k in range(parts)]
        attended, mixed = [], []
        for p in range(parts):
            inputs = heads[p] if p == 0 else [after(h, attended[-1][1]) for h in heads[p]]
            attended.append(attend(meta, inputs, span))
            if p < parts - 1:
                mixed.append(to_rows(attended[-1][0]))
        attended, mixed = fence(attended, mixed)
        mixed = mixed + [to_rows(attended[-1][0])]
        side_gathered = after(side_gathered, attended[-1][1], mixed[-1])
        side_weights.append((side_gathered, other_core(side_gathered, SIDE // 2)))
        if not last:
            head_gathered = gather_head(layer + 1, attended[-1][1], side_gathered)
        results = feed(
            meta,
            mlp_gain[layer][None],
            attn_gain[(layer + 1) % LAYERS][None],
            mixed,
            hidden,
            side_weights[layer],
            last,
        )
        kept.append(
            (hidden, groups, heads, [p[-1] for p in projected], attended, mixed, factor)
            + tuple(results[:3])
        )
        if last:
            layer_output = results[3]
        else:
            hidden, normed = results[3:]

    grad = cotangent[0]
    pending = None
    sums = [None] * LAYERS
    for layer in reversed(range(LAYERS)):
        hidden, groups, heads, lows, attended, mixed, factor, middle, inner, low = kept[layer]
        gain = mlp_gain[layer][None]
        results = feed_back(
            meta, gain, grad, middle, inner, side_weights[layer], parts, seq_count, pending
        )
        results = fence(*results)
        grad_in = grad if pending is None else results[5 + parts]
        grad, gi, gm, dl, il = results[:5]
        mixed_grads = [to_heads(results[5])]
        side_sum = feed_sums(gain, grad_in, middle, inner, gi, gm, dl, il, low, mixed)
        mixed_grads, side_sum = fence(mixed_grads, side_sum)
        side_total = reduce_rows(side_sum)
        factor_row = jnp.pad(factor, (0, 128 - HD)).reshape(1, 128)
        head_grads = []
        for p in range(parts):
            if p < parts - 1:
                mixed_grads.append(to_heads(after(results[6 + p], side_sum)))
            head_grads.append(
                attend_back(meta, factor_row, attended[p][1], attended[p][0], mixed_grads[p])
            )
            if p == parts - 1 and layer < LAYERS - 1 and paired:
                whole = sum_over_seq(jnp.stack(sums[layer + 1]), seq_count)
                head_grads, mixed_grads, whole = fence(head_grads, mixed_grads, whole)
                sums[layer + 1] = (whole[0], whole[1])
            else:
                head_grads, mixed_grads = fence(head_grads, mixed_grads)
        if paired:
            own, far = groups
            far_back = project_back(
                meta, head_grads, head_weights[layer], far[1], 2, rows, "far"
            )
            far_sum = (
                far_back[0].astype(F32) + swap(far_back[1], "seq", seq_count, 1).astype(F32)
            ).astype(BF)
            far_sum, head_grads, side_total = fence(far_sum, head_grads, side_total)
            cut = rows * (3 if layer > 0 else 2) // 5
            crossed = swap(far_sum[:cut], "seq", seq_count, 2)
            head_sum, lora_own = project_sums(
                meta, head_grads, lows, far_back[2], [g[0] for g in groups], head_weights[layer]
            )
            if layer == 0:
                side_total = sum_over_seq(side_total, seq_count)
            head_sum, lora_own, crossed, head_grads, rest, side_total = fence(
                head_sum, lora_own, crossed, head_grads, far_sum[cut:], side_total
            )
            if layer > 0:
                head_total = reduce_rows(head_sum)
            else:
                head_total = reduce_quarter(head_sum, core, chip, seq_count, fsdp_count)
            if layer > 0:
                rest = swap(rest, "seq", seq_count, 2)
            own_back = project_back(
                meta, head_grads, head_weights[layer], own[1], 2, rows, "own", lora_own
            )
            if layer > 0:
                own_back, rest = fence(own_back, rest)
            else:
                own_back, head_total, rest = fence(own_back, head_total, rest)
                rest = swap(rest, "seq", seq_count, 2)
                head_total = owned(head_total)
                head_total, rest = fence(head_total, rest)
            near = swap(own_back[1], "seq", seq_count, 1)
            sums[layer] = (side_total, head_total)
            terms = [own_back[0], near, crossed, rest]
        else:
            back = project_back(
                meta, head_grads, head_weights[layer], place * 0, 1, GLEN, "all"
            )
            terms = [lax.psum_scatter(back[0], "seq", scatter_dimension=0, tiled=True)]
            head_sum = project_sums(
                meta, head_grads, lows, back[1], [g[0] for g in groups], head_weights[layer]
            )[0]
            sums[layer] = tuple(lax.psum(v, "seq") for v in (side_total, reduce_rows(head_sum)))
        if layer > 0 and paired:
            pending = (attn_gain[layer][None], hidden, terms)
        else:
            grad = norm_back(attn_gain[layer][None], grad, hidden, terms)
            if paired:
                head_total = joined(jnp.sum(head_total.astype(F32), axis=0).astype(BF), chip, seq_count, 2)
                grad, head_total = fence(grad, head_total)
                sums[0] = (sums[0][0], joined(head_total, core, seq_count, 1))

    side = jnp.stack([s[0] for s in sums]).astype(F32)
    head = jnp.stack([s[1] for s in sums]).astype(F32)

    def columns(slot):
        return side[:, :, slot * AR : (slot + 1) * AR]

    return (
        layer_output[None],
        grad[None],
        head[:, :, : 3 * AR],
        head[:, :, 3 * AR :].reshape(LAYERS, shard, 3, AR).transpose(0, 2, 3, 1),
        columns(0),
        columns(1).transpose(0, 2, 1),
        columns(2),
        columns(3).transpose(0, 2, 1),
        columns(4),
        columns(5).transpose(0, 2, 1),
    )


def solution(mesh):
    rows = P("fsdp", "seq", None)
    first = P(None, "fsdp", None)
    second = P(None, None, "fsdp")
    return jax.shard_map(
        partial(local, seq_count=mesh.shape["seq"], fsdp_count=mesh.shape["fsdp"]),
        mesh=mesh,
        in_specs=(
            rows,
            P("fsdp", None),
            P("fsdp", None),
            P(),
            P(),
            P(),
            first,
            first,
            first,
            first,
            first,
            P(None, None, None, "fsdp"),
            first,
            second,
            first,
            second,
            first,
            second,
            rows,
        ),
        out_specs=(
            rows,
            rows,
            first,
            P(None, None, None, "fsdp"),
            first,
            second,
            first,
            second,
            first,
            second,
        ),
        check_vma=False,
    )
```
